128 devices in a mesh: ep: 32 (over z, x, core), tp: 4 (over y).
Axes of the slice: x: 4, y: 4, z: 4, core: 2. Of those that a mesh axis runs over, the one named last changes fastest.
Arguments:
- hidden_in: bfloat16 [32768, 1024], P(('ep', 'tp')), may hold values from -6 to 6
- segment_ids: int32 [32, 1024], P('ep'), may hold values from 0 to 3, never falling along the last dimension, each value on 1 to 512 neighbouring positions
- expert_ids: int32 [32768, 8], P(('ep', 'tp')), may hold values from 0 to 31, as said below
- slot_index: int32 [32768, 8], P(('ep', 'tp')), may hold values from 0 to 95, as said below
- attn_gain: bfloat16 [1024], replicated, may hold values from 0.5 to 1.5
- w_query: bfloat16 [1024, 1024], P(None, 'tp'), may hold values from -0.75 to 0.75
- w_key: bfloat16 [1024, 512], P(None, 'tp'), may hold values from -0.75 to 0.75
- w_value: bfloat16 [1024, 512], P(None, 'tp'), may hold values from -0.1875 to 0.1875
- w_output: bfloat16 [1024, 1024], P('tp'), may hold values from -3 to 3
- ffn_gain: bfloat16 [1024], replicated, may hold values from 0.5 to 1.5
- w_router: bfloat16 [1024, 32], replicated, may hold values from -0.09375 to 0.09375
- w_gate_up: bfloat16 [32, 1024, 2, 512], P('ep'), may hold values from -0.1875 to 0.1875
- w_down: bfloat16 [32, 512, 1024], P('ep'), may hold values from -6 to 6
- cotangent: bfloat16 [32768, 1024], P(('ep', 'tp')), may hold values from -6 to 6
Outputs:
- output: bfloat16 [32768, 1024], P(('ep', 'tp'))
- grad_hidden: float32 [32768, 1024], P(('ep', 'tp'))
- grad_attn_gain: float32 [1024], replicated
- grad_query: float32 [1024, 1024], P(None, 'tp')
- grad_key: float32 [1024, 512], P(None, 'tp')
- grad_value: float32 [1024, 512], P(None, 'tp')
- grad_output: float32 [1024, 1024], P('tp')
- grad_ffn_gain: float32 [1024], replicated
- grad_router: float32 [1024, 32], replicated
- grad_gate_up: float32 [32, 1024, 2, 512], P('ep')
- grad_down: float32 [32, 512, 1024], P('ep')
The draws below stay inside these ranges and needn't reach their ends.
Inputs may be any that keep to these rules, and one draw needn't show every extreme that they name: `segment_ids`: segment numbers never fall along a sequence. `expert_ids`: each row names 8 different experts. Among the rows of one device (aligned blocks of 256 rows) no expert is named more than 96 times, and some expert is named exactly 96 times by the rows of every device. `slot_index`: within the rows of one device, the rows naming one expert hold distinct slots, numbered from 0 up to that count minus one.
All inputs are finite; a program needn't handle non-finite values.
Results may differ from the reference program's by a relative error of at most 0.024.
Values may be sent and summed in bfloat16 or wider, within the bound.
No kernel may reach another device: no remote copies, remote signals or barrier semaphores. Data moves between devices by JAX's collectives and lax.ppermute only.
A program may use at most 192 MiB of HBM per device.

```python
import math
from functools import partial
import jax
import jax.numpy as jnp
import numpy as np
from jax import lax

D = 1024
H = 16
KVH = 8
HD = 64
FF_E = 512
EXPERTS = 32
TOPK = 8
LEN = 1024
TOK_DEV = 256
TOKENS = 32768
SEQS = 32
CAP = 96
N_EP = 32


def route_table(key):
    blocks = TOKENS // TOK_DEV
    average = TOK_DEV * TOPK // EXPERTS
    swing_most = average // 2
    order_key, swing_key, shuffle_key = jax.random.split(key, 3)
    ranking = jax.random.permutation(order_key, EXPERTS).astype(jnp.int32)
    swings = jax.random.randint(swing_key, (blocks, EXPERTS // 2), 0, swing_most + 1, dtype=jnp.int32)
    swings = swings.at[:, 0].set(swing_most)
    loads = jnp.stack([average + swings, average - swings], axis=2).reshape(blocks, EXPERTS)
    run_ends = jnp.cumsum(loads, axis=1).astype(jnp.int32)
    run_starts = run_ends - loads
    places = jnp.arange(TOPK * TOK_DEV, dtype=jnp.int32)
    holder = jnp.sum((places[None, :, None] >= run_ends[:, None, :]).astype(jnp.int32), axis=2)
    slots_made = places[None, :] - jnp.take_along_axis(run_starts, holder, axis=1)
    chosen = ranking[holder]
    chosen = chosen.reshape(blocks, TOPK, TOK_DEV).transpose(0, 2, 1)
    slots_made = slots_made.reshape(blocks, TOPK, TOK_DEV).transpose(0, 2, 1)
    shuffle_keys = jax.random.split(shuffle_key, blocks)
    shuffles = jax.vmap(lambda member: jax.random.permutation(member, TOK_DEV))(shuffle_keys).astype(jnp.int32)
    chosen = jnp.take_along_axis(chosen, shuffles[:, :, None], axis=1)
    slots_made = jnp.take_along_axis(slots_made, shuffles[:, :, None], axis=1)
    return (chosen.reshape(TOKENS, TOPK).astype(jnp.int32), slots_made.reshape(TOKENS, TOPK).astype(jnp.int32))


def draw_expert_ids(key, part):
    tables = route_table(key)
    return tables[0]


def draw_slot_index(key, part):
    tables = route_table(key)
    return tables[1]


def block_levels(own_key, dims, pieces, least, high):
    loudness, own = 1.0, jax.random.fold_in(own_key, 6)
    for dim, shards_of in pieces:
        draws = jnp.exp(jax.random.uniform(jax.random.fold_in(own, dim), (shards_of,), jnp.float32, least / len(pieces), high / len(pieces)))
        loudness = loudness * jnp.repeat(draws, dims[dim] // shards_of).reshape([-1 if axis == dim else 1 for axis in range(len(dims))])
    return loudness


def profile(number_of, total, most, lean):
    weights = [(1 << 20) // math.isqrt(standing ** lean) + 1 for standing in range(2, number_of + 1)]
    rest, counts = total - most - (number_of - 1), [1] * (number_of - 1)
    while rest > 0:
        candidates = [i for i in range(number_of - 1) if counts[i] < most]
        mass, remaining = sum([weights[i] for i in candidates]), rest
        for i in candidates:
            more = min(most - counts[i], max(1, remaining * weights[i] // mass), rest)
            counts[i] = counts[i] + more
            rest = rest - more
    return np.array([most] + counts)


def ragged(rng, count, total, most, lean):
    if count == 2:
        one = jax.random.randint(rng, (), max(1, total - most), min(most, total - 1) + 1)
        return jnp.stack([one, total - one])
    sizes = jnp.asarray(profile(count, total, most, lean), jnp.int32)
    couples = (count - 1) // 2
    donor, taker = sizes[1:1 + 2 * couples:2], sizes[2:2 + 2 * couples:2]
    room = jnp.minimum(donor - 1, most - taker)
    moved = jax.random.randint(jax.random.fold_in(rng, 1), (couples,), 0, 1 << 20) % (room + 1)
    sizes = sizes.at[1:1 + 2 * couples:2].set(donor - moved).at[2:2 + 2 * couples:2].set(taker + moved)
    return sizes[jax.random.permutation(jax.random.fold_in(rng, 2), count)]


def normal_values(own_key, extent, spread, bound, cuts=(), held_as=jnp.bfloat16):
    array = spread * jax.random.normal(own_key, extent, jnp.float32)
    if cuts:
        array = array * block_levels(own_key, extent, cuts, -0.22, 0.18)
    return jnp.clip(array, -bound, bound).astype(held_as)


def setup_inputs(seed: int = 0) -> dict:
    streams_of = jax.random.split(jax.random.key(seed), 15)
    hidden_in = normal_values(streams_of[0], (TOKENS, D), 1.0, 6.0, ((0, 128),))
    segment_ids = jax.vmap(lambda own: jnp.searchsorted(jnp.cumsum(ragged(own, 4, LEN, LEN // 2, 0)), jnp.arange(LEN), side="right"))(jax.random.split(streams_of[1], SEQS)).reshape((SEQS, LEN)).astype(jnp.int32)
    expert_ids = draw_expert_ids(jax.random.fold_in(streams_of[14], 71), 0)
    slot_index = draw_slot_index(jax.random.fold_in(streams_of[14], 71), 0)
    attn_gain = jnp.clip(1.0 + 0.1 * jax.random.normal(streams_of[4], (D,), jnp.float32), 0.5, 1.5).astype(jnp.bfloat16)
    w_query = normal_values(streams_of[5], (D, H * HD), (D // 16) ** -0.5, 0.75, ((1, 4),))
    w_key = normal_values(streams_of[6], (D, KVH * HD), (D // 16) ** -0.5, 0.75, ((1, 4),))
    w_value = normal_values(streams_of[7], (D, KVH * HD), D ** -0.5, 0.1875, ((1, 4),))
    w_output = normal_values(streams_of[8], (H * HD, D), 0.5, 3.0, ((0, 4),))
    ffn_gain = jnp.clip(1.0 + 0.1 * jax.random.normal(streams_of[9], (D,), jnp.float32), 0.5, 1.5).astype(jnp.bfloat16)
    w_router = normal_values(streams_of[10], (D, EXPERTS), (4 * D) ** -0.5, 0.09375)
    w_gate_up = normal_values(streams_of[11], (EXPERTS, D, 2, FF_E), D ** -0.5, 0.1875, ((0, 32),))
    w_down = normal_values(streams_of[12], (EXPERTS, FF_E, D), 1.0, 6.0, ((0, 32),))
    cotangent = normal_values(streams_of[13], (TOKENS, D), 1.0, 6.0, ((0, 128),))
    return dict(hidden_in=hidden_in, segment_ids=segment_ids, expert_ids=expert_ids, slot_index=slot_index, attn_gain=attn_gain, w_query=w_query, w_key=w_key, w_value=w_value, w_output=w_output, ffn_gain=ffn_gain, w_router=w_router, w_gate_up=w_gate_up, w_down=w_down, cotangent=cotangent)


@jax.custom_vjp
def low(v):
    return lax.optimization_barrier(v.astype(jnp.bfloat16)).astype(jnp.float32)

@jax.custom_vjp
def low_back(v):
    return v

def low_keep(v):
    return (low(v), None)

def low_pass(kept, grad):
    return (grad,)

def back_keep(v):
    return (v, None)

def back_low(kept, grad):
    return (low(grad),)
low.defvjp(low_keep, low_pass)
low_back.defvjp(back_keep, back_low)
ATT_SCALE = 0.015625
RES_SCALE = 0.22
NORM_EPS = 1e-06
ROPE_BASE = 10000.0
NEG_FILL = -1e+30
HIGHEST = lax.Precision.HIGHEST

def rms_norm(vector, gain):
    return vector * lax.rsqrt(lax.optimization_barrier(jnp.mean(vector * vector, axis=-1, keepdims=True)) + NORM_EPS) * gain

def rope_tables(length, width):
    halfway = width // 2
    freqs = ROPE_BASE ** (-jnp.arange(halfway, dtype=jnp.float32) * 2.0 / width)
    angles = jnp.arange(length, dtype=jnp.float32)[:, None] * freqs[None, :]
    cosine = jnp.concatenate([jnp.cos(angles), jnp.cos(angles)], axis=1)
    sine = jnp.concatenate([jnp.sin(angles), jnp.sin(angles)], axis=1)
    return (cosine, sine)

def rotate(vector, cosine, sine):
    halfway = vector.shape[-1] // 2
    turned = jnp.concatenate([-vector[..., halfway:], vector[..., :halfway]], axis=-1)
    return vector * cosine[:, None, :] + turned * sine[:, None, :]

def attend_sequence(normed, segments_here, w_query, w_key, w_value):
    length = normed.shape[0]
    cosine, sine = rope_tables(length, HD)
    query_pre = low_back(jnp.dot(normed, w_query, precision=HIGHEST)).reshape(length, H, HD)
    key_pre = low_back(jnp.dot(normed, w_key, precision=HIGHEST)).reshape(length, KVH, HD)
    values = low(low_back(jnp.dot(normed, w_value, precision=HIGHEST))).reshape(length, KVH, HD)
    queries = low(rotate(query_pre, cosine, sine)).reshape(length, KVH, H // KVH, HD)
    keys_rot = low(rotate(key_pre, cosine, sine))
    block_rows = min(512, length)
    positions = jnp.arange(length, dtype=jnp.int32)

    def one_block(begin_row):
        query_block = lax.dynamic_slice_in_dim(queries, begin_row, block_rows, 0)
        query_pos = begin_row + jnp.arange(block_rows, dtype=jnp.int32)
        query_seg = lax.dynamic_slice_in_dim(segments_here, begin_row, block_rows, 0)
        allowed = (query_seg[:, None] == segments_here[None, :]) & (positions[None, :] <= query_pos[:, None])
        scores = jnp.einsum('qkgd,tkd->kgqt', query_block, keys_rot, precision=HIGHEST) * ATT_SCALE
        scores = low_back(jnp.where(allowed[None, None], scores, NEG_FILL))
        probs = low(jax.nn.softmax(scores, axis=-1))
        return jnp.einsum('kgqt,tkd->qkgd', probs, values, precision=HIGHEST)
    begins = (jnp.arange(length // block_rows) * block_rows).astype(jnp.int32)
    blocks_out = lax.map(jax.checkpoint(one_block), begins)
    return blocks_out.reshape(length, H * HD)

def expert_block(packed, w_gate_up, w_down):
    block_rows, block_gates, block_ids, block_slots = packed
    positions = (block_ids * CAP + block_slots).reshape(-1)
    owners = jnp.full((EXPERTS * CAP,), TOK_DEV, jnp.int32).at[positions].set(jnp.repeat(jnp.arange(TOK_DEV, dtype=jnp.int32), TOPK))
    padded = jnp.concatenate([block_rows, jnp.zeros((1, D), jnp.float32)], axis=0)
    dispatched = low_back(padded[owners]).reshape(EXPERTS, CAP, D)
    gate_up = low_back(jnp.einsum('ecd,edgf->ecgf', dispatched, w_gate_up, precision=HIGHEST))
    inner_act = low(jax.nn.silu(gate_up[:, :, 0, :]) * gate_up[:, :, 1, :])
    expert_out = low(low_back(jnp.einsum('ecf,efd->ecd', inner_act, w_down, precision=HIGHEST)))
    picked = expert_out.reshape(EXPERTS * CAP, D)[positions].reshape(TOK_DEV, TOPK, D)
    return lax.optimization_barrier(jnp.sum(block_gates[:, :, None] * picked, axis=1))

def layer(hidden, attn_gain, w_query, w_key, w_value, w_output, ffn_gain, w_router, w_gate_up, w_down, segment_ids, expert_ids, slot_index):
    normed = low(rms_norm(hidden, attn_gain))

    def per_sequence(seq_pair):
        return attend_sequence(seq_pair[0], seq_pair[1], w_query, w_key, w_value)
    attended = lax.map(per_sequence, (normed.reshape(N_EP, LEN, D), segment_ids))
    mixed = low(low_back(attended.reshape(TOKENS, H * HD)))
    branch = low_back(jnp.dot(mixed, w_output, precision=HIGHEST))
    middle = hidden + RES_SCALE * branch
    routed = low(rms_norm(middle, ffn_gain))
    logits = jnp.dot(routed, w_router, precision=HIGHEST)
    gates = jax.nn.softmax(jnp.take_along_axis(logits, expert_ids, axis=1), axis=-1)
    blocks = TOKENS // TOK_DEV
    packed = (routed.reshape(blocks, TOK_DEV, D), gates.reshape(blocks, TOK_DEV, TOPK), expert_ids.reshape(blocks, TOK_DEV, TOPK), slot_index.reshape(blocks, TOK_DEV, TOPK))
    moe = lax.map(jax.checkpoint(partial(expert_block, w_gate_up=w_gate_up, w_down=w_down)), packed)
    return middle + RES_SCALE * moe.reshape(TOKENS, D)

def reference(hidden_in, segment_ids, expert_ids, slot_index, attn_gain, w_query, w_key, w_value, w_output, ffn_gain, w_router, w_gate_up, w_down, cotangent):
    floats = [item.astype(jnp.float32) for item in (hidden_in, attn_gain, w_query, w_key, w_value, w_output, ffn_gain, w_router, w_gate_up, w_down)]

    def forward(hidden, gain_one, query_w, key_w, value_w, output_w, gain_two, router_w, gate_up_w, down_w):
        return layer(hidden, gain_one, query_w, key_w, value_w, output_w, gain_two, router_w, gate_up_w, down_w, segment_ids, expert_ids, slot_index)
    result, pullback = jax.vjp(forward, *floats)
    grads = pullback(cotangent.astype(jnp.float32))
    return (result.astype(jnp.bfloat16), grads[0], grads[1], grads[2], grads[3], grads[4], grads[5], grads[6], grads[7], grads[8], grads[9])
```

```python
import jax
import jax.numpy as jnp
from jax import lax
from jax.experimental import pallas as pl
from jax.experimental.pallas import tpu as pltpu
from jax.sharding import PartitionSpec as P

HD = 64
ATT_SCALE = 0.015625
RES_SCALE = 0.22
NORM_EPS = 1e-06
ROPE_BASE = 10000.0
NEG_FILL = -1e30
HIGHEST = lax.Precision.HIGHEST
F32 = jnp.float32
BF16 = jnp.bfloat16

ROWS = 256
WIDTH = 1024
HALF = 512
CAP = 96
EXPERTS = 32
RING = 4
HEADS = 4
LANES = 128
VMEM_BYTES = 58 * 1024 * 1024
WHOLE = pl.BlockSpec(memory_space=pltpu.VMEM)
SCALARS = pl.BlockSpec(memory_space=pltpu.SMEM)
ANYWHERE = pl.BlockSpec(memory_space=pl.ANY)


def params():
    return pltpu.CompilerParams(vmem_limit_bytes=VMEM_BYTES)


def dot(a, b, precision=None):
    return jnp.dot(a, b, preferred_element_type=F32, precision=precision)


def dot_nt(a, b):
    return lax.dot_general(a, b, (((1,), (1,)), ((), ())), preferred_element_type=F32)


def dot_tn(a, b):
    return lax.dot_general(a, b, (((0,), (0,)), ((), ())), preferred_element_type=F32)


def place(z, x, core):
    return ((z % RING) * RING + (x % RING)) * 2 + core


def push(value, dz, dx, dc):
    if (dz % RING, dx % RING, dc) == (0, 0, 0):
        return value
    pairs = [
        (place(z, x, c), place(z + dz, x + dx, c ^ dc))
        for z in range(RING)
        for x in range(RING)
        for c in range(2)
    ]
    return lax.ppermute(value, "ep", pairs)


def push_tp(value, dy):
    if dy % RING == 0:
        return value
    return lax.ppermute(value, "tp", [(y, (y + dy) % RING) for y in range(RING)])


def swap_halves(v):
    lane = lax.broadcasted_iota(jnp.int32, v.shape, 1)
    return jnp.where(lane % HD < HD // 2, pltpu.roll(v, LANES - HD // 2, 1), pltpu.roll(v, HD // 2, 1))


def block_at(index):
    return pl.ds(pl.multiple_of(index * ROWS, ROWS), ROWS)


def key_range(block):
    return max(0, block - 2) * ROWS, (block + 1) * ROWS


def mask_bias(block, seg_col, seg_row):
    lo, hi = key_range(block)
    key_pos = lo + lax.broadcasted_iota(jnp.int32, (hi - lo, ROWS), 0)
    query_pos = block * ROWS + lax.broadcasted_iota(jnp.int32, (hi - lo, ROWS), 1)
    same = seg_col[lo:hi, :] == seg_row[:, block * ROWS : (block + 1) * ROWS]
    return jnp.where(same & (key_pos <= query_pos), 0.0, NEG_FILL)


def attend_kernel(
    rank, x0, x1, x2, x3, gain, wq, wk, wv, wo, cos, sin, seg_col, seg_row,
    normed, q_out, k_out, v_out, mixed, lse, br0, br1, br2, br3, vt, bias,
):
    me = rank[0]
    lane = lax.broadcasted_iota(jnp.int32, (ROWS, LANES), 1)
    for d, x_ref in enumerate((x0, x1, x2, x3)):
        at = block_at((me + d) % RING)
        x = x_ref[...].astype(F32)
        inverse = lax.rsqrt(jnp.mean(x * x, axis=-1, keepdims=True) + NORM_EPS)
        low = (x * inverse * gain[...]).astype(BF16)
        normed[at, :] = low
        cos_here, sin_here = cos[at, :], sin[at, :]

        def rope(v):
            return v * cos_here + swap_halves(v) * sin_here

        query = dot(low, wq[...])
        for pair in range(2):
            q = rope(query[:, pair * LANES : (pair + 1) * LANES]) * ATT_SCALE
            other = pltpu.roll(q, HD, 1)
            keep = (lane < HD) if pair == 0 else (lane >= HD)
            first, second = (q, other) if pair == 0 else (other, q)
            at_head = 2 * pair * LANES
            q_out[at, at_head : at_head + LANES] = jnp.where(keep, first, 0.0).astype(BF16)
            q_out[at, at_head + LANES : at_head + 2 * LANES] = jnp.where(keep, second, 0.0).astype(BF16)
        k_out[at, :] = rope(dot(low, wk[...])).astype(BF16)
        v_out[at, :] = dot(low, wv[...]).astype(BF16)
    vt[...] = v_out[...].astype(F32).T.astype(BF16)
    for b in range(RING):
        lo, hi = key_range(b)
        rows = slice(b * ROWS, (b + 1) * ROWS)
        bias[0 : hi - lo, :] = mask_bias(b, seg_col, seg_row)
        outs = []
        for h in range(HEADS):
            q = q_out[rows, h * LANES : (h + 1) * LANES]
            scores = dot_nt(k_out[lo:hi, :], q) + bias[0 : hi - lo, :]
            top = jnp.max(scores, axis=0, keepdims=True)
            weights = jnp.exp(scores - top)
            total = jnp.sum(weights, axis=0, keepdims=True)
            out = dot(vt[:, lo:hi], weights.astype(BF16)) * (1.0 / total)
            outs.append(out.T)
            lse[h : h + 1, rows] = top + jnp.log(total)
        mixed[rows, 0:LANES] = jnp.where(lane < HD, outs[0], pltpu.roll(outs[1], HD, 1)).astype(BF16)
        mixed[rows, LANES:] = jnp.where(lane < HD, pltpu.roll(outs[2], HD, 1), outs[3]).astype(BF16)
        branch = dot(mixed[rows, :], wo[...]).astype(BF16)
        relative = (b - me + RING) % RING
        for d, br in enumerate((br0, br1, br2, br3)):

            @pl.when(relative == d)
            def _():
                br[...] = branch


def attend(rank, pieces, gain, wq, wk, wv, wo, cos, sin, seg_col, seg_row):
    length = RING * ROWS
    return pl.pallas_call(
        attend_kernel,
        out_shape=[
            jax.ShapeDtypeStruct((length, WIDTH), BF16),
            jax.ShapeDtypeStruct((length, HEADS * LANES), BF16),
            jax.ShapeDtypeStruct((length, LANES), BF16),
            jax.ShapeDtypeStruct((length, LANES), BF16),
            jax.ShapeDtypeStruct((length, HEADS * HD), BF16),
            jax.ShapeDtypeStruct((8, length), F32),
        ]
        + [jax.ShapeDtypeStruct((ROWS, WIDTH), BF16)] * RING,
        in_specs=[SCALARS] + [WHOLE] * 13,
        out_specs=[WHOLE] * 10,
        scratch_shapes=[pltpu.VMEM((LANES, length), BF16), pltpu.VMEM((3 * ROWS, ROWS), F32)],
        compiler_params=params(),
        cost_estimate=pl.CostEstimate(flops=6_000_000_000, bytes_accessed=14_000_000, transcendentals=4_000_000),
        name="attend",
    )(rank, *pieces, gain, wq, wk, wv, wo, cos, sin, seg_col, seg_row)


def route_kernel(x, b0, b1, b2, b3, gain, wr, chosen, middle, half_a, half_b, gates_t):
    branch = b0[...].astype(F32) + b1[...].astype(F32) + b2[...].astype(F32) + b3[...].astype(F32)
    mid = x[...].astype(F32) + RES_SCALE * branch
    middle[...] = mid
    inverse = lax.rsqrt(jnp.mean(mid * mid, axis=-1, keepdims=True) + NORM_EPS)
    routed = (mid * inverse * gain[...]).astype(BF16)
    half_a[...] = routed[:, :HALF]
    half_b[...] = routed[:, HALF:]
    logits = jnp.where(chosen[...] > 0.0, dot(routed, wr[...]), NEG_FILL)
    weights = jnp.exp(logits - jnp.max(logits, axis=-1, keepdims=True))
    gates_t[...] = (weights / jnp.sum(weights, axis=-1, keepdims=True)).T


def route(x, branches, gain, wr, chosen):
    return pl.pallas_call(
        route_kernel,
        out_shape=[
            jax.ShapeDtypeStruct((ROWS, WIDTH), F32),
            jax.ShapeDtypeStruct((ROWS, HALF), BF16),
            jax.ShapeDtypeStruct((ROWS, HALF), BF16),
            jax.ShapeDtypeStruct((EXPERTS, ROWS), F32),
        ],
        in_specs=[WHOLE] * 8,
        out_specs=[WHOLE] * 4,
        compiler_params=params(),
        cost_estimate=pl.CostEstimate(flops=20_000_000, bytes_accessed=5_000_000, transcendentals=8192),
        name="route",
    )(x, *branches, gain, wr, chosen)


def slot_matrix(slots, row):
    slot = lax.broadcasted_iota(jnp.int32, (CAP, ROWS), 0).astype(F32)
    return jnp.where(slot == slots[row : row + 1, :], 1.0, 0.0)


def line_matrix(slots, d):
    return jnp.concatenate([slot_matrix(slots, d * 8 + j).astype(BF16) for j in range(8)], axis=0)


def dispatch_kernel(slots_a, slots_b, *refs):
    for half, slots in enumerate((slots_a, slots_b)):
        rows, pieces = refs[4 * half : 4 * half + 4], refs[8 + 8 * half : 16 + 8 * half]
        for d in range(RING):
            filled = dot(line_matrix(slots, d), rows[d][...]).astype(BF16)
            for j in range(8):
                pieces[j][d * CAP : (d + 1) * CAP, :] = filled[j * CAP : (j + 1) * CAP, :]


def combine_kernel(slots_a, slots_b, *refs):
    for half, slots in enumerate((slots_a, slots_b)):
        pieces, rows = refs[8 * half : 8 * half + 8], refs[16 + 4 * half : 20 + 4 * half]
        for d in range(RING):
            filled = jnp.concatenate([pieces[j][d * CAP : (d + 1) * CAP, :] for j in range(8)], axis=0)
            rows[d][...] = dot_tn(line_matrix(slots, d), filled).astype(BF16)


SLOT_COST = pl.CostEstimate(flops=1_700_000_000, bytes_accessed=8_500_000, transcendentals=0)


def dispatch(slots_a, slots_b, half_a, half_b):
    along_z = [push(half_a, -d, 0, 0) for d in range(RING)]
    along_x = [push(half_b, 0, -d, 0) for d in range(RING)]
    pieces = pl.pallas_call(
        dispatch_kernel,
        out_shape=[jax.ShapeDtypeStruct((RING * CAP, HALF), BF16)] * 16,
        in_specs=[WHOLE] * 10,
        out_specs=[WHOLE] * 16,
        compiler_params=params(),
        cost_estimate=SLOT_COST,
        name="dispatch",
    )(slots_a, slots_b, *along_z, *along_x)
    return exchange(pieces)


def exchange(pieces):
    pieces_a, pieces_b = pieces[:8], pieces[8:]
    got_a, got_b = [None] * 8, [None] * 8
    for d in (1, 3, 2, 0):
        for dc in (0, 1):
            source = ((-d) % RING) * 2 + dc
            got_a[source] = push(pieces_a[d * 2 + dc], 0, d, dc)
            got_b[source] = push(pieces_b[d * 2 + dc], d, 0, dc)
    return got_a + got_b


def combine(slots_a, slots_b, pieces):
    pieces = exchange(pieces)
    partial = pl.pallas_call(
        combine_kernel,
        out_shape=[jax.ShapeDtypeStruct((ROWS, HALF), BF16)] * 8,
        in_specs=[WHOLE] * 18,
        out_specs=[WHOLE] * 8,
        compiler_params=params(),
        cost_estimate=SLOT_COST,
        name="combine",
    )(slots_a, slots_b, *pieces)
    return [push(partial[d], d, 0, 0) for d in range(RING)] + [
        push(partial[4 + d], 0, d, 0) for d in range(RING)
    ]


STEPS = 8
STEP_ROWS = RING * CAP


def expert_kernel(slots, gates, wgu, wgu_t, wd, wd_t, *refs):
    ra, rb, ca, cb = (refs[8 * i : 8 * i + 8] for i in range(4))
    qa, qb, ma, mb = (refs[32 + 8 * i : 40 + 8 * i] for i in range(4))
    dgate_out, disp_out, dgu_out, inner_out, dex_out = refs[64:69]
    rows_in, cot_in, back_out, moe_out, in_sem, out_sem = refs[69:]
    step = pl.program_id(0)

    def copies(j, pairs, sems, outward):
        slot, dx, dc, made = j % 2, j // 2, j % 2, []
        for which, (half_a, half_b, buf) in enumerate(pairs):
            ends = [(half_a[j], buf.at[slot, :, pl.ds(0, HALF)])]
            for dz in range(RING):
                ends.append(
                    (half_b[dz * 2 + dc].at[pl.ds(dx * CAP, CAP)], buf.at[slot, pl.ds(dz * CAP, CAP), pl.ds(HALF, HALF)])
                )
            for n, (far, near) in enumerate(ends):
                source, target = (near, far) if outward else (far, near)
                made.append(pltpu.make_async_copy(source, target, sems.at[slot, which * 5 + n]))
        return made

    def fetches(j):
        return copies(j, ((ra, rb, rows_in), (ca, cb, cot_in)), in_sem, False)

    def stores(j):
        return copies(j, ((qa, qb, back_out), (ma, mb, moe_out)), out_sem, True)

    for j in range(STEPS):

        @pl.when(step == j)
        def _():
            if j == 0:
                for copy in fetches(0):
                    copy.start()
            if j + 1 < STEPS:
                for copy in fetches(j + 1):
                    copy.start()
            for copy in fetches(j):
                copy.wait()
            if j >= 2:
                for copy in stores(j - 2):
                    copy.wait()

    slot = step % 2
    fills = [slot_matrix(slots.at[0], dz) for dz in range(RING)]
    gate_slot = jnp.concatenate(
        [jnp.sum(fills[dz] * gates[0, dz : dz + 1, :], axis=1, keepdims=True) for dz in range(RING)], axis=0
    )
    rows = rows_in[slot]
    disp_out[...] = rows
    gate_up = dot(rows, wgu[...])
    gate, up = gate_up[:, :HALF], gate_up[:, HALF:]
    sigmoid = jax.nn.sigmoid(gate)
    silu = gate * sigmoid
    inner = (silu * up).astype(BF16)
    inner_out[...] = inner
    made = dot(inner, wd[...]).astype(BF16).astype(F32)
    dmoe = RES_SCALE * cot_in[slot].astype(F32)
    dgate_slot = jnp.sum(dmoe * made, axis=1, keepdims=True)
    for dz in range(RING):
        dgate_out[0, dz : dz + 1, :] = jnp.sum(
            fills[dz] * dgate_slot[dz * CAP : (dz + 1) * CAP, :], axis=0, keepdims=True
        )
    moe_out[slot] = (gate_slot * made).astype(BF16)
    dex = (gate_slot * dmoe).astype(BF16)
    dex_out[...] = dex
    dinner = dot(dex, wd_t[...])
    dgate = dinner * up * sigmoid * (1.0 + gate * (1.0 - sigmoid))
    dgu = jnp.concatenate([dgate.astype(BF16), (dinner * silu).astype(BF16)], axis=1)
    dgu_out[...] = dgu
    back_out[slot] = dot(dgu, wgu_t[...]).astype(BF16)

    for j in range(STEPS):

        @pl.when(step == j)
        def _():
            for copy in stores(j):
                copy.start()
            if j == STEPS - 1:
                for copy in stores(j - 1) + stores(j):
                    copy.wait()


def experts(slots, gates, wgu, wgu_t, wd, wd_t, rows, cots):
    piece = jax.ShapeDtypeStruct((STEP_ROWS, HALF), BF16)
    total = STEPS * STEP_ROWS
    by_step = pl.BlockSpec((1, RING, ROWS), lambda s: (s, 0, 0))
    wide = pl.BlockSpec((STEP_ROWS, WIDTH), lambda s: (s, 0))
    narrow = pl.BlockSpec((STEP_ROWS, HALF), lambda s: (s, 0))
    buf = pltpu.VMEM((2, STEP_ROWS, WIDTH), BF16)
    made = pl.pallas_call(
        expert_kernel,
        grid=(STEPS,),
        out_shape=[piece] * 32
        + [
            jax.ShapeDtypeStruct((STEPS, RING, ROWS), F32),
            jax.ShapeDtypeStruct((total, WIDTH), BF16),
            jax.ShapeDtypeStruct((total, WIDTH), BF16),
            jax.ShapeDtypeStruct((total, HALF), BF16),
            jax.ShapeDtypeStruct((total, WIDTH), BF16),
        ],
        in_specs=[by_step, by_step] + [WHOLE] * 4 + [ANYWHERE] * 32,
        out_specs=[ANYWHERE] * 32 + [by_step, wide, wide, narrow, wide],
        scratch_shapes=[buf, buf, buf, buf, pltpu.SemaphoreType.DMA((2, 10)), pltpu.SemaphoreType.DMA((2, 10))],
        compiler_params=params(),
        cost_estimate=pl.CostEstimate(flops=19_000_000_000, bytes_accessed=60_000_000, transcendentals=1_600_000),
        name="experts",
    )(slots, gates, wgu, wgu_t, wd, wd_t, *rows, *cots)
    return made[:16], made[16:32], made[32], made[33], made[34], made[35], made[36]


def unroute_kernel(*refs):
    parts, (gates_t, dgates_t, middle, cot, gain, wr_t, dmiddle, dbranch, sums) = refs[:8], refs[8:]

    def four(pieces):
        a, b, c, d = (piece[...].astype(F32) for piece in pieces)
        return (a + b) + (c + d)

    gates, dgates = gates_t[...], dgates_t[...]
    dlogits = gates * (dgates - jnp.sum(gates * dgates, axis=0, keepdims=True))
    drouted = jnp.concatenate([four(parts[:4]), four(parts[4:])], axis=1)
    drouted = drouted + dot(dlogits.T, wr_t[...], HIGHEST)
    mid = middle[...]
    inverse = lax.rsqrt(jnp.mean(mid * mid, axis=-1, keepdims=True) + NORM_EPS)
    plain = mid * inverse
    routed = (plain * gain[...]).astype(BF16).astype(F32)
    sums[0:EXPERTS, :] = dot(dlogits, routed, HIGHEST)
    sums[EXPERTS : EXPERTS + 8, :] = jnp.broadcast_to(jnp.sum(drouted * plain, axis=0, keepdims=True), (8, WIDTH))
    scaled = drouted * gain[...]
    along = jnp.mean(scaled * plain, axis=-1, keepdims=True)
    total = cot[...].astype(F32) + inverse * (scaled - plain * along)
    dmiddle[...] = total
    dbranch[...] = (RES_SCALE * total).astype(BF16)


def unroute(parts, gates_t, dgates_t, middle, cot, gain, wr_t):
    return pl.pallas_call(
        unroute_kernel,
        out_shape=[
            jax.ShapeDtypeStruct((ROWS, WIDTH), F32),
            jax.ShapeDtypeStruct((ROWS, WIDTH), BF16),
            jax.ShapeDtypeStruct((EXPERTS + 8, WIDTH), F32),
        ],
        in_specs=[WHOLE] * 14,
        out_specs=[WHOLE] * 3,
        compiler_params=params(),
        cost_estimate=pl.CostEstimate(flops=200_000_000, bytes_accessed=6_000_000, transcendentals=0),
        name="unroute",
    )(*parts, gates_t, dgates_t, middle, cot, gain, wr_t)


def unmix_kernel(rank, d0, d1, d2, d3, mixed, wo, dmixed, grad_out):
    me = rank[0]
    lane = lax.broadcasted_iota(jnp.int32, (ROWS, LANES), 1)
    for d, ref in enumerate((d0, d1, d2, d3)):
        at = block_at((me + d) % RING)
        low = dot_nt(ref[...], wo[...])
        for pair in range(2):
            both = low[:, pair * LANES : (pair + 1) * LANES]
            other = pltpu.roll(both, HD, 1)
            keep = (lane < HD) if pair == 0 else (lane >= HD)
            first, second = (both, other) if pair == 0 else (other, both)
            at_head = 2 * pair * LANES
            dmixed[at, at_head : at_head + LANES] = jnp.where(keep, first, 0.0).astype(BF16)
            dmixed[at, at_head + LANES : at_head + 2 * LANES] = jnp.where(keep, second, 0.0).astype(BF16)
        term = dot_tn(mixed[at, :], ref[...])
        total = term if d == 0 else total + term
    grad_out[...] = total.astype(BF16)


def unmix(rank, pieces, mixed, wo):
    length = RING * ROWS
    return pl.pallas_call(
        unmix_kernel,
        out_shape=[
            jax.ShapeDtypeStruct((length, HEADS * LANES), BF16),
            jax.ShapeDtypeStruct((HEADS * HD, WIDTH), BF16),
        ],
        in_specs=[SCALARS] + [WHOLE] * 6,
        out_specs=[WHOLE] * 2,
        compiler_params=params(),
        cost_estimate=pl.CostEstimate(flops=1_100_000_000, bytes_accessed=5_000_000, transcendentals=0),
        name="unmix",
    )(rank, *pieces, mixed, wo)


def unattend_kernel(
    rank, q_in, k_in, v_in, lse, dmixed, normed, gain_col, wq, wk, wv, cos, sin, seg_col, seg_row,
    dn0, dn1, dn2, dn3, grads, dgain, kt, bias, dk, dv, dqkv,
):
    me = rank[0]
    lane = lax.broadcasted_iota(jnp.int32, (ROWS, LANES), 1)
    kt[...] = k_in[...].astype(F32).T.astype(BF16)
    dk[...] = jnp.zeros_like(dk)
    dv[...] = jnp.zeros_like(dv)

    def unrope(v, rows):
        return v * cos[rows, :] - swap_halves(v) * sin[rows, :]

    for b in range(RING):
        lo, hi = key_range(b)
        rows = slice(b * ROWS, (b + 1) * ROWS)
        bias[0 : hi - lo, :] = mask_bias(b, seg_col, seg_row)
        dqs = []
        for h in range(HEADS):
            cols = slice(h * LANES, (h + 1) * LANES)
            q, do = q_in[rows, cols], dmixed[rows, cols]
            scores = dot_nt(k_in[lo:hi, :], q) + bias[0 : hi - lo, :]
            probs = jnp.exp(scores - lse[h : h + 1, rows])
            dprobs = dot_nt(v_in[lo:hi, :], do)
            delta = jnp.sum(probs * dprobs, axis=0, keepdims=True)
            dscores = (probs * (dprobs - delta)).astype(BF16)
            dv[lo:hi, :] += dot(probs.astype(BF16), do)
            dk[lo:hi, :] += dot(dscores, q)
            dqs.append(dot(kt[:, lo:hi], dscores).T * ATT_SCALE)
        first = jnp.where(lane < HD, dqs[0], pltpu.roll(dqs[1], HD, 1))
        second = jnp.where(lane < HD, pltpu.roll(dqs[2], HD, 1), dqs[3])
        dqkv[rows, 0:LANES] = unrope(first, rows).astype(BF16)
        dqkv[rows, LANES : 2 * LANES] = unrope(second, rows).astype(BF16)
    for b in range(RING):
        rows = slice(b * ROWS, (b + 1) * ROWS)
        dqkv[rows, 2 * LANES : 3 * LANES] = unrope(dk[rows, :], rows).astype(BF16)
        dqkv[rows, 3 * LANES :] = dv[rows, :].astype(BF16)
        dn = dot_nt(dqkv[rows, : 2 * LANES], wq[...])
        dn = dn + dot_nt(dqkv[rows, 2 * LANES : 3 * LANES], wk[...])
        dn = (dn + dot_nt(dqkv[rows, 3 * LANES :], wv[...])).astype(BF16)
        relative = (b - me + RING) % RING
        for d, ref in enumerate((dn0, dn1, dn2, dn3)):

            @pl.when(relative == d)
            def _():
                ref[...] = dn

    for b in range(RING):
        rows = slice(b * ROWS, (b + 1) * ROWS)
        grad = dot_tn(normed[:, rows], dqkv[...])
        grads[rows, :] = grad.astype(BF16)
        terms = jnp.sum(wq[rows, :].astype(F32) * grad[:, : 2 * LANES], axis=1, keepdims=True)
        terms += jnp.sum(wk[rows, :].astype(F32) * grad[:, 2 * LANES : 3 * LANES], axis=1, keepdims=True)
        terms += jnp.sum(wv[rows, :].astype(F32) * grad[:, 3 * LANES :], axis=1, keepdims=True)
        dgain[rows, :] = terms / gain_col[rows, :]


def unattend(rank, q, k, v, lse, dmixed, normed, gain_col, wq, wk, wv, cos, sin, seg_col, seg_row):
    length = RING * ROWS
    return pl.pallas_call(
        unattend_kernel,
        out_shape=[jax.ShapeDtypeStruct((ROWS, WIDTH), BF16)] * RING
        + [jax.ShapeDtypeStruct((WIDTH, HALF), BF16), jax.ShapeDtypeStruct((WIDTH, 1), F32)],
        in_specs=[SCALARS] + [WHOLE] * 14,
        out_specs=[WHOLE] * 6,
        scratch_shapes=[
            pltpu.VMEM((LANES, length), BF16),
            pltpu.VMEM((3 * ROWS, ROWS), F32),
            pltpu.VMEM((length, LANES), F32),
            pltpu.VMEM((length, LANES), F32),
            pltpu.VMEM((length, HALF), BF16),
        ],
        compiler_params=params(),
        cost_estimate=pl.CostEstimate(flops=10_000_000_000, bytes_accessed=14_000_000, transcendentals=4_000_000),
        name="unattend",
    )(rank, q, k, v, lse, dmixed, normed, gain_col, wq, wk, wv, cos, sin, seg_col, seg_row)


def rope_tables(length):
    freqs = ROPE_BASE ** (-jnp.arange(HD // 2, dtype=F32) * 2.0 / HD)
    angles = jnp.arange(length, dtype=F32)[:, None] * freqs[None, :]
    cosine, sine = jnp.cos(angles), jnp.sin(angles)
    return jnp.concatenate([cosine] * 4, axis=1), jnp.concatenate([-sine, sine] * 2, axis=1)


def shards(
    hidden_in, segment_ids, expert_ids, slot_index, attn_gain, w_query, w_key, w_value, w_output,
    ffn_gain, w_router, w_gate_up, w_down, cotangent,
):
    length = RING * ROWS
    here, rank = lax.axis_index("ep"), lax.axis_index("tp")
    z, x, core = here // 8, (here // 2) % 4, here % 2
    rank_in = rank.astype(jnp.int32).reshape(1)

    named = expert_ids[:, :, None] == jnp.arange(EXPERTS, dtype=jnp.int32)[None, None, :]
    slot_of = jnp.sum(jnp.where(named, slot_index[:, :, None] + 1, 0), axis=1) - 1
    chosen = (slot_of >= 0).astype(F32)
    all_slots = lax.all_gather(slot_of.astype(F32).T, "ep", axis=0, tiled=True)

    near = jnp.arange(RING, dtype=jnp.int32)
    cores = jnp.arange(2, dtype=jnp.int32)
    four, mid, two = near[:, None, None], near[None, :, None], cores[None, None, :]
    rows_a = place(z + four, x, core) * EXPERTS + place(z, x + mid, core ^ two)
    rows_b = place(z, x + four, core) * EXPERTS + place(z + mid, x, core ^ two)
    blocks = place(z + near[None, None, :], x + near[:, None, None], core ^ cores[None, :, None]).reshape(-1)
    rows_e = blocks * EXPERTS + here
    slots_a = jnp.take(all_slots, rows_a.reshape(-1), axis=0)
    slots_b = jnp.take(all_slots, rows_b.reshape(-1), axis=0)
    slots_e = jnp.take(all_slots, rows_e, axis=0).reshape(STEPS, RING, ROWS)

    gain_one = attn_gain.astype(F32).reshape(1, WIDTH)
    gain_two = ffn_gain.astype(F32).reshape(1, WIDTH)
    cos, sin = rope_tables(length)
    seg_row = segment_ids
    seg_col = segment_ids.reshape(length, 1)

    group = [push_tp(hidden_in, -d) for d in range(RING)]
    cots = dispatch(slots_a, slots_b, cotangent[:, :HALF], cotangent[:, HALF:])
    made = attend(rank_in, group, gain_one, w_query, w_key, w_value, w_output, cos, sin, seg_col, seg_row)
    normed, q, k, v, mixed, lse = made[:6]
    branches = [push_tp(made[6 + d], d) for d in range(RING)]
    middle, half_a, half_b, gates_t = route(hidden_in, branches, gain_two, w_router, chosen)
    all_gates = lax.all_gather(gates_t, "ep", axis=0, tiled=True)
    gates_e = jnp.take(all_gates, rows_e, axis=0).reshape(STEPS, RING, ROWS)
    rows = dispatch(slots_a, slots_b, half_a, half_b)

    wgu = w_gate_up.reshape(WIDTH, 2 * HALF)
    wd = w_down.reshape(HALF, WIDTH)
    back, moe_slots, dgate_rows, disp, dgu, inner, dex = experts(
        slots_e, gates_e, wgu, wgu.T, wd, wd.T, rows, cots
    )
    devices = jnp.arange(EXPERTS, dtype=jnp.int32)
    dz, dx, dc = (devices // 8 - z) % 4, ((devices // 2) % 4 - x) % 4, (devices % 2) ^ core
    order = (dx * 2 + dc) * RING + dz
    dgates = jnp.take(dgate_rows.reshape(EXPERTS, ROWS), order, axis=0).reshape(EXPERTS, 1, ROWS)
    dgates_t = lax.all_to_all(dgates, "ep", split_axis=0, concat_axis=0, tiled=True).reshape(EXPERTS, ROWS)
    parts = combine(slots_a, slots_b, back)

    grad_gate_up = dot_tn(disp, dgu).astype(BF16)
    grad_down = dot_tn(inner, dex).astype(BF16)
    grad_gate_up, grad_down = lax.psum((grad_gate_up, grad_down), "tp")

    dmiddle, dbranch, sums = unroute(parts, gates_t, dgates_t, middle, cotangent, gain_two, w_router.T.astype(F32))
    sums = lax.psum(sums, ("ep", "tp"))
    group_grad = [push_tp(dbranch, -d) for d in range(RING)]

    moe_parts = combine(slots_a, slots_b, moe_slots)

    dmixed, grad_output = unmix(rank_in, group_grad, mixed, w_output)
    grad_output = lax.psum(grad_output, "ep")
    last = unattend(
        rank_in, q, k, v, lse, dmixed, normed, gain_one.reshape(WIDTH, 1), w_query, w_key, w_value, cos, sin,
        seg_col, seg_row,
    )
    grads = lax.psum(last[4], "ep")
    dgain = lax.all_gather(last[5].reshape(8, LANES), ("ep", "tp"), axis=0)
    grad_attn_gain = jnp.sum(dgain, axis=0).reshape(WIDTH)
    dn = [push_tp(last[d], d).astype(F32) for d in range(RING)]
    dnormed = (dn[0] + dn[1]) + (dn[2] + dn[3])

    local = hidden_in.astype(F32)
    inverse = lax.rsqrt(jnp.mean(local * local, axis=-1, keepdims=True) + NORM_EPS)
    plain = local * inverse
    scaled = dnormed * gain_one
    along = jnp.mean(scaled * plain, axis=-1, keepdims=True)
    grad_hidden = dmiddle + inverse * (scaled - plain * along)

    def four_sum(p):
        a, b, c, d = (piece.astype(F32) for piece in p)
        return (a + b) + (c + d)

    moe = jnp.concatenate([four_sum(moe_parts[:4]), four_sum(moe_parts[4:])], axis=1)
    output = (middle + RES_SCALE * moe).astype(BF16)
    return (
        output,
        grad_hidden,
        grad_attn_gain,
        grads[:, : 2 * LANES].astype(F32),
        grads[:, 2 * LANES : 3 * LANES].astype(F32),
        grads[:, 3 * LANES :].astype(F32),
        grad_output.astype(F32),
        sums[EXPERTS],
        sums[:EXPERTS].T,
        grad_gate_up.astype(F32).reshape(1, WIDTH, 2, HALF),
        grad_down.astype(F32).reshape(1, HALF, WIDTH),
    )


def solution(mesh):
    placed = (
        P(("ep", "tp"), None),
        P("ep", None),
        P(("ep", "tp"), None),
        P(("ep", "tp"), None),
        P(),
        P(None, "tp"),
        P(None, "tp"),
        P(None, "tp"),
        P("tp", None),
        P(),
        P(),
        P("ep", None, None, None),
        P("ep", None, None),
        P(("ep", "tp"), None),
    )
    return jax.shard_map(
        shards,
        mesh=mesh,
        in_specs=placed,
        out_specs=(
            P(("ep", "tp"), None),
            P(("ep", "tp"), None),
            P(),
            P(None, "tp"),
            P(None, "tp"),
            P(None, "tp"),
            P("tp", None),
            P(),
            P(),
            P("ep", None, None, None),
            P("ep", None, None),
        ),
        check_vma=False,
    )
```

```python
import jax
import jax.numpy as jnp
from jax import lax
from jax.experimental import pallas as pl
from jax.experimental.pallas import tpu as pltpu
from jax.sharding import PartitionSpec as P

HD = 64
ATT_SCALE = 0.015625
RES_SCALE = 0.22
NORM_EPS = 1e-06
ROPE_BASE = 10000.0
NEG_FILL = -1e30
HIGHEST = lax.Precision.HIGHEST
F32 = jnp.float32
BF16 = jnp.bfloat16

ROWS = 256
WIDTH = 1024
HALF = 512
CAP = 96
EXPERTS = 32
RING = 4
HEADS = 4
LANES = 128
VMEM_BYTES = 58 * 1024 * 1024
WHOLE = pl.BlockSpec(memory_space=pltpu.VMEM)
SCALARS = pl.BlockSpec(memory_space=pltpu.SMEM)
ANYWHERE = pl.BlockSpec(memory_space=pl.ANY)


def params():
    return pltpu.CompilerParams(vmem_limit_bytes=VMEM_BYTES)


NO_COST = pl.CostEstimate(flops=0, bytes_accessed=0, transcendentals=0)


def dot(a, b, precision=None):
    return jnp.dot(a, b, preferred_element_type=F32, precision=precision)


def dot_nt(a, b):
    return lax.dot_general(a, b, (((1,), (1,)), ((), ())), preferred_element_type=F32)


def dot_tn(a, b):
    return lax.dot_general(a, b, (((0,), (0,)), ((), ())), preferred_element_type=F32)


def place(z, x, core):
    return ((z % RING) * RING + (x % RING)) * 2 + core


def push(value, dz, dx, dc):
    if (dz % RING, dx % RING, dc) == (0, 0, 0):
        return value
    pairs = [
        (place(z, x, c), place(z + dz, x + dx, c ^ dc))
        for z in range(RING)
        for x in range(RING)
        for c in range(2)
    ]
    return lax.ppermute(value, "ep", pairs)


def push_tp(value, dy):
    if dy % RING == 0:
        return value
    return lax.ppermute(value, "tp", [(y, (y + dy) % RING) for y in range(RING)])


def after(values, *others):
    count = len(values)
    return pl.pallas_call(
        lambda *refs: None,
        out_shape=[jax.ShapeDtypeStruct(v.shape, v.dtype) for v in values],
        in_specs=[ANYWHERE] * (count + len(others)),
        out_specs=[ANYWHERE] * count,
        input_output_aliases={i: i for i in range(count)},
        cost_estimate=NO_COST,
        name="after",
    )(*values, *others)


def gather_tp(rows):
    after_me, before_me = push_tp(rows, -1), push_tp(rows, 1)
    half = rows.shape[0] // 2
    across = push_tp(after_me[:half], -1), push_tp(before_me[half:], 1)
    return rows, after_me, across, before_me


def scatter_tp(pieces):
    half = pieces[2].shape[0] // 2
    first, rest = push_tp(pieces[2][:half], 1), push_tp(pieces[2][half:], -1)
    ahead = (pieces[1][:half].astype(F32) + first.astype(F32)).astype(BF16)
    behind = (pieces[3][half:].astype(F32) + rest.astype(F32)).astype(BF16)
    ahead = jnp.concatenate([ahead, pieces[1][half:]], axis=0)
    behind = jnp.concatenate([pieces[3][:half], behind], axis=0)
    return pieces[0], push_tp(ahead, 1), push_tp(behind, -1)


def ignoring(kernel, first, count):
    return lambda *refs: kernel(*refs[:first], *refs[first + count :])


def swap_halves(v):
    lane = lax.broadcasted_iota(jnp.int32, v.shape, 1)
    return jnp.where(lane % HD < HD // 2, pltpu.roll(v, LANES - HD // 2, 1), pltpu.roll(v, HD // 2, 1))


def block_at(index):
    return pl.ds(pl.multiple_of(index * ROWS, ROWS), ROWS)


def key_range(block):
    return max(0, block - 2) * ROWS, (block + 1) * ROWS


def mask_bias(block, seg_col, seg_row):
    lo, hi = key_range(block)
    key_pos = lo + lax.broadcasted_iota(jnp.int32, (hi - lo, ROWS), 0)
    query_pos = block * ROWS + lax.broadcasted_iota(jnp.int32, (hi - lo, ROWS), 1)
    same = seg_col[lo:hi, :] == seg_row[:, block * ROWS : (block + 1) * ROWS]
    return jnp.where(same & (key_pos <= query_pos), 0.0, NEG_FILL)


def attend_kernel(
    rank, x0, x1, x2, x2_rest, x3, gain, wq, wk, wv, wo, cos, sin, seg_col, seg_row,
    normed, q_out, k_out, v_out, mixed, lse, br0, br1, br2, br3, vt, bias,
):
    me = rank[0]
    lane = lax.broadcasted_iota(jnp.int32, (ROWS, LANES), 1)
    for d, x_ref in enumerate((x0, x1, x2, x3)):
        at = block_at((me + d) % RING)
        x = jnp.concatenate([x2[...], x2_rest[...]], axis=0) if d == 2 else x_ref[...]
        x = x.astype(F32)
        inverse = lax.rsqrt(jnp.mean(x * x, axis=-1, keepdims=True) + NORM_EPS)
        low = (x * inverse * gain[...]).astype(BF16)
        normed[at, :] = low
        cos_here, sin_here = cos[at, :], sin[at, :]

        def rope(v):
            return v * cos_here + swap_halves(v) * sin_here

        query = dot(low, wq[...])
        for pair in range(2):
            q = rope(query[:, pair * LANES : (pair + 1) * LANES]) * ATT_SCALE
            other = pltpu.roll(q, HD, 1)
            keep = (lane < HD) if pair == 0 else (lane >= HD)
            first, second = (q, other) if pair == 0 else (other, q)
            at_head = 2 * pair * LANES
            q_out[at, at_head : at_head + LANES] = jnp.where(keep, first, 0.0).astype(BF16)
            q_out[at, at_head + LANES : at_head + 2 * LANES] = jnp.where(keep, second, 0.0).astype(BF16)
        k_out[at, :] = rope(dot(low, wk[...])).astype(BF16)
        v_out[at, :] = dot(low, wv[...]).astype(BF16)
    vt[...] = v_out[...].astype(F32).T.astype(BF16)
    for b in range(RING):
        lo, hi = key_range(b)
        rows = slice(b * ROWS, (b + 1) * ROWS)
        bias[0 : hi - lo, :] = mask_bias(b, seg_col, seg_row)
        outs = []
        for h in range(HEADS):
            q = q_out[rows, h * LANES : (h + 1) * LANES]
            scores = dot_nt(k_out[lo:hi, :], q) + bias[0 : hi - lo, :]
            top = jnp.max(scores, axis=0, keepdims=True)
            weights = jnp.exp(scores - top)
            total = jnp.sum(weights, axis=0, keepdims=True)
            out = dot(vt[:, lo:hi], weights.astype(BF16)) * (1.0 / total)
            outs.append(out.T)
            lse[h : h + 1, rows] = top + jnp.log(total)
        mixed[rows, 0:LANES] = jnp.where(lane < HD, outs[0], pltpu.roll(outs[1], HD, 1)).astype(BF16)
        mixed[rows, LANES:] = jnp.where(lane < HD, pltpu.roll(outs[2], HD, 1), outs[3]).astype(BF16)
        branch = dot(mixed[rows, :], wo[...]).astype(BF16)
        relative = (b - me + RING) % RING
        for d, br in enumerate((br0, br1, br2, br3)):

            @pl.when(relative == d)
            def _():
                br[...] = branch


def attend(rank, pieces, gain, wq, wk, wv, wo, cos, sin, seg_col, seg_row, *others):
    length = RING * ROWS
    return pl.pallas_call(
        ignoring(attend_kernel, 15, len(others)),
        out_shape=[
            jax.ShapeDtypeStruct((length, WIDTH), BF16),
            jax.ShapeDtypeStruct((length, HEADS * LANES), BF16),
            jax.ShapeDtypeStruct((length, LANES), BF16),
            jax.ShapeDtypeStruct((length, LANES), BF16),
            jax.ShapeDtypeStruct((length, HEADS * HD), BF16),
            jax.ShapeDtypeStruct((8, length), F32),
        ]
        + [jax.ShapeDtypeStruct((ROWS, WIDTH), BF16)] * RING,
        in_specs=[SCALARS] + [WHOLE] * 14 + [ANYWHERE] * len(others),
        out_specs=[WHOLE] * 10,
        scratch_shapes=[pltpu.VMEM((LANES, length), BF16), pltpu.VMEM((3 * ROWS, ROWS), F32)],
        compiler_params=params(),
        cost_estimate=NO_COST,
        name="attend",
    )(rank, pieces[0], pieces[1], *pieces[2], pieces[3], gain, wq, wk, wv, wo, cos, sin, seg_col, seg_row, *others)


def high_low(v):
    high = v.astype(BF16)
    return jnp.concatenate([high, (v - high.astype(F32)).astype(BF16)], axis=1)


def high_plus_low(v):
    return v[:, :ROWS].astype(F32) + v[:, ROWS:].astype(F32)


def route_kernel(x, b0, b1, b2, b3, gain, wr, chosen, middle, half_a, half_b, gates_t):
    branch = b0[...].astype(F32) + b1[...].astype(F32) + b2[...].astype(F32) + b3[...].astype(F32)
    mid = x[...].astype(F32) + RES_SCALE * branch
    middle[...] = mid
    inverse = lax.rsqrt(jnp.mean(mid * mid, axis=-1, keepdims=True) + NORM_EPS)
    routed = (mid * inverse * gain[...]).astype(BF16)
    half_b[...] = routed[:, HALF:]
    logits = jnp.where(chosen[...] > 0.0, dot(routed, wr[...]), NEG_FILL)
    weights = jnp.exp(logits - jnp.max(logits, axis=-1, keepdims=True))
    gates = (weights / jnp.sum(weights, axis=-1, keepdims=True)).T
    gates_t[...] = gates
    half_a[0:ROWS, :] = routed[:, :HALF]
    half_a[ROWS:, :] = high_low(gates)


def route(x, branches, gain, wr, chosen, *others):
    return pl.pallas_call(
        ignoring(route_kernel, 8, len(others)),
        out_shape=[
            jax.ShapeDtypeStruct((ROWS, WIDTH), F32),
            jax.ShapeDtypeStruct((ROWS + EXPERTS, HALF), BF16),
            jax.ShapeDtypeStruct((ROWS, HALF), BF16),
            jax.ShapeDtypeStruct((EXPERTS, ROWS), F32),
        ],
        in_specs=[WHOLE] * 8 + [ANYWHERE] * len(others),
        out_specs=[WHOLE] * 4,
        compiler_params=params(),
        cost_estimate=pl.CostEstimate(flops=20_000_000, bytes_accessed=5_000_000, transcendentals=8192),
        name="route",
    )(x, *branches, gain, wr, chosen, *others)


PIECE = 8 * CAP
EXTRA = 16


def line_row(d, p, e):
    return p * 8 + e * 4 + d


def slot_matrix(row):
    slot = lax.broadcasted_iota(jnp.int32, (CAP, ROWS), 0).astype(F32)
    return jnp.where(slot == row, 1.0, 0.0)


def line_matrix(slots, d):
    rows = [line_row(d, p, e) for p in range(RING) for e in range(2)]
    return jnp.concatenate([slot_matrix(slots[r : r + 1, :]).astype(BF16) for r in rows], axis=0)


def expert_row(spot, half, d, p, e):
    z, x, core = spot[1], spot[2], spot[3]
    if half == 0:
        x = (x + p) % RING
    else:
        z = (z + p) % RING
    return (z * RING + x) * 2 + (core + e) % 2


def fill_pieces(slots, rows, pieces):
    for d in range(RING):
        filled = dot(line_matrix(slots, d), rows[d][0:ROWS, :]).astype(BF16)
        for p in range(RING):
            for e in range(2):
                at = (e * 4 + d) * CAP
                pieces[p][at : at + CAP, :] = filled[(p * 2 + e) * CAP : (p * 2 + e + 1) * CAP, :]


def pick_rows(spot, half, blocks, table, picked):
    for d in range(RING):
        table[...] = blocks[d][ROWS:, :].astype(F32)
        for p in range(RING):
            for e in range(2):
                r = line_row(d, p, e)
                picked[r : r + 1, :] = table[pl.ds(expert_row(spot, half, d, p, e), 1), :]


def add_extra(pieces, picked):
    for p in range(RING):
        extra = picked[p * 8 : (p + 1) * 8, :]
        pieces[p][PIECE:, :] = jnp.concatenate([extra, jnp.zeros_like(extra)], axis=0).astype(BF16)


def dispatch_cot_kernel(spot, *refs):
    blocks, pieces, slots, (table, picked) = refs[:8], refs[8:16], refs[16:18], refs[18:]
    for half in range(2):
        mine = slice(4 * half, 4 * half + 4)
        pick_rows(spot, half, blocks[mine], table, picked)
        slots[half][...] = picked[:, :ROWS]
        fill_pieces(slots[half], blocks[mine], pieces[mine])
        if half == 0:
            add_extra(pieces[mine], picked)


def dispatch_rows_kernel(spot, slots_a, slots_b, *refs):
    blocks, pieces, (table, picked) = refs[:8], refs[8:16], refs[16:]
    fill_pieces(slots_a, blocks[:4], pieces[:4])
    fill_pieces(slots_b, blocks[4:], pieces[4:])
    pick_rows(spot, 0, blocks[:4], table, picked)
    add_extra(pieces[:4], picked)


def combine_kernel(with_extra, slots_a, slots_b, *refs):
    everyone = range(RING)
    for half, slots in enumerate((slots_a, slots_b)):
        pieces, rows = refs[4 * half : 4 * half + 4], refs[8 + 4 * half : 12 + 4 * half]
        for d in everyone:
            filled = jnp.concatenate(
                [pieces[p][(e * 4 + d) * CAP : (e * 4 + d + 1) * CAP, :] for p in everyone for e in range(2)], axis=0
            )
            rows[d][0:ROWS, :] = dot_tn(line_matrix(slots, d), filled).astype(BF16)
        if half == 0 and with_extra:
            tables = [pieces[p][PIECE:, :].astype(F32) for p in everyone]
            for d in everyone:
                picked = [tables[p][e * 4 + d : e * 4 + d + 1, :] for p in everyone for e in range(2)]
                extra = jnp.concatenate(picked + [jnp.zeros((8, HALF), F32)], axis=0)
                rows[d][ROWS:, :] = extra.astype(BF16)


SLOT_COST = pl.CostEstimate(flops=1_000_000_000, bytes_accessed=5_000_000, transcendentals=0)
TABLE = pltpu.VMEM((EXPERTS, HALF), F32)


def shape_of(rows, dtype=BF16):
    return jax.ShapeDtypeStruct((rows, HALF), dtype)


def payload_kernel(cot, table, half_a, half_b):
    for half, out in enumerate((half_a, half_b)):
        out[0:ROWS, :] = cot[:, half * HALF : (half + 1) * HALF]
        out[ROWS:, :] = table[...]


def payload(cot, table, *others):
    return pl.pallas_call(
        ignoring(payload_kernel, 2, len(others)),
        out_shape=[shape_of(ROWS + EXPERTS)] * 2,
        in_specs=[WHOLE] * 2 + [ANYWHERE] * len(others),
        out_specs=[WHOLE] * 2,
        compiler_params=params(),
        name="payload",
    )(cot, table, *others)


def spread_cot(cot, table, *others):
    half_a, half_b = payload(cot, table)
    a1, a3, b1 = push(half_a, -1, 0, 0), push(half_a, -3, 0, 0), push(half_b, 0, -1, 0)
    later_a, later_b = payload(cot, table, a1, a3, b1, *others)
    b3, a2, b2 = push(later_b, 0, -3, 0), push(later_a, -2, 0, 0), push(later_b, 0, -2, 0)
    return [half_a, a1, a2, a3, half_b, b1, b2, b3]


def spread_rows(half_a, half_b):
    return [push(half_a, -d, 0, 0) for d in range(RING)] + [push(half_b, 0, -d, 0) for d in range(RING)]


def made_pieces(kernel, operands, slot_outputs=0, others=()):
    count = len(operands)
    return pl.pallas_call(
        ignoring(kernel, count, len(others)),
        out_shape=[shape_of(PIECE + EXTRA)] * RING
        + [shape_of(PIECE)] * RING
        + [jax.ShapeDtypeStruct((EXPERTS, ROWS), F32)] * slot_outputs,
        in_specs=[SCALARS if v.ndim == 1 else WHOLE for v in operands] + [ANYWHERE] * len(others),
        out_specs=[WHOLE] * (8 + slot_outputs),
        scratch_shapes=[TABLE] * 2,
        compiler_params=params(),
        cost_estimate=SLOT_COST,
        name="dispatch",
    )(*operands, *others)


def exchange(pieces):
    got = exchange_near(pieces)
    got[2] = push(pieces[2], 0, 2, 0)
    (last,) = after((pieces[6],), got[5], got[7])
    got[6] = push(last, 2, 0, 0)
    return got


def exchange_near(pieces):
    got = [pieces[0], None, None, None, pieces[4], None, None, None]
    got[3], got[1] = push(pieces[1], 0, 1, 0), push(pieces[3], 0, 3, 0)
    got[7], got[5] = push(pieces[5], 1, 0, 0), push(pieces[7], 3, 0, 0)
    return got


def exchange_far(pieces, got, with_them, *others):
    held = after((pieces[2], pieces[6], *with_them), got[1], got[3], got[5], got[7], *others)
    got[2], got[6] = push(held[0], 0, 2, 0), push(held[1], 2, 0, 0)
    return held[2:]


def combine(slots_a, slots_b, pieces, with_extra, *others):
    rows_a = shape_of(ROWS + EXTRA) if with_extra else shape_of(ROWS)
    return pl.pallas_call(
        ignoring(lambda *refs: combine_kernel(with_extra, *refs), 10, len(others)),
        out_shape=[rows_a] * RING + [shape_of(ROWS)] * RING,
        in_specs=[WHOLE] * 10 + [ANYWHERE] * len(others),
        out_specs=[WHOLE] * 8,
        compiler_params=params(),
        cost_estimate=SLOT_COST,
        name="combine",
    )(slots_a, slots_b, *pieces, *others)


def to_owners(partial):
    got = [None] * 8
    for d in range(RING):
        got[-d % RING] = push(partial[d], d, 0, 0)
        got[4 + -d % RING] = push(partial[4 + d], 0, d, 0)
    return got


STEPS = 8
STEP_ROWS = RING * CAP


def expert_kernel(*refs):
    ra, rb, ca, cb = (refs[4 * i : 4 * i + 4] for i in range(4))
    weights = refs[16:18]
    qa, qb, ma, mb = (refs[18 + 4 * i : 22 + 4 * i] for i in range(4))
    disp_out, dgu_out, inner_out, dex_out = refs[34:38]
    wgu, wd, rows_in, cot_in, gates_in, slots_in, back_out, moe_out, dgate_out, extra_out = refs[38:48]
    weight_sem, in_sem, out_sem, extra_sem = refs[48:]
    step = pl.program_id(0)

    def loads(e):
        up, down = weights[e].at[pl.ds(0, WIDTH)], weights[e].at[pl.ds(WIDTH, HALF)]
        return [
            pltpu.make_async_copy(up, wgu.at[e], weight_sem.at[e, 0]),
            pltpu.make_async_copy(down, wd.at[e], weight_sem.at[e, 1]),
        ]

    def copies(j, groups, sems, outward):
        slot, e, dx, made = j % 2, j // 4, j % 4, []
        for which, (half_a, half_b, buf) in enumerate(groups):
            ends = [(half_a[dx].at[pl.ds(e * STEP_ROWS, STEP_ROWS)], buf.at[slot, :, pl.ds(0, HALF)])]
            for dz in range(RING):
                far = half_b[dz].at[pl.ds((e * 4 + dx) * CAP, CAP)]
                ends.append((far, buf.at[slot, pl.ds(dz * CAP, CAP), pl.ds(HALF, HALF)]))
            for n, (far, near) in enumerate(ends):
                source, target = (near, far) if outward else (far, near)
                made.append(pltpu.make_async_copy(source, target, sems.at[slot, which * 6 + n]))
        return made

    def fetches(j):
        made = copies(j, ((ra, rb, rows_in), (ca, cb, cot_in)), in_sem, False)
        slot, dx = j % 2, j % 4
        for which, (far, near) in enumerate(((ra, gates_in), (ca, slots_in))):
            made.append(
                pltpu.make_async_copy(far[dx].at[pl.ds(PIECE, EXTRA)], near.at[slot], in_sem.at[slot, which * 6 + 5])
            )
        return made

    def stores(j):
        return copies(j, ((qa, qb, back_out), (ma, mb, moe_out)), out_sem, True)

    for j in range(STEPS):

        @pl.when(step == j)
        def _():
            if j == 0:
                for copy in fetches(0) + loads(0) + loads(1):
                    copy.start()
            if j + 1 < STEPS:
                for copy in fetches(j + 1):
                    copy.start()
            for copy in fetches(j):
                copy.wait()
            if j % 4 == 0:
                for copy in loads(j // 4):
                    copy.wait()
            if j >= 2:
                for copy in stores(j - 2):
                    copy.wait()

    slot = step % 2
    e = step // 4
    gates = high_plus_low(gates_in[slot])
    slots = slots_in[slot].astype(F32)
    gates = jnp.where(e == 0, gates[0:4, :], gates[4:8, :])
    slots = jnp.where(e == 0, slots[0:4, :ROWS], slots[4:8, :ROWS])
    fills = [slot_matrix(slots[dz : dz + 1, :]) for dz in range(RING)]
    gate_slot = jnp.concatenate(
        [jnp.sum(fills[dz] * gates[dz : dz + 1, :], axis=1, keepdims=True) for dz in range(RING)], axis=0
    )
    rows = rows_in[slot]
    disp_out[...] = rows
    gate_up = dot(rows, wgu[e])
    gate, up = gate_up[:, :HALF], gate_up[:, HALF:]
    sigmoid = jax.nn.sigmoid(gate)
    silu = gate * sigmoid
    inner = (silu * up).astype(BF16)
    inner_out[...] = inner
    made = dot(inner, wd[e]).astype(BF16).astype(F32)
    dmoe = RES_SCALE * cot_in[slot].astype(F32)
    dgate_slot = jnp.sum(dmoe * made, axis=1, keepdims=True)
    dgates = [
        jnp.sum(fills[dz] * dgate_slot[dz * CAP : (dz + 1) * CAP, :], axis=0, keepdims=True) for dz in range(RING)
    ]
    at_row = pl.multiple_of((step % 4) * 8, 8)
    dgates = jnp.concatenate(dgates + dgates, axis=0)
    first = lax.broadcasted_iota(jnp.int32, (8, ROWS), 0) < 4
    dgate_out[pl.ds(at_row, 8), :] = jnp.where(first == (e == 0), dgates, dgate_out[pl.ds(at_row, 8), :])
    moe_out[slot] = (gate_slot * made).astype(BF16)
    dex = (gate_slot * dmoe).astype(BF16)
    dex_out[...] = dex
    dinner = dot_nt(dex, wd[e])
    dgate = dinner * up * sigmoid * (1.0 + gate * (1.0 - sigmoid))
    dgu = jnp.concatenate([dgate.astype(BF16), (dinner * silu).astype(BF16)], axis=1)
    dgu_out[...] = dgu
    back_out[slot] = dot_nt(dgu, wgu[e]).astype(BF16)

    for j in range(STEPS):

        @pl.when(step == j)
        def _():
            for copy in stores(j):
                copy.start()
            if j == STEPS - 1:
                last = []
                for dx in range(RING):
                    extra = high_low(dgate_out[dx * 8 : (dx + 1) * 8, :]).astype(F32)
                    extra_out[dx] = jnp.concatenate([extra, jnp.zeros_like(extra)], axis=0).astype(BF16)
                    last.append(
                        pltpu.make_async_copy(
                            extra_out.at[dx], qa[dx].at[pl.ds(PIECE, EXTRA)], extra_sem.at[dx]
                        )
                    )
                for copy in last:
                    copy.start()
                for copy in stores(j - 1) + stores(j) + last:
                    copy.wait()


def experts(rows, cots, weights):
    total = STEPS * STEP_ROWS
    wide = pl.BlockSpec((STEP_ROWS, WIDTH), lambda s: (s, 0))
    narrow = pl.BlockSpec((STEP_ROWS, HALF), lambda s: (s, 0))
    buf = pltpu.VMEM((2, STEP_ROWS, WIDTH), BF16)
    small = pltpu.VMEM((2, EXTRA, HALF), BF16)
    made = pl.pallas_call(
        expert_kernel,
        grid=(STEPS,),
        out_shape=[shape_of(PIECE + EXTRA)] * RING
        + [shape_of(PIECE)] * 12
        + [
            jax.ShapeDtypeStruct((total, WIDTH), BF16),
            jax.ShapeDtypeStruct((total, WIDTH), BF16),
            jax.ShapeDtypeStruct((total, HALF), BF16),
            jax.ShapeDtypeStruct((total, WIDTH), BF16),
        ],
        in_specs=[ANYWHERE] * 18,
        out_specs=[ANYWHERE] * 16 + [wide, wide, narrow, wide],
        scratch_shapes=[
            pltpu.VMEM((2, WIDTH, WIDTH), BF16),
            pltpu.VMEM((2, HALF, WIDTH), BF16),
            buf, buf, small, small, buf, buf,
            pltpu.VMEM((EXPERTS, ROWS), F32),
            pltpu.VMEM((RING, EXTRA, HALF), BF16),
            pltpu.SemaphoreType.DMA((2, 2)),
            pltpu.SemaphoreType.DMA((2, 12)),
            pltpu.SemaphoreType.DMA((2, 12)),
            pltpu.SemaphoreType.DMA((RING,)),
        ],
        compiler_params=params(),
        cost_estimate=pl.CostEstimate(flops=19_000_000_000, bytes_accessed=60_000_000, transcendentals=1_600_000),
        name="experts",
    )(*rows, *cots, *weights)
    return made[:8], made[8:16], made[16:]


def weight_grads_kernel(which, disp, dgu, inner, dex, out, disp_in, dgu_in, inner_in, dex_in, made, sems, out_sems):
    rows = pl.ds(which * 4 * STEP_ROWS, 4 * STEP_ROWS)
    pairs = ((disp, disp_in), (dgu, dgu_in), (inner, inner_in), (dex, dex_in))
    fetches = [pltpu.make_async_copy(far.at[rows], near, sems.at[i]) for i, (far, near) in enumerate(pairs)]
    stores = [
        pltpu.make_async_copy(made.at[pl.ds(i * HALF, HALF)], out.at[pl.ds(i * HALF, HALF)], out_sems.at[i])
        for i in range(3)
    ]
    for copy in fetches:
        copy.start()
    fetches[0].wait()
    fetches[1].wait()
    for i in range(2):
        made[i * HALF : (i + 1) * HALF, :] = dot_tn(disp_in[:, i * HALF : (i + 1) * HALF], dgu_in[...]).astype(BF16)
        stores[i].start()
    fetches[2].wait()
    fetches[3].wait()
    made[WIDTH:, :] = dot_tn(inner_in[...], dex_in[...]).astype(BF16)
    stores[2].start()
    for copy in stores:
        copy.wait()


def weight_grads(which, saved):
    wide, narrow = pltpu.VMEM((4 * STEP_ROWS, WIDTH), BF16), pltpu.VMEM((4 * STEP_ROWS, HALF), BF16)
    return pl.pallas_call(
        lambda *refs: weight_grads_kernel(which, *refs),
        out_shape=jax.ShapeDtypeStruct((WIDTH + HALF, WIDTH), BF16),
        in_specs=[ANYWHERE] * 4,
        out_specs=ANYWHERE,
        scratch_shapes=[
            wide, wide, narrow, wide, pltpu.VMEM((WIDTH + HALF, WIDTH), BF16),
            pltpu.SemaphoreType.DMA((4,)), pltpu.SemaphoreType.DMA((3,)),
        ],
        compiler_params=params(),
        cost_estimate=NO_COST,
        name="weight_grads",
    )(*saved)


def unroute_kernel(spot, *refs):
    parts, (gates_t, middle, cot, gain, wr_t, dmiddle, dbranch, sums, gates, dlogits) = refs[:8], refs[8:]

    def four(pieces):
        a, b, c, d = (piece[0:ROWS, :].astype(F32) for piece in pieces)
        return (a + b) + (c + d)

    order = [
        (((spot[1] + dz) % RING) * RING + (spot[2] + dx) % RING) * 2 + (spot[3] + e) % 2
        for dz in range(RING)
        for dx in range(RING)
        for e in range(2)
    ]
    for i, at in enumerate(order):
        gates[i : i + 1, :] = gates_t[pl.ds(at, 1), :]
    tables = [part[ROWS:, :].astype(F32) for part in parts[:4]]
    dgates = jnp.concatenate([t[0:8, :ROWS] + t[0:8, ROWS:] for t in tables], axis=0)
    made = gates[...] * (dgates - jnp.sum(gates[...] * dgates, axis=0, keepdims=True))
    for i, at in enumerate(order):
        dlogits[pl.ds(at, 1), :] = made[i : i + 1, :]
    drouted = jnp.concatenate([four(parts[:4]), four(parts[4:])], axis=1)
    drouted = drouted + dot(dlogits[...].T, wr_t[...], HIGHEST)
    mid = middle[...]
    inverse = lax.rsqrt(jnp.mean(mid * mid, axis=-1, keepdims=True) + NORM_EPS)
    plain = mid * inverse
    routed = (plain * gain[...]).astype(BF16).astype(F32)
    sums[0:EXPERTS, :] = dot(dlogits[...], routed, HIGHEST)
    sums[EXPERTS : EXPERTS + 8, :] = jnp.broadcast_to(jnp.sum(drouted * plain, axis=0, keepdims=True), (8, WIDTH))
    scaled = drouted * gain[...]
    along = jnp.mean(scaled * plain, axis=-1, keepdims=True)
    total = cot[...].astype(F32) + inverse * (scaled - plain * along)
    dmiddle[...] = total
    dbranch[...] = (RES_SCALE * total).astype(BF16)


def unroute(spot, parts, gates_t, middle, cot, gain, wr_t, *others):
    return pl.pallas_call(
        ignoring(unroute_kernel, 14, len(others)),
        out_shape=[
            jax.ShapeDtypeStruct((ROWS, WIDTH), F32),
            jax.ShapeDtypeStruct((ROWS, WIDTH), BF16),
            jax.ShapeDtypeStruct((EXPERTS + 8, WIDTH), F32),
        ],
        in_specs=[SCALARS] + [WHOLE] * 13 + [ANYWHERE] * len(others),
        out_specs=[WHOLE] * 3,
        scratch_shapes=[pltpu.VMEM((EXPERTS, ROWS), F32), pltpu.VMEM((EXPERTS, ROWS), F32)],
        compiler_params=params(),
        cost_estimate=pl.CostEstimate(flops=100_000_000_000, bytes_accessed=6_000_000, transcendentals=0),
        name="unroute",
    )(spot, *parts, gates_t, middle, cot, gain, wr_t, *others)


def unmix_kernel(rank, d0, d1, d2, d2_rest, d3, mixed, wo, dmixed, grad_out):
    me = rank[0]
    lane = lax.broadcasted_iota(jnp.int32, (ROWS, LANES), 1)
    for d, ref in enumerate((d0, d1, d2, d3)):
        at = block_at((me + d) % RING)
        grad = jnp.concatenate([d2[...], d2_rest[...]], axis=0) if d == 2 else ref[...]
        low = dot_nt(grad, wo[...])
        for pair in range(2):
            both = low[:, pair * LANES : (pair + 1) * LANES]
            other = pltpu.roll(both, HD, 1)
            keep = (lane < HD) if pair == 0 else (lane >= HD)
            first, second = (both, other) if pair == 0 else (other, both)
            at_head = 2 * pair * LANES
            dmixed[at, at_head : at_head + LANES] = jnp.where(keep, first, 0.0).astype(BF16)
            dmixed[at, at_head + LANES : at_head + 2 * LANES] = jnp.where(keep, second, 0.0).astype(BF16)
        term = dot_tn(mixed[at, :], grad)
        total = term if d == 0 else total + term
    grad_out[...] = total.astype(BF16)


def unmix(rank, pieces, mixed, wo, *others):
    length = RING * ROWS
    return pl.pallas_call(
        ignoring(unmix_kernel, 8, len(others)),
        out_shape=[
            jax.ShapeDtypeStruct((length, HEADS * LANES), BF16),
            jax.ShapeDtypeStruct((HEADS * HD, WIDTH), BF16),
        ],
        in_specs=[SCALARS] + [WHOLE] * 7 + [ANYWHERE] * len(others),
        out_specs=[WHOLE] * 2,
        compiler_params=params(),
        cost_estimate=pl.CostEstimate(flops=1_100_000_000, bytes_accessed=5_000_000, transcendentals=0),
        name="unmix",
    )(rank, pieces[0], pieces[1], *pieces[2], pieces[3], mixed, wo, *others)


def unattend_kernel(
    spot, q_in, k_in, v_in, lse, dmixed, normed, gain, wq, wk, wv, cos, sin, seg_col, seg_row,
    dqkv, dgain, dn0, dn1, dn2, dn3, kt, bias, dk, dv,
):
    me = spot[0]
    lane = lax.broadcasted_iota(jnp.int32, (ROWS, LANES), 1)
    kt[...] = k_in[...].astype(F32).T.astype(BF16)
    dk[...] = jnp.zeros_like(dk)
    dv[...] = jnp.zeros_like(dv)

    def unrope(v, rows):
        return v * cos[rows, :] - swap_halves(v) * sin[rows, :]

    for b in range(RING):
        lo, hi = key_range(b)
        rows = slice(b * ROWS, (b + 1) * ROWS)
        bias[0 : hi - lo, :] = mask_bias(b, seg_col, seg_row)
        dqs = []
        for h in range(HEADS):
            cols = slice(h * LANES, (h + 1) * LANES)
            q, do = q_in[rows, cols], dmixed[rows, cols]
            scores = dot_nt(k_in[lo:hi, :], q) + bias[0 : hi - lo, :]
            probs = jnp.exp(scores - lse[h : h + 1, rows])
            dprobs = dot_nt(v_in[lo:hi, :], do)
            delta = jnp.sum(probs * dprobs, axis=0, keepdims=True)
            dscores = (probs * (dprobs - delta)).astype(BF16)
            dv[lo:hi, :] += dot(probs.astype(BF16), do)
            dk[lo:hi, :] += dot(dscores, q)
            dqs.append(dot(kt[:, lo:hi], dscores).T * ATT_SCALE)
        first = jnp.where(lane < HD, dqs[0], pltpu.roll(dqs[1], HD, 1))
        second = jnp.where(lane < HD, pltpu.roll(dqs[2], HD, 1), dqs[3])
        dqkv[rows, 0:LANES] = unrope(first, rows).astype(BF16)
        dqkv[rows, LANES : 2 * LANES] = unrope(second, rows).astype(BF16)
    for b in range(RING):
        rows = slice(b * ROWS, (b + 1) * ROWS)
        dqkv[rows, 2 * LANES : 3 * LANES] = unrope(dk[rows, :], rows).astype(BF16)
        dqkv[rows, 3 * LANES :] = dv[rows, :].astype(BF16)
        dn = dot_nt(dqkv[rows, : 2 * LANES], wq[...])
        dn = dn + dot_nt(dqkv[rows, 2 * LANES : 3 * LANES], wk[...])
        dn = dn + dot_nt(dqkv[rows, 3 * LANES :], wv[...])
        term = jnp.sum(dn * normed[rows, :].astype(F32), axis=0, keepdims=True)
        gain_sum = term if b == 0 else gain_sum + term
        dn = dn.astype(BF16)
        relative = (b - me + RING) % RING
        for d, ref in enumerate((dn0, dn1, dn2, dn3)):

            @pl.when(relative == d)
            def _():
                ref[...] = dn

    dgain[...] = jnp.broadcast_to(gain_sum / gain[...], (8, WIDTH))


def unattend(spot, q, k, v, lse, dmixed, normed, gain, wq, wk, wv, cos, sin, seg_col, seg_row):
    length = RING * ROWS
    return pl.pallas_call(
        unattend_kernel,
        out_shape=[
            jax.ShapeDtypeStruct((length, HALF), BF16),
            jax.ShapeDtypeStruct((8, WIDTH), F32),
        ]
        + [jax.ShapeDtypeStruct((ROWS, WIDTH), BF16)] * RING,
        in_specs=[SCALARS] + [WHOLE] * 14,
        out_specs=[WHOLE] * 6,
        scratch_shapes=[
            pltpu.VMEM((LANES, length), BF16),
            pltpu.VMEM((3 * ROWS, ROWS), F32),
            pltpu.VMEM((length, LANES), F32),
            pltpu.VMEM((length, LANES), F32),
        ],
        compiler_params=params(),
        cost_estimate=pl.CostEstimate(flops=300_000_000_000, bytes_accessed=14_000_000, transcendentals=4_000_000),
        name="unattend",
    )(spot, q, k, v, lse, dmixed, normed, gain, wq, wk, wv, cos, sin, seg_col, seg_row)


PAY = 832
QUARTER = PAY // RING
GAINS = 768 + EXPERTS


def pack_kernel(spot, normed, dqkv, grad_out, s0, s1, s2, s3, own, other):
    core = spot[3]
    sums = (s0[...] + s1[...]) + (s2[...] + s3[...])
    row = lax.broadcasted_iota(jnp.int32, (32, HALF), 0)
    for side, out in enumerate((own, other)):
        cols = pl.ds(pl.multiple_of(((core + side) % 2) * HALF, HALF), HALF)
        left = (core + side) % 2 == 0
        out[0:HALF, :] = dot_tn(normed[:, cols], dqkv[...]).astype(BF16)
        out[HALF:768, :] = grad_out[:, cols]
        here = jnp.where(left, sums[:, :HALF], sums[:, HALF:])
        out[768:GAINS, :] = here[0:EXPERTS, :].astype(BF16)
        out[GAINS:, :] = jnp.where(row == 0, here[EXPERTS : EXPERTS + 1, :], 0.0).astype(BF16)


def add_all(refs):
    total = refs[0][...].astype(F32)
    for ref in refs[1:]:
        total = total + ref[...].astype(F32)
    return total.astype(BF16)


def quarter_rows(index):
    return pl.ds(pl.multiple_of(index * QUARTER, 16), QUARTER)


def reduce_core_kernel(spot, own, got, g0, g1, g2, g3, p0, p1, p2, p3, total):
    total[...] = add_all((own, got))
    gain = (g0[...] + g1[...]) + (g2[...] + g3[...])
    mine = jnp.where(spot[3] == 0, gain[0:1, :HALF], gain[0:1, HALF:])
    row = lax.broadcasted_iota(jnp.int32, (32, HALF), 0)
    total[GAINS:, :] = jnp.where(row == 1, mine, total[GAINS:, :].astype(F32)).astype(BF16)
    for d, piece in enumerate((p0, p1, p2, p3)):
        piece[...] = total[quarter_rows((spot[2] + d) % RING), :]


def sum_kernel(spot, a, b, c, d, out):
    out[...] = add_all((a, b, c, d))


def gather_x_kernel(spot, a, b, c, d, out):
    for d, piece in enumerate((a, b, c, d)):
        out[quarter_rows((spot[2] + d) % RING), :] = piece[...]


def unpack_kernel(spot, own, got, query, key, value, grad_out, router, gains):
    for side, half in enumerate((own, got)):
        at = pl.ds(pl.multiple_of(((spot[3] + side) % 2) * HALF, HALF), HALF)
        query[at, :] = half[0:HALF, : 2 * LANES].astype(F32)
        key[at, :] = half[0:HALF, 2 * LANES : 3 * LANES].astype(F32)
        value[at, :] = half[0:HALF, 3 * LANES :].astype(F32)
        grad_out[:, at] = half[HALF:768, :].astype(F32)
        router[:, at] = half[768:GAINS, :].astype(F32)
        gains[:, at] = half[GAINS:, :].astype(F32)[0:8, :]


def small_call(kernel, spot, refs, shapes, scratch=None, flops=1_000_000, others=()):
    return pl.pallas_call(
        ignoring(kernel, 1 + len(refs), len(others)),
        out_shape=[jax.ShapeDtypeStruct(shape, dtype) for shape, dtype in shapes],
        in_specs=[SCALARS] + [WHOLE] * len(refs) + [ANYWHERE] * len(others),
        out_specs=[WHOLE] * len(shapes),
        scratch_shapes=[pltpu.VMEM(scratch, BF16)] if scratch else [],
        compiler_params=params(),
        cost_estimate=pl.CostEstimate(flops=flops, bytes_accessed=2_000_000, transcendentals=0),
    )(spot, *refs, *others)


def sum_over_ep(spot, normed, dqkv, grad_out, sums, gains, moe_got, beside, finished):
    own, other = small_call(
        pack_kernel, spot, (normed, dqkv, grad_out, *sums), [((PAY, HALF), BF16)] * 2, flops=0, others=moe_got
    )
    got = push(other, 0, 0, 1)
    pieces = small_call(
        reduce_core_kernel, spot, (own, got, *gains), [((QUARTER, HALF), BF16)] * 4, (PAY, HALF)
    )
    beside[0](pieces[0])
    pieces = [push(pieces[d], 0, d, 0) for d in range(RING)]
    quarter = [((QUARTER, HALF), BF16)]
    (line,) = small_call(sum_kernel, spot, pieces, quarter)
    beside[1](line)
    (line,) = small_call(sum_kernel, spot, [push(line, d, 0, 0) for d in range(RING)], quarter)
    beside[2](line)
    pieces = [push(line, 0, -d, 0) for d in range(RING)]
    (half,) = small_call(gather_x_kernel, spot, pieces, [((PAY, HALF), BF16)], others=finished)
    made = small_call(
        unpack_kernel,
        spot,
        (half, push(half, 0, 0, 1)),
        [
            ((WIDTH, 2 * LANES), F32),
            ((WIDTH, LANES), F32),
            ((WIDTH, LANES), F32),
            ((ROWS, WIDTH), F32),
            ((EXPERTS, WIDTH), F32),
            ((8, WIDTH), F32),
        ],
    )
    return made


def rope_tables(length):
    freqs = ROPE_BASE ** (-jnp.arange(HD // 2, dtype=F32) * 2.0 / HD)
    angles = jnp.arange(length, dtype=F32)[:, None] * freqs[None, :]
    cosine, sine = jnp.cos(angles), jnp.sin(angles)
    return jnp.concatenate([cosine] * 4, axis=1), jnp.concatenate([-sine, sine] * 2, axis=1)


def shards(
    hidden_in, segment_ids, expert_ids, slot_index, attn_gain, w_query, w_key, w_value, w_output,
    ffn_gain, w_router, w_gate_up, w_down, cotangent,
):
    length = RING * ROWS
    here, rank = lax.axis_index("ep"), lax.axis_index("tp")
    spot = jnp.stack([rank, here // 8, (here // 2) % 4, here % 2]).astype(jnp.int32)

    named = expert_ids[:, :, None] == jnp.arange(EXPERTS, dtype=jnp.int32)[None, None, :]
    slot_of = jnp.sum(jnp.where(named, slot_index[:, :, None] + 1, 0), axis=1) - 1
    chosen = (slot_of >= 0).astype(F32)
    table = jnp.pad(slot_of.T.astype(BF16), ((0, 0), (0, HALF - ROWS)))

    gain_one = attn_gain.astype(F32).reshape(1, WIDTH)
    gain_two = ffn_gain.astype(F32).reshape(1, WIDTH)
    cos, sin = rope_tables(length)
    seg_row = segment_ids
    seg_col = segment_ids.reshape(length, 1)

    group = gather_tp(hidden_in)
    blocks = spread_cot(cotangent, table, group[1], group[3])
    made = made_pieces(dispatch_cot_kernel, (spot, *blocks), 2, (*group[2], cos, sin, seg_col))
    slots_a, slots_b = made[8:]
    cot_pieces = made[:8]
    cots = exchange_near(cot_pieces)
    weights = jnp.concatenate([w_gate_up.reshape(WIDTH, 2 * HALF), w_down.reshape(HALF, WIDTH)], axis=0)
    (weights,) = after((weights,), slots_a)
    weights = weights, push(weights, 0, 0, 1)

    made = attend(spot, group, gain_one, w_query, w_key, w_value, w_output, cos, sin, seg_col, seg_row, slots_a)
    normed, q, k, v, mixed, lse = made[:6]
    sent = exchange_far(cot_pieces, cots, made[7:10], lse, weights[1])
    branches = [made[6]] + [push_tp(sent[d], d + 1) for d in range(RING - 1)]
    middle, half_a, half_b, gates_t = route(
        hidden_in, branches, gain_two, w_router, chosen, cots[2], cots[6]
    )
    blocks = spread_rows(half_a, half_b)
    rows = exchange(made_pieces(dispatch_rows_kernel, (spot, slots_a, slots_b, *blocks)))

    back, moe_slots, saved = experts(rows, cots, weights)
    got = exchange_near(back)
    (grads_other,) = exchange_far(back, got, (weight_grads(1, saved),))
    grads_other = push(grads_other, 0, 0, 1)
    grads_own = weight_grads(0, saved)
    grads_e = (grads_own.astype(F32) + grads_other.astype(F32)).astype(BF16)
    parts = to_owners(combine(slots_a, slots_b, got, True, grads_e))

    dmiddle, dbranch, sums = unroute(
        spot, parts, gates_t, middle, cotangent, gain_two, w_router.T.astype(F32), grads_e
    )
    grads_e = lax.psum_scatter(grads_e, "tp", scatter_dimension=0, tiled=True)
    group_grad = gather_tp(dbranch)
    sums = [push_tp(sums, d) for d in range(RING)]

    moe_got = [moe_slots[0], None, None, None, moe_slots[4], None, None, None]
    one, two, three = after((moe_slots[1], moe_slots[3], moe_slots[5]), dbranch)
    moe_got[3], moe_got[1], moe_got[7] = push(one, 0, 1, 0), push(two, 0, 3, 0), push(three, 1, 0, 0)
    one, two = after((moe_slots[7], moe_slots[2]), moe_got[3], moe_got[1], moe_got[7])
    moe_got[5], moe_got[2] = push(one, 3, 0, 0), push(two, 0, 2, 0)
    (one,) = after((moe_slots[6],), moe_got[5], moe_got[2])
    moe_got[6] = push(one, 2, 0, 0)

    (grads_e,) = after((grads_e,), *group_grad[2])
    grads_e = lax.all_gather(grads_e, "tp", axis=0, tiled=True).astype(F32)
    grad_up = grads_e[:WIDTH].reshape(1, WIDTH, 2, HALF)
    grad_down = grads_e[WIDTH:].reshape(1, HALF, WIDTH)
    dmixed, grad_output = unmix(spot, group_grad, mixed, w_output, moe_got[1], moe_got[3], moe_got[7], *sums[1:])
    last = unattend(
        spot, q, k, v, lse, dmixed, normed, gain_one, w_query, w_key, w_value, cos, sin, seg_col, seg_row
    )
    gain = last[1] + push(last[1], 0, 0, 1)
    gains = [push_tp(gain, d) for d in range(RING)]
    dn, moe_parts = [], []

    def beside_x(piece):
        dn.extend(scatter_tp(after(last[2:6], piece)))

    def beside_z(line):
        moe_parts.extend(combine(slots_a, slots_b, after(moe_got, line), False))

    def beside_last(line):
        moe_parts[:] = to_owners(after(moe_parts, line))

    grad_query, grad_key, grad_value, grad_output, grad_router, grad_gains = sum_over_ep(
        spot, normed, last[0], grad_output, sums, gains, (moe_got[2], moe_got[5]), (beside_x, beside_z, beside_last),
        (grad_up, grad_down),
    )
    dnormed = dn[0].astype(F32) + dn[1].astype(F32) + dn[2].astype(F32)

    local = hidden_in.astype(F32)
    inverse = lax.rsqrt(jnp.mean(local * local, axis=-1, keepdims=True) + NORM_EPS)
    plain = local * inverse
    scaled = dnormed * gain_one
    along = jnp.mean(scaled * plain, axis=-1, keepdims=True)
    grad_hidden = dmiddle + inverse * (scaled - plain * along)

    def four_sum(p):
        a, b, c, d = (piece.astype(F32) for piece in p)
        return (a + b) + (c + d)

    moe = jnp.concatenate([four_sum(moe_parts[:4]), four_sum(moe_parts[4:])], axis=1)
    output = (middle + RES_SCALE * moe).astype(BF16)
    return (
        output,
        grad_hidden,
        grad_gains[1],
        grad_query,
        grad_key,
        grad_value,
        grad_output,
        grad_gains[0],
        grad_router.T,
        grad_up,
        grad_down,
    )


def solution(mesh):
    placed = (
        P(("ep", "tp"), None),
        P("ep", None),
        P(("ep", "tp"), None),
        P(("ep", "tp"), None),
        P(),
        P(None, "tp"),
        P(None, "tp"),
        P(None, "tp"),
        P("tp", None),
        P(),
        P(),
        P("ep", None, None, None),
        P("ep", None, None),
        P(("ep", "tp"), None),
    )
    return jax.shard_map(
        shards,
        mesh=mesh,
        in_specs=placed,
        out_specs=(
            P(("ep", "tp"), None),
            P(("ep", "tp"), None),
            P(),
            P(None, "tp"),
            P(None, "tp"),
            P(None, "tp"),
            P("tp", None),
            P(),
            P(),
            P("ep", None, None, None),
            P("ep", None, None),
        ),
        check_vma=False,
    )
```

```python
import jax
import jax.numpy as jnp
from jax import lax
from jax.experimental import pallas as pl
from jax.experimental.pallas import tpu as pltpu
from jax.sharding import PartitionSpec as P

HD = 64
ATT_SCALE = 0.015625
RES_SCALE = 0.22
NORM_EPS = 1e-06
ROPE_BASE = 10000.0
NEG_FILL = -1e30
HIGHEST = lax.Precision.HIGHEST
F32 = jnp.float32
BF16 = jnp.bfloat16

ROWS = 256
WIDTH = 1024
HALF = 512
CAP = 96
EXPERTS = 32
RING = 4
HEADS = 4
LANES = 128
VMEM_BYTES = 58 * 1024 * 1024
WHOLE = pl.BlockSpec(memory_space=pltpu.VMEM)
SCALARS = pl.BlockSpec(memory_space=pltpu.SMEM)
ANYWHERE = pl.BlockSpec(memory_space=pl.ANY)


def params():
    return pltpu.CompilerParams(vmem_limit_bytes=VMEM_BYTES)


NO_COST = pl.CostEstimate(flops=0, bytes_accessed=0, transcendentals=0)


def dot(a, b, precision=None):
    return jnp.dot(a, b, preferred_element_type=F32, precision=precision)


def dot_nt(a, b):
    return lax.dot_general(a, b, (((1,), (1,)), ((), ())), preferred_element_type=F32)


def dot_tn(a, b):
    return lax.dot_general(a, b, (((0,), (0,)), ((), ())), preferred_element_type=F32)


def place(z, x, core):
    return ((z % RING) * RING + (x % RING)) * 2 + core


def push(value, dz, dx, dc):
    if (dz % RING, dx % RING, dc) == (0, 0, 0):
        return value
    pairs = [
        (place(z, x, c), place(z + dz, x + dx, c ^ dc))
        for z in range(RING)
        for x in range(RING)
        for c in range(2)
    ]
    return lax.ppermute(value, "ep", pairs)


def push_tp(value, dy):
    if dy % RING == 0:
        return value
    return lax.ppermute(value, "tp", [(y, (y + dy) % RING) for y in range(RING)])


def after(values, *others):
    count = len(values)
    return pl.pallas_call(
        lambda *refs: None,
        out_shape=[jax.ShapeDtypeStruct(v.shape, v.dtype) for v in values],
        in_specs=[ANYWHERE] * (count + len(others)),
        out_specs=[ANYWHERE] * count,
        input_output_aliases={i: i for i in range(count)},
        cost_estimate=NO_COST,
        name="after",
    )(*values, *others)


def gather_tp(rows):
    after_me, before_me = push_tp(rows, -1), push_tp(rows, 1)
    half = rows.shape[0] // 2
    across = push_tp(after_me[:half], -1), push_tp(before_me[half:], 1)
    return rows, after_me, across, before_me


def scatter_tp(pieces):
    half = pieces[2].shape[0] // 2
    first, rest = push_tp(pieces[2][:half], 1), push_tp(pieces[2][half:], -1)
    ahead = (pieces[1][:half].astype(F32) + first.astype(F32)).astype(BF16)
    behind = (pieces[3][half:].astype(F32) + rest.astype(F32)).astype(BF16)
    ahead = jnp.concatenate([ahead, pieces[1][half:]], axis=0)
    behind = jnp.concatenate([pieces[3][:half], behind], axis=0)
    return (pieces[0], push_tp(ahead, 1), push_tp(behind, -1)), (first, rest)


def ignoring(kernel, first, count):
    return lambda *refs: kernel(*refs[:first], *refs[first + count :])


def swap_halves(v):
    lane = lax.broadcasted_iota(jnp.int32, v.shape, 1)
    return jnp.where(lane % HD < HD // 2, pltpu.roll(v, LANES - HD // 2, 1), pltpu.roll(v, HD // 2, 1))


def block_at(index):
    return pl.ds(pl.multiple_of(index * ROWS, ROWS), ROWS)


def key_range(block):
    return max(0, block - 2) * ROWS, (block + 1) * ROWS


def mask_bias(block, seg_col, seg_row):
    lo, hi = key_range(block)
    key_pos = lo + lax.broadcasted_iota(jnp.int32, (hi - lo, ROWS), 0)
    query_pos = block * ROWS + lax.broadcasted_iota(jnp.int32, (hi - lo, ROWS), 1)
    same = seg_col[lo:hi, :] == seg_row[:, block * ROWS : (block + 1) * ROWS]
    return jnp.where(same & (key_pos <= query_pos), 0.0, NEG_FILL)


def attend_kernel(
    rank, x0, x1, x2, x3, gain, wq, wk, wv, wo, cos, sin, seg_col, seg_row,
    normed, q_out, k_out, v_out, mixed, lse, br0, br1, br2, br3, vt, bias,
):
    me = rank[0]
    lane = lax.broadcasted_iota(jnp.int32, (ROWS, LANES), 1)
    for d, x_ref in enumerate((x0, x1, x2, x3)):
        at = block_at((me + d) % RING)
        x = x_ref[...].astype(F32)
        inverse = lax.rsqrt(jnp.mean(x * x, axis=-1, keepdims=True) + NORM_EPS)
        low = (x * inverse * gain[...]).astype(BF16)
        normed[at, :] = low
        cos_here, sin_here = cos[at, :], sin[at, :]

        def rope(v):
            return v * cos_here + swap_halves(v) * sin_here

        query = dot(low, wq[...])
        for pair in range(2):
            q = rope(query[:, pair * LANES : (pair + 1) * LANES]) * ATT_SCALE
            other = pltpu.roll(q, HD, 1)
            keep = (lane < HD) if pair == 0 else (lane >= HD)
            first, second = (q, other) if pair == 0 else (other, q)
            at_head = 2 * pair * LANES
            q_out[at, at_head : at_head + LANES] = jnp.where(keep, first, 0.0).astype(BF16)
            q_out[at, at_head + LANES : at_head + 2 * LANES] = jnp.where(keep, second, 0.0).astype(BF16)
        k_out[at, :] = rope(dot(low, wk[...])).astype(BF16)
        v_out[at, :] = dot(low, wv[...]).astype(BF16)
    vt[...] = v_out[...].astype(F32).T.astype(BF16)
    for b in range(RING):
        lo, hi = key_range(b)
        rows = slice(b * ROWS, (b + 1) * ROWS)
        bias[0 : hi - lo, :] = mask_bias(b, seg_col, seg_row)
        outs = []
        for h in range(HEADS):
            q = q_out[rows, h * LANES : (h + 1) * LANES]
            scores = dot_nt(k_out[lo:hi, :], q) + bias[0 : hi - lo, :]
            top = jnp.max(scores, axis=0, keepdims=True)
            weights = jnp.exp(scores - top)
            total = jnp.sum(weights, axis=0, keepdims=True)
            out = dot(vt[:, lo:hi], weights.astype(BF16)) * (1.0 / total)
            outs.append(out.T)
            lse[h : h + 1, rows] = top + jnp.log(total)
        mixed[rows, 0:LANES] = jnp.where(lane < HD, outs[0], pltpu.roll(outs[1], HD, 1)).astype(BF16)
        mixed[rows, LANES:] = jnp.where(lane < HD, pltpu.roll(outs[2], HD, 1), outs[3]).astype(BF16)
        branch = dot(mixed[rows, :], wo[...]).astype(BF16)
        relative = (b - me + RING) % RING
        for d, br in enumerate((br0, br1, br2, br3)):

            @pl.when(relative == d)
            def _():
                br[...] = branch


def attend(rank, pieces, gain, wq, wk, wv, wo, cos, sin, seg_col, seg_row, *others):
    length = RING * ROWS
    return pl.pallas_call(
        ignoring(attend_kernel, 14, len(others)),
        out_shape=[
            jax.ShapeDtypeStruct((length, WIDTH), BF16),
            jax.ShapeDtypeStruct((length, HEADS * LANES), BF16),
            jax.ShapeDtypeStruct((length, LANES), BF16),
            jax.ShapeDtypeStruct((length, LANES), BF16),
            jax.ShapeDtypeStruct((length, HEADS * HD), BF16),
            jax.ShapeDtypeStruct((8, length), F32),
        ]
        + [jax.ShapeDtypeStruct((ROWS, WIDTH), BF16)] * RING,
        in_specs=[SCALARS] + [WHOLE] * 13 + [ANYWHERE] * len(others),
        out_specs=[WHOLE] * 10,
        scratch_shapes=[pltpu.VMEM((LANES, length), BF16), pltpu.VMEM((3 * ROWS, ROWS), F32)],
        compiler_params=params(),
        cost_estimate=NO_COST,
        name="attend",
    )(rank, *pieces, gain, wq, wk, wv, wo, cos, sin, seg_col, seg_row, *others)


def high_low(v):
    high = v.astype(BF16)
    return jnp.concatenate([high, (v - high.astype(F32)).astype(BF16)], axis=1)


def route_kernel(x, b0, b1, b2, b3, gain, wr, chosen, table, middle, half_a, half_b, gates_t):
    branch = b0[...].astype(F32) + b1[...].astype(F32) + b2[...].astype(F32) + b3[...].astype(F32)
    mid = x[...].astype(F32) + RES_SCALE * branch
    middle[...] = mid
    inverse = lax.rsqrt(jnp.mean(mid * mid, axis=-1, keepdims=True) + NORM_EPS)
    routed = (mid * inverse * gain[...]).astype(BF16)
    half_b[0:ROWS, :] = routed[:, HALF:]
    logits = jnp.where(chosen[...] > 0.0, dot(routed, wr[...]), NEG_FILL)
    weights = jnp.exp(logits - jnp.max(logits, axis=-1, keepdims=True))
    gates = (weights / jnp.sum(weights, axis=-1, keepdims=True)).T
    gates_t[...] = gates
    half_a[0:ROWS, :] = routed[:, :HALF]
    half_a[ROWS : ROWS + EXPERTS, :] = high_low(gates)
    slots = jnp.concatenate([table[...], jnp.zeros_like(gates)], axis=1).astype(BF16)
    half_a[ROWS + EXPERTS :, :] = slots
    half_b[ROWS:, :] = slots


def route(x, branches, gain, wr, chosen, table, *others):
    return pl.pallas_call(
        ignoring(route_kernel, 9, len(others)),
        out_shape=[
            jax.ShapeDtypeStruct((ROWS, WIDTH), F32),
            jax.ShapeDtypeStruct((ROWS + 2 * EXPERTS, HALF), BF16),
            jax.ShapeDtypeStruct((ROWS + EXPERTS, HALF), BF16),
            jax.ShapeDtypeStruct((EXPERTS, ROWS), F32),
        ],
        in_specs=[WHOLE] * 9 + [ANYWHERE] * len(others),
        out_specs=[WHOLE] * 4,
        compiler_params=params(),
        cost_estimate=pl.CostEstimate(flops=20_000_000, bytes_accessed=5_000_000, transcendentals=8192),
        name="route",
    )(x, *branches, gain, wr, chosen, table, *others)


PIECE = 8 * CAP
EXTRA = 16


def line_row(d, p, e):
    return p * 8 + e * 4 + d


def slot_matrix(row):
    slot = lax.broadcasted_iota(jnp.int32, (CAP, ROWS), 0).astype(F32)
    return jnp.where(slot == row, 1.0, 0.0)


def line_matrix(slots, d):
    rows = [line_row(d, p, e) for p in range(RING) for e in range(2)]
    return jnp.concatenate([slot_matrix(slots[r : r + 1, :]).astype(BF16) for r in rows], axis=0)


def expert_row(spot, half, d, p, e):
    z, x, core = spot[1], spot[2], spot[3]
    if half == 0:
        x = (x + p) % RING
    else:
        z = (z + p) % RING
    return (z * RING + x) * 2 + (core + e) % 2


def fill_pieces(slots, rows, pieces):
    for d in range(RING):
        filled = dot(line_matrix(slots, d), rows[d][0:ROWS, :]).astype(BF16)
        for p in range(RING):
            for e in range(2):
                at = (e * 4 + d) * CAP
                pieces[p][at : at + CAP, :] = filled[(p * 2 + e) * CAP : (p * 2 + e + 1) * CAP, :]


def pick_rows(spot, half, blocks, first, table, picked):
    for d in range(RING):
        table[...] = blocks[d][first : first + EXPERTS, :].astype(F32)
        for p in range(RING):
            for e in range(2):
                r = line_row(d, p, e)
                picked[r : r + 1, :] = table[pl.ds(expert_row(spot, half, d, p, e), 1), :]


def dispatch_kernel(spot, *refs):
    blocks, pieces, slots, (table, gates, picked) = refs[:8], refs[8:16], refs[16:18], refs[18:]
    pick_rows(spot, 0, blocks[:4], ROWS, table, gates)
    for half in range(2):
        mine = slice(4 * half, 4 * half + 4)
        pick_rows(spot, half, blocks[mine], ROWS + EXPERTS * (1 - half), table, picked)
        slots[half][...] = picked[:, :ROWS]
        fill_pieces(slots[half], blocks[mine], pieces[mine])
        if half == 0:
            for p in range(RING):
                at = slice(p * 8, (p + 1) * 8)
                pieces[p][PIECE:, :] = jnp.concatenate([gates[at, :], picked[at, :]], axis=0).astype(BF16)


def combine_kernel(with_extra, slots_a, slots_b, *refs):
    everyone = range(RING)
    for half, slots in enumerate((slots_a, slots_b)):
        pieces, rows = refs[4 * half : 4 * half + 4], refs[8 + 4 * half : 12 + 4 * half]
        for d in everyone:
            filled = jnp.concatenate(
                [pieces[p][(e * 4 + d) * CAP : (e * 4 + d + 1) * CAP, :] for p in everyone for e in range(2)], axis=0
            )
            rows[d][0:ROWS, :] = dot_tn(line_matrix(slots, d), filled).astype(BF16)
        if half == 0 and with_extra:
            tables = [pieces[p][PIECE:, :].astype(F32) for p in everyone]
            for d in everyone:
                picked = [tables[p][e * 4 + d : e * 4 + d + 1, :] for p in everyone for e in range(2)]
                extra = jnp.concatenate(picked + [jnp.zeros((8, HALF), F32)], axis=0)
                rows[d][ROWS:, :] = extra.astype(BF16)


SLOT_COST = pl.CostEstimate(flops=1_000_000_000, bytes_accessed=5_000_000, transcendentals=0)
TABLE = pltpu.VMEM((EXPERTS, HALF), F32)


def shape_of(rows, dtype=BF16):
    return jax.ShapeDtypeStruct((rows, HALF), dtype)


def spread_rows(half_a, half_b):
    return [push(half_a, -d, 0, 0) for d in range(RING)] + [push(half_b, 0, -d, 0) for d in range(RING)]


def dispatch(spot, half_a, half_b):
    made = pl.pallas_call(
        dispatch_kernel,
        out_shape=[shape_of(PIECE + EXTRA)] * RING
        + [shape_of(PIECE)] * RING
        + [jax.ShapeDtypeStruct((EXPERTS, ROWS), F32)] * 2,
        in_specs=[SCALARS] + [WHOLE] * 8,
        out_specs=[WHOLE] * 10,
        scratch_shapes=[TABLE] * 3,
        compiler_params=params(),
        cost_estimate=SLOT_COST,
        name="dispatch",
    )(spot, *spread_rows(half_a, half_b))
    return exchange(made[:8]), made[8], made[9]


def exchange(pieces):
    got = exchange_near(pieces)
    got[2] = push(pieces[2], 0, 2, 0)
    (last,) = after((pieces[6],), got[5], got[7])
    got[6] = push(last, 2, 0, 0)
    return got


def exchange_near(pieces):
    got = [pieces[0], None, None, None, pieces[4], None, None, None]
    got[3], got[1] = push(pieces[1], 0, 1, 0), push(pieces[3], 0, 3, 0)
    got[7], got[5] = push(pieces[5], 1, 0, 0), push(pieces[7], 3, 0, 0)
    return got


def exchange_far(pieces, got, with_them, *others):
    held = after((pieces[2], pieces[6], *with_them), got[1], got[3], got[5], got[7], *others)
    got[2], got[6] = push(held[0], 0, 2, 0), push(held[1], 2, 0, 0)
    return held[2:]


def combine(slots_a, slots_b, pieces, with_extra, *others):
    rows_a = shape_of(ROWS + EXTRA) if with_extra else shape_of(ROWS)
    return pl.pallas_call(
        ignoring(lambda *refs: combine_kernel(with_extra, *refs), 10, len(others)),
        out_shape=[rows_a] * RING + [shape_of(ROWS)] * RING,
        in_specs=[WHOLE] * 10 + [ANYWHERE] * len(others),
        out_specs=[WHOLE] * 8,
        compiler_params=params(),
        cost_estimate=pl.CostEstimate(flops=60_000_000_000, bytes_accessed=0, transcendentals=0),
        name="combine",
    )(slots_a, slots_b, *pieces, *others)


def to_owners(partial):
    got = [None] * 8
    for d in range(RING):
        got[-d % RING] = push(partial[d], d, 0, 0)
        got[4 + -d % RING] = push(partial[4 + d], 0, d, 0)
    return got


CHIPS = RING * RING
PAIR = 2 * CAP


def chips_matrix(spot, table, step):
    rows = []
    for i in range(RING):
        for e in range(2):
            expert = (step * RING + i) * 2 + (spot[3] + e) % 2
            rows.append(slot_matrix(table[pl.ds(expert, 1), :]).astype(BF16))
    return jnp.concatenate(rows, axis=0)


def finish_kernel(spot, table, slots, middle, out, total):
    step = pl.program_id(0)
    term = dot_tn(chips_matrix(spot, table, step), slots[...])

    @pl.when(step == 0)
    def _():
        total[...] = term

    @pl.when(step > 0)
    def _():
        total[...] += term

    @pl.when(step == RING - 1)
    def _():
        out[...] = (middle[...] + RES_SCALE * total[...]).astype(BF16)


def finish(spot, table, slots, middle):
    return pl.pallas_call(
        finish_kernel,
        grid=(RING,),
        out_shape=jax.ShapeDtypeStruct((ROWS, WIDTH), BF16),
        in_specs=[SCALARS, WHOLE, pl.BlockSpec((RING * PAIR, WIDTH), lambda s: (s, 0)), WHOLE],
        out_specs=pl.BlockSpec((ROWS, WIDTH), lambda s: (0, 0)),
        scratch_shapes=[pltpu.VMEM((ROWS, WIDTH), F32)],
        compiler_params=params(),
        cost_estimate=SLOT_COST,
        name="finish",
    )(spot, table, slots, middle)


SAME_CORE = [list(range(core, EXPERTS, 2)) for core in range(2)]


STEPS = 8
STEP_ROWS = RING * CAP


def expert_kernel(spot, *refs):
    ra, rb, cot, weights = refs[:4], refs[4:8], refs[8], refs[9:11]
    qa, qb, moe, (disp_out, dgu_out, inner_out, dex_out) = refs[11:15], refs[15:19], refs[19], refs[20:24]
    wgu, wd, rows_in, cot_in, gates_in, back_out, moe_out, dgate_out, extra_out = refs[24:33]
    weight_sem, in_sem, out_sem, extra_sem = refs[33:]
    step = pl.program_id(0)

    def loads(e):
        up, down = weights[e].at[pl.ds(0, WIDTH)], weights[e].at[pl.ds(WIDTH, HALF)]
        return [
            pltpu.make_async_copy(up, wgu.at[e], weight_sem.at[e, 0]),
            pltpu.make_async_copy(down, wd.at[e], weight_sem.at[e, 1]),
        ]

    def places(j, half_a, half_b, far, whole, halves):
        slot, e, dx = j % 2, j // 4, j % 4
        ends = [(half_a[dx].at[pl.ds(e * STEP_ROWS, STEP_ROWS)], halves.at[slot, :, pl.ds(0, HALF)])]
        for dz in range(RING):
            at = pl.ds(dz * CAP, CAP)
            ends.append((half_b[dz].at[pl.ds((e * 4 + dx) * CAP, CAP)], halves.at[slot, at, pl.ds(HALF, HALF)]))
            chip = ((spot[1] + dz) % RING) * RING + (spot[2] + dx) % RING
            if far is cot:
                ends.append((far.at[chip], whole.at[slot, pl.ds(dz * ROWS, ROWS)]))
            else:
                ends.append((far.at[chip, pl.ds(e * CAP, CAP)], whole.at[slot, at]))
        return ends

    def fetches(j):
        slot = j % 2
        ends = places(j, ra, rb, cot, cot_in, rows_in)
        ends.append((ra[j % 4].at[pl.ds(PIECE, EXTRA)], gates_in.at[slot]))
        return [pltpu.make_async_copy(far, near, in_sem.at[slot, n]) for n, (far, near) in enumerate(ends)]

    def stores(j):
        ends = places(j, qa, qb, moe, moe_out, back_out)
        return [pltpu.make_async_copy(near, far, out_sem.at[j % 2, n]) for n, (far, near) in enumerate(ends)]

    for j in range(STEPS):

        @pl.when(step == j)
        def _():
            if j == 0:
                for copy in fetches(0) + loads(0) + loads(1):
                    copy.start()
            if j + 1 < STEPS:
                for copy in fetches(j + 1):
                    copy.start()
            for copy in fetches(j):
                copy.wait()
            if j % 4 == 0:
                for copy in loads(j // 4):
                    copy.wait()
            if j >= 2:
                for copy in stores(j - 2):
                    copy.wait()

    slot = step % 2
    e = step // 4
    extra = gates_in[slot].astype(F32)
    gates = extra[0:8, :ROWS] + extra[0:8, ROWS:]
    gates = jnp.where(e == 0, gates[0:4, :], gates[4:8, :])
    slots = jnp.where(e == 0, extra[8:12, :ROWS], extra[12:16, :ROWS])
    fills = [slot_matrix(slots[dz : dz + 1, :]) for dz in range(RING)]
    gate_slot = jnp.concatenate(
        [jnp.sum(fills[dz] * gates[dz : dz + 1, :], axis=1, keepdims=True) for dz in range(RING)], axis=0
    )
    rows = rows_in[slot]
    disp_out[...] = rows
    gate_up = dot(rows, wgu[e])
    gate, up = gate_up[:, :HALF], gate_up[:, HALF:]
    sigmoid = jax.nn.sigmoid(gate)
    silu = gate * sigmoid
    inner = (silu * up).astype(BF16)
    inner_out[...] = inner
    made = dot(inner, wd[e]).astype(BF16).astype(F32)
    dmoe = [
        dot(fills[dz].astype(BF16), cot_in[slot, dz * ROWS : (dz + 1) * ROWS, :]) for dz in range(RING)
    ]
    dmoe = RES_SCALE * jnp.concatenate(dmoe, axis=0)
    dgate_slot = jnp.sum(dmoe * made, axis=1, keepdims=True)
    dgates = [
        jnp.sum(fills[dz] * dgate_slot[dz * CAP : (dz + 1) * CAP, :], axis=0, keepdims=True) for dz in range(RING)
    ]
    at_row = pl.multiple_of((step % 4) * 8, 8)
    dgates = jnp.concatenate(dgates + dgates, axis=0)
    first = lax.broadcasted_iota(jnp.int32, (8, ROWS), 0) < 4
    dgate_out[pl.ds(at_row, 8), :] = jnp.where(first == (e == 0), dgates, dgate_out[pl.ds(at_row, 8), :])
    moe_out[slot] = (gate_slot * made).astype(BF16)
    dex = (gate_slot * dmoe).astype(BF16)
    dex_out[...] = dex
    dinner = dot_nt(dex, wd[e])
    dgate = dinner * up * sigmoid * (1.0 + gate * (1.0 - sigmoid))
    dgu = jnp.concatenate([dgate.astype(BF16), (dinner * silu).astype(BF16)], axis=1)
    dgu_out[...] = dgu
    back_out[slot] = dot_nt(dgu, wgu[e]).astype(BF16)

    for j in range(STEPS):

        @pl.when(step == j)
        def _():
            for copy in stores(j):
                copy.start()
            if j == STEPS - 1:
                last = []
                for dx in range(RING):
                    extra = high_low(dgate_out[dx * 8 : (dx + 1) * 8, :]).astype(F32)
                    extra_out[dx] = jnp.concatenate([extra, jnp.zeros_like(extra)], axis=0).astype(BF16)
                    last.append(
                        pltpu.make_async_copy(
                            extra_out.at[dx], qa[dx].at[pl.ds(PIECE, EXTRA)], extra_sem.at[dx]
                        )
                    )
                for copy in last:
                    copy.start()
                for copy in stores(j - 1) + stores(j) + last:
                    copy.wait()


def experts(spot, rows, cots, weights):
    total = STEPS * STEP_ROWS
    wide = pl.BlockSpec((STEP_ROWS, WIDTH), lambda s: (s, 0))
    narrow = pl.BlockSpec((STEP_ROWS, HALF), lambda s: (s, 0))
    buf = pltpu.VMEM((2, STEP_ROWS, WIDTH), BF16)
    made = pl.pallas_call(
        expert_kernel,
        grid=(STEPS,),
        out_shape=[shape_of(PIECE + EXTRA)] * RING
        + [shape_of(PIECE)] * RING
        + [
            jax.ShapeDtypeStruct((CHIPS, PAIR, WIDTH), BF16),
            jax.ShapeDtypeStruct((total, WIDTH), BF16),
            jax.ShapeDtypeStruct((total, WIDTH), BF16),
            jax.ShapeDtypeStruct((total, HALF), BF16),
            jax.ShapeDtypeStruct((total, WIDTH), BF16),
        ],
        in_specs=[SCALARS] + [ANYWHERE] * 11,
        out_specs=[ANYWHERE] * 9 + [wide, wide, narrow, wide],
        scratch_shapes=[
            pltpu.VMEM((2, WIDTH, WIDTH), BF16),
            pltpu.VMEM((2, HALF, WIDTH), BF16),
            buf, pltpu.VMEM((2, RING * ROWS, WIDTH), BF16), pltpu.VMEM((2, EXTRA, HALF), BF16), buf, buf,
            pltpu.VMEM((EXPERTS, ROWS), F32),
            pltpu.VMEM((RING, EXTRA, HALF), BF16),
            pltpu.SemaphoreType.DMA((2, 2)),
            pltpu.SemaphoreType.DMA((2, 10)),
            pltpu.SemaphoreType.DMA((2, 10)),
            pltpu.SemaphoreType.DMA((RING,)),
        ],
        compiler_params=params(),
        cost_estimate=pl.CostEstimate(flops=19_000_000_000, bytes_accessed=60_000_000, transcendentals=1_600_000),
        name="experts",
    )(spot, *rows, cots, *weights)
    return made[:8], made[8], made[9:]


def weight_grads_kernel(which, with_other, *refs):
    disp, dgu, inner, dex = refs[:4]
    other, out = refs[4] if with_other else None, refs[4 + with_other]
    disp_in, dgu_in, inner_in, dex_in, made, other_in, sems, out_sems = refs[5 + with_other :]
    rows = pl.ds(which * 4 * STEP_ROWS, 4 * STEP_ROWS)
    pairs = [(disp.at[rows], disp_in), (dgu.at[rows], dgu_in), (inner.at[rows], inner_in), (dex.at[rows], dex_in)]
    if with_other:
        pairs.append((other, other_in))
    fetches = [pltpu.make_async_copy(far, near, sems.at[i]) for i, (far, near) in enumerate(pairs)]
    stores = [
        pltpu.make_async_copy(made.at[pl.ds(i * HALF, HALF)], out.at[pl.ds(i * HALF, HALF)], out_sems.at[i])
        for i in range(3)
    ]
    for copy in fetches:
        copy.start()
    for i, left in enumerate((disp_in, disp_in, inner_in)):
        if i == 0:
            fetches[0].wait()
            fetches[1].wait()
        if i == 2:
            fetches[2].wait()
            fetches[3].wait()
        if with_other and i == 0:
            fetches[4].wait()
        cols = slice(i * HALF, (i + 1) * HALF) if i < 2 else slice(None)
        grad = dot_tn(left[:, cols], (dgu_in if i < 2 else dex_in)[...])
        if with_other:
            grad = grad.astype(BF16).astype(F32) + other_in[i * HALF : (i + 1) * HALF, :].astype(F32)
        made[i * HALF : (i + 1) * HALF, :] = grad.astype(BF16)
        stores[i].start()
    for copy in stores:
        copy.wait()


def weight_grads(which, saved, *other):
    wide, narrow = pltpu.VMEM((4 * STEP_ROWS, WIDTH), BF16), pltpu.VMEM((4 * STEP_ROWS, HALF), BF16)
    grads = pltpu.VMEM((WIDTH + HALF, WIDTH), BF16)
    return pl.pallas_call(
        lambda *refs: weight_grads_kernel(which, len(other), *refs),
        out_shape=jax.ShapeDtypeStruct((WIDTH + HALF, WIDTH), BF16),
        in_specs=[ANYWHERE] * (4 + len(other)),
        out_specs=ANYWHERE,
        scratch_shapes=[
            wide, wide, narrow, wide, grads, grads, pltpu.SemaphoreType.DMA((5,)), pltpu.SemaphoreType.DMA((3,)),
        ],
        compiler_params=params(),
        cost_estimate=NO_COST,
        name="weight_grads",
    )(*saved, *other)


def cast_grads_kernel(grads, up, down):
    for i in range(2):
        up[:, i, :] = grads[0:WIDTH, i * HALF : (i + 1) * HALF].astype(F32)
    down[...] = grads[WIDTH:, :].astype(F32)


def cast_grads(grads):
    return pl.pallas_call(
        cast_grads_kernel,
        out_shape=[
            jax.ShapeDtypeStruct((WIDTH, 2, HALF), F32),
            jax.ShapeDtypeStruct((HALF, WIDTH), F32),
        ],
        in_specs=[WHOLE],
        out_specs=[WHOLE] * 2,
        compiler_params=params(),
        cost_estimate=NO_COST,
        name="cast_grads",
    )(grads)


def unroute_kernel(spot, *refs):
    parts, (gates_t, middle, cot, gain, wr_t, dmiddle, dbranch, sums, gates, dlogits) = refs[:8], refs[8:]

    def four(pieces):
        a, b, c, d = (piece[0:ROWS, :].astype(F32) for piece in pieces)
        return (a + b) + (c + d)

    order = [
        (((spot[1] + dz) % RING) * RING + (spot[2] + dx) % RING) * 2 + (spot[3] + e) % 2
        for dz in range(RING)
        for dx in range(RING)
        for e in range(2)
    ]
    for i, at in enumerate(order):
        gates[i : i + 1, :] = gates_t[pl.ds(at, 1), :]
    tables = [part[ROWS:, :].astype(F32) for part in parts[:4]]
    dgates = jnp.concatenate([t[0:8, :ROWS] + t[0:8, ROWS:] for t in tables], axis=0)
    made = gates[...] * (dgates - jnp.sum(gates[...] * dgates, axis=0, keepdims=True))
    for i, at in enumerate(order):
        dlogits[pl.ds(at, 1), :] = made[i : i + 1, :]
    drouted = jnp.concatenate([four(parts[:4]), four(parts[4:])], axis=1)
    drouted = drouted + dot(dlogits[...].T, wr_t[...], HIGHEST)
    mid = middle[...]
    inverse = lax.rsqrt(jnp.mean(mid * mid, axis=-1, keepdims=True) + NORM_EPS)
    plain = mid * inverse
    routed = (plain * gain[...]).astype(BF16).astype(F32)
    sums[0:EXPERTS, :] = dot(dlogits[...], routed, HIGHEST)
    sums[EXPERTS : EXPERTS + 8, :] = jnp.broadcast_to(jnp.sum(drouted * plain, axis=0, keepdims=True), (8, WIDTH))
    scaled = drouted * gain[...]
    along = jnp.mean(scaled * plain, axis=-1, keepdims=True)
    total = cot[...].astype(F32) + inverse * (scaled - plain * along)
    dmiddle[...] = total
    dbranch[...] = (RES_SCALE * total).astype(BF16)


def unroute(spot, parts, gates_t, middle, cot, gain, wr_t, *others):
    return pl.pallas_call(
        ignoring(unroute_kernel, 14, len(others)),
        out_shape=[
            jax.ShapeDtypeStruct((ROWS, WIDTH), F32),
            jax.ShapeDtypeStruct((ROWS, WIDTH), BF16),
            jax.ShapeDtypeStruct((EXPERTS + 8, WIDTH), F32),
        ],
        in_specs=[SCALARS] + [WHOLE] * 13 + [ANYWHERE] * len(others),
        out_specs=[WHOLE] * 3,
        scratch_shapes=[pltpu.VMEM((EXPERTS, ROWS), F32), pltpu.VMEM((EXPERTS, ROWS), F32)],
        compiler_params=params(),
        cost_estimate=NO_COST,
        name="unroute",
    )(spot, *parts, gates_t, middle, cot, gain, wr_t, *others)


def unmix_kernel(rank, d0, d1, d2, d2_rest, d3, mixed, wo, dmixed, grad_out):
    me = rank[0]
    lane = lax.broadcasted_iota(jnp.int32, (ROWS, LANES), 1)
    for d, ref in enumerate((d0, d1, d2, d3)):
        at = block_at((me + d) % RING)
        grad = jnp.concatenate([d2[...], d2_rest[...]], axis=0) if d == 2 else ref[...]
        low = dot_nt(grad, wo[...])
        for pair in range(2):
            both = low[:, pair * LANES : (pair + 1) * LANES]
            other = pltpu.roll(both, HD, 1)
            keep = (lane < HD) if pair == 0 else (lane >= HD)
            first, second = (both, other) if pair == 0 else (other, both)
            at_head = 2 * pair * LANES
            dmixed[at, at_head : at_head + LANES] = jnp.where(keep, first, 0.0).astype(BF16)
            dmixed[at, at_head + LANES : at_head + 2 * LANES] = jnp.where(keep, second, 0.0).astype(BF16)
        term = dot_tn(mixed[at, :], grad)
        total = term if d == 0 else total + term
    grad_out[...] = total.astype(BF16)


def unmix(rank, pieces, mixed, wo, *others):
    length = RING * ROWS
    return pl.pallas_call(
        ignoring(unmix_kernel, 8, len(others)),
        out_shape=[
            jax.ShapeDtypeStruct((length, HEADS * LANES), BF16),
            jax.ShapeDtypeStruct((HEADS * HD, WIDTH), BF16),
        ],
        in_specs=[SCALARS] + [WHOLE] * 7 + [ANYWHERE] * len(others),
        out_specs=[WHOLE] * 2,
        compiler_params=params(),
        cost_estimate=pl.CostEstimate(flops=1_100_000_000, bytes_accessed=5_000_000, transcendentals=0),
        name="unmix",
    )(rank, pieces[0], pieces[1], *pieces[2], pieces[3], mixed, wo, *others)


def unattend_kernel(
    spot, q_in, k_in, v_in, lse, dmixed, normed, gain, wq, wk, wv, cos, sin, seg_col, seg_row,
    dqkv, dgain, dn0, dn1, dn2, dn3, kt, bias, dk, dv,
):
    me = spot[0]
    lane = lax.broadcasted_iota(jnp.int32, (ROWS, LANES), 1)
    kt[...] = k_in[...].astype(F32).T.astype(BF16)
    dk[...] = jnp.zeros_like(dk)
    dv[...] = jnp.zeros_like(dv)

    def unrope(v, rows):
        return v * cos[rows, :] - swap_halves(v) * sin[rows, :]

    for b in range(RING):
        lo, hi = key_range(b)
        rows = slice(b * ROWS, (b + 1) * ROWS)
        bias[0 : hi - lo, :] = mask_bias(b, seg_col, seg_row)
        dqs = []
        for h in range(HEADS):
            cols = slice(h * LANES, (h + 1) * LANES)
            q, do = q_in[rows, cols], dmixed[rows, cols]
            scores = dot_nt(k_in[lo:hi, :], q) + bias[0 : hi - lo, :]
            probs = jnp.exp(scores - lse[h : h + 1, rows])
            dprobs = dot_nt(v_in[lo:hi, :], do)
            delta = jnp.sum(probs * dprobs, axis=0, keepdims=True)
            dscores = (probs * (dprobs - delta)).astype(BF16)
            dv[lo:hi, :] += dot(probs.astype(BF16), do)
            dk[lo:hi, :] += dot(dscores, q)
            dqs.append(dot(kt[:, lo:hi], dscores).T * ATT_SCALE)
        first = jnp.where(lane < HD, dqs[0], pltpu.roll(dqs[1], HD, 1))
        second = jnp.where(lane < HD, pltpu.roll(dqs[2], HD, 1), dqs[3])
        dqkv[rows, 0:LANES] = unrope(first, rows).astype(BF16)
        dqkv[rows, LANES : 2 * LANES] = unrope(second, rows).astype(BF16)
    for b in range(RING):
        rows = slice(b * ROWS, (b + 1) * ROWS)
        dqkv[rows, 2 * LANES : 3 * LANES] = unrope(dk[rows, :], rows).astype(BF16)
        dqkv[rows, 3 * LANES :] = dv[rows, :].astype(BF16)
        dn = dot_nt(dqkv[rows, : 2 * LANES], wq[...])
        dn = dn + dot_nt(dqkv[rows, 2 * LANES : 3 * LANES], wk[...])
        dn = dn + dot_nt(dqkv[rows, 3 * LANES :], wv[...])
        term = jnp.sum(dn * normed[rows, :].astype(F32), axis=0, keepdims=True)
        gain_sum = term if b == 0 else gain_sum + term
        dn = dn.astype(BF16)
        relative = (b - me + RING) % RING
        for d, ref in enumerate((dn0, dn1, dn2, dn3)):

            @pl.when(relative == d)
            def _():
                ref[...] = dn

    dgain[...] = jnp.broadcast_to(gain_sum / gain[...], (8, WIDTH))


def unattend(spot, q, k, v, lse, dmixed, normed, gain, wq, wk, wv, cos, sin, seg_col, seg_row):
    length = RING * ROWS
    return pl.pallas_call(
        unattend_kernel,
        out_shape=[
            jax.ShapeDtypeStruct((length, HALF), BF16),
            jax.ShapeDtypeStruct((8, WIDTH), F32),
        ]
        + [jax.ShapeDtypeStruct((ROWS, WIDTH), BF16)] * RING,
        in_specs=[SCALARS] + [WHOLE] * 14,
        out_specs=[WHOLE] * 6,
        scratch_shapes=[
            pltpu.VMEM((LANES, length), BF16),
            pltpu.VMEM((3 * ROWS, ROWS), F32),
            pltpu.VMEM((length, LANES), F32),
            pltpu.VMEM((length, LANES), F32),
        ],
        compiler_params=params(),
        cost_estimate=NO_COST,
        name="unattend",
    )(spot, q, k, v, lse, dmixed, normed, gain, wq, wk, wv, cos, sin, seg_col, seg_row)


PAY = 832
QUARTER = PAY // RING
GAINS = 768 + EXPERTS


def pack_kernel(spot, normed, dqkv, grad_out, s0, s1, s2, s3, own, other):
    core = spot[3]
    sums = (s0[...] + s1[...]) + (s2[...] + s3[...])
    row = lax.broadcasted_iota(jnp.int32, (32, HALF), 0)
    for side, out in enumerate((own, other)):
        cols = pl.ds(pl.multiple_of(((core + side) % 2) * HALF, HALF), HALF)
        left = (core + side) % 2 == 0
        out[0:HALF, :] = dot_tn(normed[:, cols], dqkv[...]).astype(BF16)
        out[HALF:768, :] = grad_out[:, cols]
        here = jnp.where(left, sums[:, :HALF], sums[:, HALF:])
        out[768:GAINS, :] = here[0:EXPERTS, :].astype(BF16)
        out[GAINS:, :] = jnp.where(row == 0, here[EXPERTS : EXPERTS + 1, :], 0.0).astype(BF16)


def add_all(refs):
    total = refs[0][...].astype(F32)
    for ref in refs[1:]:
        total = total + ref[...].astype(F32)
    return total.astype(BF16)


def quarter_rows(index):
    return pl.ds(pl.multiple_of(index * QUARTER, 16), QUARTER)


def reduce_core_kernel(spot, own, got, g0, g1, g2, g3, p0, p1, p2, p3, total):
    total[...] = add_all((own, got))
    gain = (g0[...] + g1[...]) + (g2[...] + g3[...])
    mine = jnp.where(spot[3] == 0, gain[0:1, :HALF], gain[0:1, HALF:])
    row = lax.broadcasted_iota(jnp.int32, (32, HALF), 0)
    total[GAINS:, :] = jnp.where(row == 1, mine, total[GAINS:, :].astype(F32)).astype(BF16)
    for d, piece in enumerate((p0, p1, p2, p3)):
        piece[...] = total[quarter_rows((spot[2] + d) % RING), :]


def sum_kernel(spot, a, b, c, d, out):
    out[...] = add_all((a, b, c, d))


def gather_x_kernel(spot, a, b, c, d, out):
    for d, piece in enumerate((a, b, c, d)):
        out[quarter_rows((spot[2] + d) % RING), :] = piece[...]


def unpack_kernel(spot, own, got, query, key, value, grad_out, router, gains):
    for side, half in enumerate((own, got)):
        at = pl.ds(pl.multiple_of(((spot[3] + side) % 2) * HALF, HALF), HALF)
        query[at, :] = half[0:HALF, : 2 * LANES].astype(F32)
        key[at, :] = half[0:HALF, 2 * LANES : 3 * LANES].astype(F32)
        value[at, :] = half[0:HALF, 3 * LANES :].astype(F32)
        grad_out[:, at] = half[HALF:768, :].astype(F32)
        router[:, at] = half[768:GAINS, :].astype(F32)
        gains[:, at] = half[GAINS:, :].astype(F32)[0:8, :]


def small_call(kernel, spot, refs, shapes, scratch=None, flops=1_000_000, others=()):
    return pl.pallas_call(
        ignoring(kernel, 1 + len(refs), len(others)),
        out_shape=[jax.ShapeDtypeStruct(shape, dtype) for shape, dtype in shapes],
        in_specs=[SCALARS] + [WHOLE] * len(refs) + [ANYWHERE] * len(others),
        out_specs=[WHOLE] * len(shapes),
        scratch_shapes=[pltpu.VMEM(scratch, BF16)] if scratch else [],
        compiler_params=params(),
        cost_estimate=pl.CostEstimate(flops=flops, bytes_accessed=2_000_000, transcendentals=0),
    )(spot, *refs, *others)


def sum_over_ep(spot, normed, dqkv, grad_out, sums, gains, dn, finished, output):
    own, other = small_call(
        pack_kernel, spot, (normed, dqkv, grad_out, *sums), [((PAY, HALF), BF16)] * 2, flops=0
    )
    got = push(other, 0, 0, 1)
    pieces = small_call(
        reduce_core_kernel, spot, (own, got, *gains), [((QUARTER, HALF), BF16)] * 4, (PAY, HALF)
    )
    dn, halves = scatter_tp(after(dn, pieces[0]))
    pieces = [push(pieces[d], 0, d, 0) for d in range(RING)]
    quarter = [((QUARTER, HALF), BF16)]
    (line,) = small_call(sum_kernel, spot, pieces, quarter, others=(*halves, output))
    (line,) = small_call(sum_kernel, spot, [push(line, d, 0, 0) for d in range(RING)], quarter)
    pieces = [push(line, 0, -d, 0) for d in range(RING)]
    (half,) = small_call(gather_x_kernel, spot, pieces, [((PAY, HALF), BF16)], others=(*finished, *dn[1:]))
    made = small_call(
        unpack_kernel,
        spot,
        (half, push(half, 0, 0, 1)),
        [
            ((WIDTH, 2 * LANES), F32),
            ((WIDTH, LANES), F32),
            ((WIDTH, LANES), F32),
            ((ROWS, WIDTH), F32),
            ((EXPERTS, WIDTH), F32),
            ((8, WIDTH), F32),
        ],
    )
    return *made, dn


def hidden_kernel(a, b, c, hidden, gain, dmiddle, out):
    dn = a[...].astype(F32) + b[...].astype(F32) + c[...].astype(F32)
    x = hidden[...].astype(F32)
    inverse = lax.rsqrt(jnp.mean(x * x, axis=-1, keepdims=True) + NORM_EPS)
    plain = x * inverse
    scaled = dn * gain[...]
    along = jnp.mean(scaled * plain, axis=-1, keepdims=True)
    out[...] = dmiddle[...] + inverse * (scaled - plain * along)


def hidden_grad(dn, hidden, gain, dmiddle):
    return pl.pallas_call(
        hidden_kernel,
        out_shape=jax.ShapeDtypeStruct((ROWS, WIDTH), F32),
        in_specs=[WHOLE] * 6,
        out_specs=WHOLE,
        compiler_params=params(),
        cost_estimate=NO_COST,
        name="hidden_grad",
    )(*dn, hidden, gain, dmiddle)


def rope_tables(length):
    freqs = ROPE_BASE ** (-jnp.arange(HD // 2, dtype=F32) * 2.0 / HD)
    angles = jnp.arange(length, dtype=F32)[:, None] * freqs[None, :]
    cosine, sine = jnp.cos(angles), jnp.sin(angles)
    return jnp.concatenate([cosine] * 4, axis=1), jnp.concatenate([-sine, sine] * 2, axis=1)


def shards(
    hidden_in, segment_ids, expert_ids, slot_index, attn_gain, w_query, w_key, w_value, w_output,
    ffn_gain, w_router, w_gate_up, w_down, cotangent,
):
    length = RING * ROWS
    here, rank = lax.axis_index("ep"), lax.axis_index("tp")
    spot = jnp.stack([rank, here // 8, (here // 2) % 4, here % 2]).astype(jnp.int32)

    named = expert_ids[:, :, None] == jnp.arange(EXPERTS, dtype=jnp.int32)[None, None, :]
    slot_of = jnp.sum(jnp.where(named, slot_index[:, :, None] + 1, 0), axis=1) - 1
    chosen = (slot_of >= 0).astype(F32)
    table = slot_of.T.astype(F32)

    gain_one = attn_gain.astype(F32).reshape(1, WIDTH)
    gain_two = ffn_gain.astype(F32).reshape(1, WIDTH)
    cos, sin = rope_tables(length)
    seg_row = segment_ids
    seg_col = segment_ids.reshape(length, 1)

    group = [push_tp(hidden_in, -d) for d in range(RING)]
    cots = lax.all_gather(cotangent, "ep", axis=0, tiled=False, axis_index_groups=SAME_CORE)
    weights = jnp.concatenate([w_gate_up.reshape(WIDTH, 2 * HALF), w_down.reshape(HALF, WIDTH)], axis=0)
    made = attend(spot, group, gain_one, w_query, w_key, w_value, w_output, cos, sin, seg_col, seg_row)
    normed, q, k, v, mixed, lse = made[:6]
    branches = [push_tp(made[6 + d], d) for d in range(RING)]
    (weights,) = after((weights,), lse)
    weights = weights, push(weights, 0, 0, 1)
    middle, half_a, half_b, gates_t = route(hidden_in, branches, gain_two, w_router, chosen, table, weights[1])
    rows, slots_a, slots_b = dispatch(spot, half_a, half_b)
    back, moe_slots, saved = experts(spot, rows, cots, weights)
    got = exchange_near(back)
    (grads_other,) = exchange_far(back, got, (weight_grads(1, saved),))
    grads_e = weight_grads(0, saved, push(grads_other, 0, 0, 1))
    parts = to_owners(combine(slots_a, slots_b, got, True, grads_e))
    grads_e = lax.psum_scatter(grads_e, "tp", scatter_dimension=0, tiled=True)

    dmiddle, dbranch, sums = unroute(
        spot, parts, gates_t, middle, cotangent, gain_two, w_router.T.astype(F32)
    )
    group_grad = gather_tp(dbranch)
    sums = [push_tp(sums, d) for d in range(RING)]

    (moe_slots,) = after((moe_slots,), *parts)
    moe_slots = lax.all_to_all(
        moe_slots, "ep", split_axis=0, concat_axis=0, tiled=True, axis_index_groups=SAME_CORE
    )

    dmixed, grad_output = unmix(spot, group_grad, mixed, w_output, *sums[1:])
    (grads_e,) = after((grads_e,), dmixed)
    grad_up, grad_down = cast_grads(lax.all_gather(grads_e, "tp", axis=0, tiled=True))
    last = unattend(
        spot, q, k, v, lse, dmixed, normed, gain_one, w_query, w_key, w_value, cos, sin, seg_col, seg_row
    )
    gain = last[1] + push(last[1], 0, 0, 1)
    gains = [push_tp(gain, d) for d in range(RING)]
    output = finish(spot, table, moe_slots.reshape(CHIPS * PAIR, WIDTH), middle)
    grad_query, grad_key, grad_value, grad_output, grad_router, grad_gains, dn = sum_over_ep(
        spot, normed, last[0], grad_output, sums, gains, last[2:6], (grad_up, grad_down), output
    )
    grad_hidden = hidden_grad(dn, hidden_in, gain_one, dmiddle)
    return (
        output,
        grad_hidden,
        grad_gains[1],
        grad_query,
        grad_key,
        grad_value,
        grad_output,
        grad_gains[0],
        grad_router.T,
        grad_up.reshape(1, WIDTH, 2, HALF),
        grad_down.reshape(1, HALF, WIDTH),
    )


def solution(mesh):
    placed = (
        P(("ep", "tp"), None),
        P("ep", None),
        P(("ep", "tp"), None),
        P(("ep", "tp"), None),
        P(),
        P(None, "tp"),
        P(None, "tp"),
        P(None, "tp"),
        P("tp", None),
        P(),
        P(),
        P("ep", None, None, None),
        P("ep", None, None),
        P(("ep", "tp"), None),
    )
    return jax.shard_map(
        shards,
        mesh=mesh,
        in_specs=placed,
        out_specs=(
            P(("ep", "tp"), None),
            P(("ep", "tp"), None),
            P(),
            P(None, "tp"),
            P(None, "tp"),
            P(None, "tp"),
            P("tp", None),
            P(),
            P(),
            P("ep", None, None, None),
            P("ep", None, None),
        ),
        check_vma=False,
    )
```

```python
import jax
import jax.numpy as jnp
from jax import lax
from jax.experimental import pallas as pl
from jax.experimental.pallas import tpu as pltpu
from jax.sharding import PartitionSpec as P

HD = 64
ATT_SCALE = 0.015625
RES_SCALE = 0.22
NORM_EPS = 1e-06
ROPE_BASE = 10000.0
NEG_FILL = -1e30
HIGHEST = lax.Precision.HIGHEST
F32 = jnp.float32
BF16 = jnp.bfloat16

ROWS = 256
WIDTH = 1024
HALF = 512
CAP = 96
EXPERTS = 32
RING = 4
HEADS = 4
LANES = 128
VMEM_BYTES = 58 * 1024 * 1024
WHOLE = pl.BlockSpec(memory_space=pltpu.VMEM)
SCALARS = pl.BlockSpec(memory_space=pltpu.SMEM)
ANYWHERE = pl.BlockSpec(memory_space=pl.ANY)


def params():
    return pltpu.CompilerParams(vmem_limit_bytes=VMEM_BYTES)


NO_COST = pl.CostEstimate(flops=0, bytes_accessed=0, transcendentals=0)


def dot(a, b, precision=None):
    return jnp.dot(a, b, preferred_element_type=F32, precision=precision)


def dot_nt(a, b):
    return lax.dot_general(a, b, (((1,), (1,)), ((), ())), preferred_element_type=F32)


def dot_tn(a, b):
    return lax.dot_general(a, b, (((0,), (0,)), ((), ())), preferred_element_type=F32)


def place(z, x, core):
    return ((z % RING) * RING + (x % RING)) * 2 + core


def push(value, dz, dx, dc):
    if (dz % RING, dx % RING, dc) == (0, 0, 0):
        return value
    pairs = [
        (place(z, x, c), place(z + dz, x + dx, c ^ dc))
        for z in range(RING)
        for x in range(RING)
        for c in range(2)
    ]
    return lax.ppermute(value, "ep", pairs)


def push_tp(value, dy):
    if dy % RING == 0:
        return value
    return lax.ppermute(value, "tp", [(y, (y + dy) % RING) for y in range(RING)])


def after(values, *others):
    count = len(values)
    return pl.pallas_call(
        lambda *refs: None,
        out_shape=[jax.ShapeDtypeStruct(v.shape, v.dtype) for v in values],
        in_specs=[ANYWHERE] * (count + len(others)),
        out_specs=[ANYWHERE] * count,
        input_output_aliases={i: i for i in range(count)},
        cost_estimate=NO_COST,
        name="after",
    )(*values, *others)


def gather_tp(rows):
    after_me, before_me = push_tp(rows, -1), push_tp(rows, 1)
    half = rows.shape[0] // 2
    across = push_tp(after_me[:half], -1), push_tp(before_me[half:], 1)
    return rows, after_me, across, before_me


def add_halves_kernel(one, three, first, rest, ahead, behind):
    half = first.shape[0]
    ahead[0:half, :] = (one[0:half, :].astype(F32) + first[...].astype(F32)).astype(BF16)
    ahead[half:, :] = one[half:, :]
    behind[0:half, :] = three[0:half, :]
    behind[half:, :] = (three[half:, :].astype(F32) + rest[...].astype(F32)).astype(BF16)


def scatter_tp(own, one, two, two_rest, three):
    first, rest = push_tp(two, 1), push_tp(two_rest, -1)
    ahead, behind = pl.pallas_call(
        add_halves_kernel,
        out_shape=[jax.ShapeDtypeStruct(one.shape, BF16)] * 2,
        in_specs=[WHOLE] * 4,
        out_specs=[WHOLE] * 2,
        compiler_params=params(),
        cost_estimate=NO_COST,
        name="add_halves",
    )(one, three, first, rest)
    return (own, push_tp(ahead, 1), push_tp(behind, -1)), (first, rest)


def ignoring(kernel, first, count):
    return lambda *refs: kernel(*refs[:first], *refs[first + count :])


def swap_halves(v):
    lane = lax.broadcasted_iota(jnp.int32, v.shape, 1)
    return jnp.where(lane % HD < HD // 2, pltpu.roll(v, LANES - HD // 2, 1), pltpu.roll(v, HD // 2, 1))


def block_at(index):
    return pl.ds(pl.multiple_of(index * ROWS, ROWS), ROWS)


def key_range(block):
    return max(0, block - 2) * ROWS, (block + 1) * ROWS


def mask_bias(block, seg_col, seg_row):
    lo, hi = key_range(block)
    key_pos = lo + lax.broadcasted_iota(jnp.int32, (hi - lo, ROWS), 0)
    query_pos = block * ROWS + lax.broadcasted_iota(jnp.int32, (hi - lo, ROWS), 1)
    same = seg_col[lo:hi, :] == seg_row[:, block * ROWS : (block + 1) * ROWS]
    return jnp.where(same & (key_pos <= query_pos), 0.0, NEG_FILL)


def attend_kernel(
    rank, x0, x1, x2, x3, gain, wq, wk, wv, wo, cos, sin, seg_col, seg_row,
    normed, q_out, k_out, v_out, mixed, lse, br0, br1, br2, br3, vt, bias,
):
    me = rank[0]
    lane = lax.broadcasted_iota(jnp.int32, (ROWS, LANES), 1)
    for d, x_ref in enumerate((x0, x1, x2, x3)):
        at = block_at((me + d) % RING)
        x = x_ref[...].astype(F32)
        inverse = lax.rsqrt(jnp.mean(x * x, axis=-1, keepdims=True) + NORM_EPS)
        low = (x * inverse * gain[...]).astype(BF16)
        normed[at, :] = low
        cos_here, sin_here = cos[at, :], sin[at, :]

        def rope(v):
            return v * cos_here + swap_halves(v) * sin_here

        query = dot(low, wq[...])
        for pair in range(2):
            q = rope(query[:, pair * LANES : (pair + 1) * LANES]) * ATT_SCALE
            other = pltpu.roll(q, HD, 1)
            keep = (lane < HD) if pair == 0 else (lane >= HD)
            first, second = (q, other) if pair == 0 else (other, q)
            at_head = 2 * pair * LANES
            q_out[at, at_head : at_head + LANES] = jnp.where(keep, first, 0.0).astype(BF16)
            q_out[at, at_head + LANES : at_head + 2 * LANES] = jnp.where(keep, second, 0.0).astype(BF16)
        k_out[at, :] = rope(dot(low, wk[...])).astype(BF16)
        v_out[at, :] = dot(low, wv[...]).astype(BF16)
    vt[...] = v_out[...].astype(F32).T.astype(BF16)
    for b in range(RING):
        lo, hi = key_range(b)
        rows = slice(b * ROWS, (b + 1) * ROWS)
        bias[0 : hi - lo, :] = mask_bias(b, seg_col, seg_row)
        outs = []
        for h in range(HEADS):
            q = q_out[rows, h * LANES : (h + 1) * LANES]
            scores = dot_nt(k_out[lo:hi, :], q) + bias[0 : hi - lo, :]
            top = jnp.max(scores, axis=0, keepdims=True)
            weights = jnp.exp(scores - top)
            total = jnp.sum(weights, axis=0, keepdims=True)
            out = dot(vt[:, lo:hi], weights.astype(BF16)) * (1.0 / total)
            outs.append(out.T)
            lse[h : h + 1, rows] = top + jnp.log(total)
        mixed[rows, 0:LANES] = jnp.where(lane < HD, outs[0], pltpu.roll(outs[1], HD, 1)).astype(BF16)
        mixed[rows, LANES:] = jnp.where(lane < HD, pltpu.roll(outs[2], HD, 1), outs[3]).astype(BF16)
        branch = dot(mixed[rows, :], wo[...]).astype(BF16)
        relative = (b - me + RING) % RING
        for d, br in enumerate((br0, br1, br2, br3)):

            @pl.when(relative == d)
            def _():
                br[...] = branch


def attend(rank, pieces, gain, wq, wk, wv, wo, cos, sin, seg_col, seg_row, *others):
    length = RING * ROWS
    return pl.pallas_call(
        ignoring(attend_kernel, 14, len(others)),
        out_shape=[
            jax.ShapeDtypeStruct((length, WIDTH), BF16),
            jax.ShapeDtypeStruct((length, HEADS * LANES), BF16),
            jax.ShapeDtypeStruct((length, LANES), BF16),
            jax.ShapeDtypeStruct((length, LANES), BF16),
            jax.ShapeDtypeStruct((length, HEADS * HD), BF16),
            jax.ShapeDtypeStruct((8, length), F32),
        ]
        + [jax.ShapeDtypeStruct((ROWS, WIDTH), BF16)] * RING,
        in_specs=[SCALARS] + [WHOLE] * 13 + [ANYWHERE] * len(others),
        out_specs=[WHOLE] * 10,
        scratch_shapes=[pltpu.VMEM((LANES, length), BF16), pltpu.VMEM((3 * ROWS, ROWS), F32)],
        compiler_params=params(),
        cost_estimate=NO_COST,
        name="attend",
    )(rank, *pieces, gain, wq, wk, wv, wo, cos, sin, seg_col, seg_row, *others)


def high_low(v):
    high = v.astype(BF16)
    return jnp.concatenate([high, (v - high.astype(F32)).astype(BF16)], axis=1)


def route_kernel(x, b0, b1, b2, b3, gain, wr, chosen, table, middle, half_a, half_b, gates_t):
    branch = b0[...].astype(F32) + b1[...].astype(F32) + b2[...].astype(F32) + b3[...].astype(F32)
    mid = x[...].astype(F32) + RES_SCALE * branch
    middle[...] = mid
    inverse = lax.rsqrt(jnp.mean(mid * mid, axis=-1, keepdims=True) + NORM_EPS)
    routed = (mid * inverse * gain[...]).astype(BF16)
    half_b[0:ROWS, :] = routed[:, HALF:]
    logits = jnp.where(chosen[...] > 0.0, dot(routed, wr[...]), NEG_FILL)
    weights = jnp.exp(logits - jnp.max(logits, axis=-1, keepdims=True))
    gates = (weights / jnp.sum(weights, axis=-1, keepdims=True)).T
    gates_t[...] = gates
    half_a[0:ROWS, :] = routed[:, :HALF]
    half_a[ROWS : ROWS + EXPERTS, :] = high_low(gates)
    slots = jnp.concatenate([table[...], jnp.zeros_like(gates)], axis=1).astype(BF16)
    half_a[ROWS + EXPERTS :, :] = slots
    half_b[ROWS:, :] = slots


def route(x, branches, gain, wr, chosen, table, *others):
    return pl.pallas_call(
        ignoring(route_kernel, 9, len(others)),
        out_shape=[
            jax.ShapeDtypeStruct((ROWS, WIDTH), F32),
            jax.ShapeDtypeStruct((ROWS + 2 * EXPERTS, HALF), BF16),
            jax.ShapeDtypeStruct((ROWS + EXPERTS, HALF), BF16),
            jax.ShapeDtypeStruct((EXPERTS, ROWS), F32),
        ],
        in_specs=[WHOLE] * 9 + [ANYWHERE] * len(others),
        out_specs=[WHOLE] * 4,
        compiler_params=params(),
        cost_estimate=pl.CostEstimate(flops=20_000_000, bytes_accessed=5_000_000, transcendentals=8192),
        name="route",
    )(x, *branches, gain, wr, chosen, table, *others)


PIECE = RING * CAP
EXTRA = 16


def line_row(d, p, e):
    return p * 8 + e * 4 + d


def slot_matrix(row):
    slot = lax.broadcasted_iota(jnp.int32, (CAP, ROWS), 0).astype(F32)
    return jnp.where(slot == row, 1.0, 0.0)


def line_matrix(slots, d):
    rows = [line_row(d, p, e) for p in range(RING) for e in range(2)]
    return jnp.concatenate([slot_matrix(slots[r : r + 1, :]).astype(BF16) for r in rows], axis=0)


def expert_row(spot, half, d, p, e):
    z, x, core = spot[1], spot[2], spot[3]
    if half == 0:
        x = (x + p) % RING
    else:
        z = (z + p) % RING
    return (z * RING + x) * 2 + (core + e) % 2


def fill_pieces(slots, rows, pieces):
    for d in range(RING):
        filled = dot(line_matrix(slots, d), rows[d][0:ROWS, :]).astype(BF16)
        for p in range(RING):
            for e in range(2):
                pieces[e * 4 + p][d * CAP : (d + 1) * CAP, :] = filled[(p * 2 + e) * CAP : (p * 2 + e + 1) * CAP, :]


def pick_rows(spot, half, blocks, first, table, picked):
    for d in range(RING):
        table[...] = blocks[d][first : first + EXPERTS, :].astype(F32)
        for p in range(RING):
            for e in range(2):
                r = line_row(d, p, e)
                picked[r : r + 1, :] = table[pl.ds(expert_row(spot, half, d, p, e), 1), :]


def dispatch_kernel(spot, *refs):
    blocks, pieces, slots, (table, gates, picked) = refs[:8], (refs[8:16], refs[16:24]), refs[24:26], refs[26:]
    pick_rows(spot, 0, blocks[:4], ROWS, table, gates)
    for half in range(2):
        mine = blocks[4 * half : 4 * half + 4]
        pick_rows(spot, half, mine, ROWS + EXPERTS * (1 - half), table, picked)
        slots[half][...] = picked[:, :ROWS]
        fill_pieces(slots[half], mine, pieces[half])
        if half == 0:
            for p in range(RING):
                for e in range(2):
                    at = slice(p * 8 + e * 4, p * 8 + e * 4 + 4)
                    extra = jnp.concatenate([gates[at, :], picked[at, :], jnp.zeros((8, HALF), F32)], axis=0)
                    pieces[0][e * 4 + p][PIECE:, :] = extra.astype(BF16)


def combine_kernel(slots_a, slots_b, *refs):
    everyone = range(RING)
    for half, slots in enumerate((slots_a, slots_b)):
        pieces, rows = refs[8 * half : 8 * half + 8], refs[16 + 4 * half : 20 + 4 * half]
        for d in everyone:
            filled = [pieces[e * 4 + p][d * CAP : (d + 1) * CAP, :] for p in everyone for e in range(2)]
            filled = jnp.concatenate(filled, axis=0)
            rows[d][0:ROWS, :] = dot_tn(line_matrix(slots, d), filled).astype(BF16)
        if half == 0:
            tables = [pieces[i][PIECE:, :].astype(F32) for i in range(8)]
            for d in everyone:
                picked = [tables[e * 4 + p][d : d + 1, :] for p in everyone for e in range(2)]
                extra = jnp.concatenate(picked + [jnp.zeros((8, HALF), F32)], axis=0)
                rows[d][ROWS:, :] = extra.astype(BF16)


SLOT_COST = pl.CostEstimate(flops=1_000_000_000, bytes_accessed=5_000_000, transcendentals=0)
TABLE = pltpu.VMEM((EXPERTS, HALF), F32)


def shape_of(rows, dtype=BF16):
    return jax.ShapeDtypeStruct((rows, HALF), dtype)


def spread_rows(half_a, half_b):
    return [push(half_a, -d, 0, 0) for d in range(RING)] + [push(half_b, 0, -d, 0) for d in range(RING)]


def dispatch(spot, half_a, half_b):
    made = pl.pallas_call(
        dispatch_kernel,
        out_shape=[shape_of(PIECE + EXTRA)] * 8
        + [shape_of(PIECE)] * 8
        + [jax.ShapeDtypeStruct((EXPERTS, ROWS), F32)] * 2,
        in_specs=[SCALARS] + [WHOLE] * 8,
        out_specs=[WHOLE] * 18,
        scratch_shapes=[TABLE] * 3,
        compiler_params=params(),
        cost_estimate=SLOT_COST,
        name="dispatch",
    )(spot, *spread_rows(half_a, half_b))
    return (made[:8], made[8:16]), made[16], made[17]


class Pieces:
    def __init__(self, half_a, half_b):
        self.made = list(half_a), list(half_b)
        self.got = [half_a[0], None, None, None], [half_b[0], None, None, None]

    def send(self, half, p, held=None):
        piece = self.made[half][p] if held is None else held
        self.got[half][-p % RING] = push(piece, 0, p, 0) if half == 0 else push(piece, p, 0, 0)
        return self.got[half][-p % RING]

    def send_near(self, held=(None,) * 4):
        places = (0, 1), (0, 3), (1, 1), (1, 3)
        return [self.send(half, p, piece) for (half, p), piece in zip(places, held)]

    def near(self):
        return self.made[0][1], self.made[0][3], self.made[1][1], self.made[1][3]


def combine(slots_a, slots_b, first, second, *others):
    pieces = [*first.got[0], *second.got[0], *first.got[1], *second.got[1]]
    return pl.pallas_call(
        ignoring(combine_kernel, 18, len(others)),
        out_shape=[shape_of(ROWS + EXTRA)] * RING + [shape_of(ROWS)] * RING,
        in_specs=[WHOLE] * 18 + [ANYWHERE] * len(others),
        out_specs=[WHOLE] * 8,
        compiler_params=params(),
        cost_estimate=pl.CostEstimate(flops=60_000_000_000, bytes_accessed=0, transcendentals=0),
        name="combine",
    )(slots_a, slots_b, *pieces, *others)


def to_owners(partial):
    got = [None] * 8
    for d in range(RING):
        got[-d % RING] = push(partial[d], d, 0, 0)
        got[4 + -d % RING] = push(partial[4 + d], 0, d, 0)
    return got


CHIPS = RING * RING
PAIR = 2 * CAP


def chips_matrix(spot, table, step):
    rows = []
    for i in range(RING):
        for e in range(2):
            expert = (step * RING + i) * 2 + (spot[3] + e) % 2
            rows.append(slot_matrix(table[pl.ds(expert, 1), :]).astype(BF16))
    return jnp.concatenate(rows, axis=0)


def finish_kernel(spot, table, slots, middle, out, total):
    step = pl.program_id(0)
    term = dot_tn(chips_matrix(spot, table, step), slots[...])

    @pl.when(step == 0)
    def _():
        total[...] = term

    @pl.when(step > 0)
    def _():
        total[...] += term

    @pl.when(step == RING - 1)
    def _():
        out[...] = (middle[...] + RES_SCALE * total[...]).astype(BF16)


def finish(spot, table, slots, middle):
    return pl.pallas_call(
        finish_kernel,
        grid=(RING,),
        out_shape=jax.ShapeDtypeStruct((ROWS, WIDTH), BF16),
        in_specs=[SCALARS, WHOLE, pl.BlockSpec((RING * PAIR, WIDTH), lambda s: (s, 0)), WHOLE],
        out_specs=pl.BlockSpec((ROWS, WIDTH), lambda s: (0, 0)),
        scratch_shapes=[pltpu.VMEM((ROWS, WIDTH), F32)],
        compiler_params=params(),
        cost_estimate=SLOT_COST,
        name="finish",
    )(spot, table, slots, middle)


SAME_CORE = [list(range(core, EXPERTS, 2)) for core in range(2)]


STEPS = RING
STEP_ROWS = RING * CAP


def expert_kernel(e, spot, *refs):
    ra, rb, cot, weights = refs[:4], refs[4:8], refs[8], refs[9]
    refs = refs[10 + e :]
    qa, qb, moe, (disp_out, dgu_out, inner_out, dex_out) = refs[:4], refs[4:8], refs[8], refs[9:13]
    wgu, wd, rows_in, cot_in, extra_in, back_out, moe_out, extra_out, weight_sem, in_sem, out_sem = refs[13:]
    step = pl.program_id(0)
    loads = [
        pltpu.make_async_copy(weights.at[pl.ds(0, WIDTH)], wgu, weight_sem.at[0]),
        pltpu.make_async_copy(weights.at[pl.ds(WIDTH, HALF)], wd, weight_sem.at[1]),
    ]

    def places(dx, half_a, half_b, halves, extra):
        slot = dx % 2
        ends = [
            (half_a[dx].at[pl.ds(0, PIECE)], halves.at[slot, :, pl.ds(0, HALF)]),
            (half_a[dx].at[pl.ds(PIECE, EXTRA)], extra.at[slot]),
        ]
        for dz in range(RING):
            ends.append((half_b[dz].at[pl.ds(dx * CAP, CAP)], halves.at[slot, pl.ds(dz * CAP, CAP), pl.ds(HALF, HALF)]))
        return ends

    def chip(dz, dx):
        return ((spot[1] + dz) % RING) * RING + (spot[2] + dx) % RING

    def fetches(dx):
        ends = places(dx, ra, rb, rows_in, extra_in)
        for dz in range(RING):
            ends.append((cot.at[chip(dz, dx)], cot_in.at[dx % 2, pl.ds(dz * ROWS, ROWS)]))
        return [pltpu.make_async_copy(far, near, in_sem.at[dx % 2, n]) for n, (far, near) in enumerate(ends)]

    def stores(dx):
        ends = places(dx, qa, qb, back_out, extra_out)
        for dz in range(RING):
            ends.append((moe.at[chip(dz, dx), pl.ds(e * CAP, CAP)], moe_out.at[dx % 2, pl.ds(dz * CAP, CAP)]))
        return [pltpu.make_async_copy(near, far, out_sem.at[dx % 2, n]) for n, (far, near) in enumerate(ends)]

    for j in range(STEPS):

        @pl.when(step == j)
        def _():
            if j == 0:
                for copy in fetches(0) + loads:
                    copy.start()
            if j + 1 < STEPS:
                for copy in fetches(j + 1):
                    copy.start()
            for copy in fetches(j):
                copy.wait()
            if j == 0:
                for copy in loads:
                    copy.wait()
            if j >= 2:
                for copy in stores(j - 2):
                    copy.wait()

    slot = step % 2
    extra = extra_in[slot].astype(F32)
    gates = extra[0:4, :ROWS] + extra[0:4, ROWS:]
    fills = [slot_matrix(extra[4 + dz : 5 + dz, :ROWS]) for dz in range(RING)]
    gate_slot = jnp.concatenate(
        [jnp.sum(fills[dz] * gates[dz : dz + 1, :], axis=1, keepdims=True) for dz in range(RING)], axis=0
    )
    rows = rows_in[slot]
    disp_out[...] = rows
    gate_up = dot(rows, wgu[...])
    gate, up = gate_up[:, :HALF], gate_up[:, HALF:]
    sigmoid = jax.nn.sigmoid(gate)
    silu = gate * sigmoid
    inner = (silu * up).astype(BF16)
    inner_out[...] = inner
    made = dot(inner, wd[...]).astype(BF16).astype(F32)
    dmoe = [
        dot(fills[dz].astype(BF16), cot_in[slot, dz * ROWS : (dz + 1) * ROWS, :]) for dz in range(RING)
    ]
    dmoe = RES_SCALE * jnp.concatenate(dmoe, axis=0)
    dgate_slot = jnp.sum(dmoe * made, axis=1, keepdims=True)
    dgates = [
        jnp.sum(fills[dz] * dgate_slot[dz * CAP : (dz + 1) * CAP, :], axis=0, keepdims=True) for dz in range(RING)
    ]
    dgates = jnp.concatenate(dgates + [jnp.zeros((EXTRA - RING, ROWS), F32)], axis=0)
    extra_out[slot] = high_low(dgates)
    moe_out[slot] = (gate_slot * made).astype(BF16)
    dex = (gate_slot * dmoe).astype(BF16)
    dex_out[...] = dex
    dinner = dot_nt(dex, wd[...])
    dgate = dinner * up * sigmoid * (1.0 + gate * (1.0 - sigmoid))
    dgu = jnp.concatenate([dgate.astype(BF16), (dinner * silu).astype(BF16)], axis=1)
    dgu_out[...] = dgu
    back_out[slot] = dot_nt(dgu, wgu[...]).astype(BF16)

    for j in range(STEPS):

        @pl.when(step == j)
        def _():
            for copy in stores(j):
                copy.start()
            if j == STEPS - 1:
                for copy in stores(j - 1) + stores(j):
                    copy.wait()


def expert(spot, e, pieces, cots, weights, *moe):
    total = STEPS * STEP_ROWS
    wide = pl.BlockSpec((STEP_ROWS, WIDTH), lambda s: (s, 0))
    narrow = pl.BlockSpec((STEP_ROWS, HALF), lambda s: (s, 0))
    buf, small = pltpu.VMEM((2, STEP_ROWS, WIDTH), BF16), pltpu.VMEM((2, EXTRA, HALF), BF16)
    made = pl.pallas_call(
        lambda *refs: expert_kernel(e, *refs),
        grid=(STEPS,),
        out_shape=[shape_of(PIECE + EXTRA)] * RING
        + [shape_of(PIECE)] * RING
        + [
            jax.ShapeDtypeStruct((CHIPS, PAIR, WIDTH), BF16),
            jax.ShapeDtypeStruct((total, WIDTH), BF16),
            jax.ShapeDtypeStruct((total, WIDTH), BF16),
            jax.ShapeDtypeStruct((total, HALF), BF16),
            jax.ShapeDtypeStruct((total, WIDTH), BF16),
        ],
        in_specs=[SCALARS] + [ANYWHERE] * (10 + e),
        out_specs=[ANYWHERE] * 9 + [wide, wide, narrow, wide],
        scratch_shapes=[
            pltpu.VMEM((WIDTH, WIDTH), BF16),
            pltpu.VMEM((HALF, WIDTH), BF16),
            buf, pltpu.VMEM((2, RING * ROWS, WIDTH), BF16), small, buf, buf, small,
            pltpu.SemaphoreType.DMA((2,)),
            pltpu.SemaphoreType.DMA((2, 10)),
            pltpu.SemaphoreType.DMA((2, 10)),
        ],
        input_output_aliases={11: 8} if e else {},
        compiler_params=params(),
        cost_estimate=NO_COST,
        name="expert",
    )(spot, *pieces.got[0], *pieces.got[1], cots, weights, *moe)
    return Pieces(made[:4], made[4:8]), made[8], made[9:]


def weight_grads_kernel(with_other, *refs):
    disp, dgu, inner, dex = refs[:4]
    other, out = refs[4] if with_other else None, refs[4 + with_other]
    disp_in, dgu_in, inner_in, dex_in, made, other_in, sems, out_sems = refs[5 + with_other :]
    pairs = [(disp, disp_in), (dgu, dgu_in), (inner, inner_in), (dex, dex_in)]
    if with_other:
        pairs.append((other, other_in))
    fetches = [pltpu.make_async_copy(far, near, sems.at[i]) for i, (far, near) in enumerate(pairs)]
    stores = [
        pltpu.make_async_copy(made.at[pl.ds(i * HALF, HALF)], out.at[pl.ds(i * HALF, HALF)], out_sems.at[i])
        for i in range(3)
    ]
    for copy in fetches:
        copy.start()
    for i, left in enumerate((disp_in, disp_in, inner_in)):
        if i == 0:
            fetches[0].wait()
            fetches[1].wait()
        if i == 2:
            fetches[2].wait()
            fetches[3].wait()
        if with_other and i == 0:
            fetches[4].wait()
        cols = slice(i * HALF, (i + 1) * HALF) if i < 2 else slice(None)
        grad = dot_tn(left[:, cols], (dgu_in if i < 2 else dex_in)[...])
        if with_other:
            grad = grad.astype(BF16).astype(F32) + other_in[i * HALF : (i + 1) * HALF, :].astype(F32)
        made[i * HALF : (i + 1) * HALF, :] = grad.astype(BF16)
        stores[i].start()
    for copy in stores:
        copy.wait()


def weight_grads(saved, *other):
    wide, narrow = pltpu.VMEM((4 * STEP_ROWS, WIDTH), BF16), pltpu.VMEM((4 * STEP_ROWS, HALF), BF16)
    grads = pltpu.VMEM((WIDTH + HALF, WIDTH), BF16)
    return pl.pallas_call(
        lambda *refs: weight_grads_kernel(len(other), *refs),
        out_shape=jax.ShapeDtypeStruct((WIDTH + HALF, WIDTH), BF16),
        in_specs=[ANYWHERE] * (4 + len(other)),
        out_specs=ANYWHERE,
        scratch_shapes=[
            wide, wide, narrow, wide, grads, grads, pltpu.SemaphoreType.DMA((5,)), pltpu.SemaphoreType.DMA((3,)),
        ],
        compiler_params=params(),
        cost_estimate=NO_COST,
        name="weight_grads",
    )(*saved, *other)


def cast_grads_kernel(grads, up, down):
    for i in range(2):
        up[:, i, :] = grads[0:WIDTH, i * HALF : (i + 1) * HALF].astype(F32)
    down[...] = grads[WIDTH:, :].astype(F32)


def cast_grads(grads, *others):
    return pl.pallas_call(
        ignoring(cast_grads_kernel, 1, len(others)),
        out_shape=[
            jax.ShapeDtypeStruct((WIDTH, 2, HALF), F32),
            jax.ShapeDtypeStruct((HALF, WIDTH), F32),
        ],
        in_specs=[WHOLE] + [ANYWHERE] * len(others),
        out_specs=[WHOLE] * 2,
        compiler_params=params(),
        cost_estimate=NO_COST,
        name="cast_grads",
    )(grads, *others)


def unroute_kernel(spot, *refs):
    parts, (gates_t, middle, cot, gain, wr_t, dmiddle, dbranch, sums, gates, dlogits) = refs[:8], refs[8:]

    def four(pieces):
        a, b, c, d = (piece[0:ROWS, :].astype(F32) for piece in pieces)
        return (a + b) + (c + d)

    order = [
        (((spot[1] + dz) % RING) * RING + (spot[2] + dx) % RING) * 2 + (spot[3] + e) % 2
        for dz in range(RING)
        for dx in range(RING)
        for e in range(2)
    ]
    for i, at in enumerate(order):
        gates[i : i + 1, :] = gates_t[pl.ds(at, 1), :]
    tables = [part[ROWS:, :].astype(F32) for part in parts[:4]]
    dgates = jnp.concatenate([t[0:8, :ROWS] + t[0:8, ROWS:] for t in tables], axis=0)
    made = gates[...] * (dgates - jnp.sum(gates[...] * dgates, axis=0, keepdims=True))
    for i, at in enumerate(order):
        dlogits[pl.ds(at, 1), :] = made[i : i + 1, :]
    drouted = jnp.concatenate([four(parts[:4]), four(parts[4:])], axis=1)
    drouted = drouted + dot(dlogits[...].T, wr_t[...], HIGHEST)
    mid = middle[...]
    inverse = lax.rsqrt(jnp.mean(mid * mid, axis=-1, keepdims=True) + NORM_EPS)
    plain = mid * inverse
    routed = (plain * gain[...]).astype(BF16).astype(F32)
    sums[0:EXPERTS, :] = dot(dlogits[...], routed, HIGHEST)
    sums[EXPERTS : EXPERTS + 8, :] = jnp.broadcast_to(jnp.sum(drouted * plain, axis=0, keepdims=True), (8, WIDTH))
    scaled = drouted * gain[...]
    along = jnp.mean(scaled * plain, axis=-1, keepdims=True)
    total = cot[...].astype(F32) + inverse * (scaled - plain * along)
    dmiddle[...] = total
    dbranch[...] = (RES_SCALE * total).astype(BF16)


def unroute(spot, parts, gates_t, middle, cot, gain, wr_t, *others):
    return pl.pallas_call(
        ignoring(unroute_kernel, 14, len(others)),
        out_shape=[
            jax.ShapeDtypeStruct((ROWS, WIDTH), F32),
            jax.ShapeDtypeStruct((ROWS, WIDTH), BF16),
            jax.ShapeDtypeStruct((EXPERTS + 8, WIDTH), F32),
        ],
        in_specs=[SCALARS] + [WHOLE] * 13 + [ANYWHERE] * len(others),
        out_specs=[WHOLE] * 3,
        scratch_shapes=[pltpu.VMEM((EXPERTS, ROWS), F32), pltpu.VMEM((EXPERTS, ROWS), F32)],
        compiler_params=params(),
        cost_estimate=NO_COST,
        name="unroute",
    )(spot, *parts, gates_t, middle, cot, gain, wr_t, *others)


def unmix_kernel(rank, d0, d1, d2, d2_rest, d3, mixed, wo, dmixed, grad_out):
    me = rank[0]
    lane = lax.broadcasted_iota(jnp.int32, (ROWS, LANES), 1)
    for d, ref in enumerate((d0, d1, d2, d3)):
        at = block_at((me + d) % RING)
        grad = jnp.concatenate([d2[...], d2_rest[...]], axis=0) if d == 2 else ref[...]
        low = dot_nt(grad, wo[...])
        for pair in range(2):
            both = low[:, pair * LANES : (pair + 1) * LANES]
            other = pltpu.roll(both, HD, 1)
            keep = (lane < HD) if pair == 0 else (lane >= HD)
            first, second = (both, other) if pair == 0 else (other, both)
            at_head = 2 * pair * LANES
            dmixed[at, at_head : at_head + LANES] = jnp.where(keep, first, 0.0).astype(BF16)
            dmixed[at, at_head + LANES : at_head + 2 * LANES] = jnp.where(keep, second, 0.0).astype(BF16)
        term = dot_tn(mixed[at, :], grad)
        total = term if d == 0 else total + term
    grad_out[...] = total.astype(BF16)


def unmix(rank, pieces, mixed, wo, *others):
    length = RING * ROWS
    return pl.pallas_call(
        ignoring(unmix_kernel, 8, len(others)),
        out_shape=[
            jax.ShapeDtypeStruct((length, HEADS * LANES), BF16),
            jax.ShapeDtypeStruct((HEADS * HD, WIDTH), BF16),
        ],
        in_specs=[SCALARS] + [WHOLE] * 7 + [ANYWHERE] * len(others),
        out_specs=[WHOLE] * 2,
        compiler_params=params(),
        cost_estimate=pl.CostEstimate(flops=1_100_000_000, bytes_accessed=5_000_000, transcendentals=0),
        name="unmix",
    )(rank, pieces[0], pieces[1], *pieces[2], pieces[3], mixed, wo, *others)


def unattend_kernel(
    spot, q_in, k_in, v_in, lse, dmixed, normed, gain, wq, wk, wv, cos, sin, seg_col, seg_row,
    dqkv, dgain, dn0, dn1, dn2, dn2_rest, dn3, kt, bias, dk, dv,
):
    me = spot[0]
    lane = lax.broadcasted_iota(jnp.int32, (ROWS, LANES), 1)
    kt[...] = k_in[...].astype(F32).T.astype(BF16)
    dk[...] = jnp.zeros_like(dk)
    dv[...] = jnp.zeros_like(dv)

    def unrope(v, rows):
        return v * cos[rows, :] - swap_halves(v) * sin[rows, :]

    for b in range(RING):
        lo, hi = key_range(b)
        rows = slice(b * ROWS, (b + 1) * ROWS)
        bias[0 : hi - lo, :] = mask_bias(b, seg_col, seg_row)
        dqs = []
        for h in range(HEADS):
            cols = slice(h * LANES, (h + 1) * LANES)
            q, do = q_in[rows, cols], dmixed[rows, cols]
            scores = dot_nt(k_in[lo:hi, :], q) + bias[0 : hi - lo, :]
            probs = jnp.exp(scores - lse[h : h + 1, rows])
            dprobs = dot_nt(v_in[lo:hi, :], do)
            delta = jnp.sum(probs * dprobs, axis=0, keepdims=True)
            dscores = (probs * (dprobs - delta)).astype(BF16)
            dv[lo:hi, :] += dot(probs.astype(BF16), do)
            dk[lo:hi, :] += dot(dscores, q)
            dqs.append(dot(kt[:, lo:hi], dscores).T * ATT_SCALE)
        first = jnp.where(lane < HD, dqs[0], pltpu.roll(dqs[1], HD, 1))
        second = jnp.where(lane < HD, pltpu.roll(dqs[2], HD, 1), dqs[3])
        dqkv[rows, 0:LANES] = unrope(first, rows).astype(BF16)
        dqkv[rows, LANES : 2 * LANES] = unrope(second, rows).astype(BF16)
    for b in range(RING):
        rows = slice(b * ROWS, (b + 1) * ROWS)
        dqkv[rows, 2 * LANES : 3 * LANES] = unrope(dk[rows, :], rows).astype(BF16)
        dqkv[rows, 3 * LANES :] = dv[rows, :].astype(BF16)
        dn = dot_nt(dqkv[rows, : 2 * LANES], wq[...])
        dn = dn + dot_nt(dqkv[rows, 2 * LANES : 3 * LANES], wk[...])
        dn = dn + dot_nt(dqkv[rows, 3 * LANES :], wv[...])
        term = jnp.sum(dn * normed[rows, :].astype(F32), axis=0, keepdims=True)
        gain_sum = term if b == 0 else gain_sum + term
        dn = dn.astype(BF16)
        relative = (b - me + RING) % RING
        for d, ref in ((0, dn0), (1, dn1), (3, dn3)):

            @pl.when(relative == d)
            def _():
                ref[...] = dn

        @pl.when(relative == 2)
        def _():
            dn2[...] = dn[: ROWS // 2, :]
            dn2_rest[...] = dn[ROWS // 2 :, :]

    dgain[...] = jnp.broadcast_to(gain_sum / gain[...], (8, WIDTH))


def unattend(spot, q, k, v, lse, dmixed, normed, gain, wq, wk, wv, cos, sin, seg_col, seg_row):
    length = RING * ROWS
    return pl.pallas_call(
        unattend_kernel,
        out_shape=[
            jax.ShapeDtypeStruct((length, HALF), BF16),
            jax.ShapeDtypeStruct((8, WIDTH), F32),
        ]
        + [jax.ShapeDtypeStruct((rows, WIDTH), BF16) for rows in (ROWS, ROWS, ROWS // 2, ROWS // 2, ROWS)],
        in_specs=[SCALARS] + [WHOLE] * 14,
        out_specs=[WHOLE] * 7,
        scratch_shapes=[
            pltpu.VMEM((LANES, length), BF16),
            pltpu.VMEM((3 * ROWS, ROWS), F32),
            pltpu.VMEM((length, LANES), F32),
            pltpu.VMEM((length, LANES), F32),
        ],
        compiler_params=params(),
        cost_estimate=NO_COST,
        name="unattend",
    )(spot, q, k, v, lse, dmixed, normed, gain, wq, wk, wv, cos, sin, seg_col, seg_row)


PAY = 832
QUARTER = PAY // RING
GAINS = 768 + EXPERTS


def pack_kernel(spot, normed, dqkv, grad_out, s0, s1, s2, s3, own, other):
    core = spot[3]
    sums = (s0[...] + s1[...]) + (s2[...] + s3[...])
    row = lax.broadcasted_iota(jnp.int32, (32, HALF), 0)
    for side, out in enumerate((own, other)):
        cols = pl.ds(pl.multiple_of(((core + side) % 2) * HALF, HALF), HALF)
        left = (core + side) % 2 == 0
        out[0:HALF, :] = dot_tn(normed[:, cols], dqkv[...]).astype(BF16)
        out[HALF:768, :] = grad_out[:, cols]
        here = jnp.where(left, sums[:, :HALF], sums[:, HALF:])
        out[768:GAINS, :] = here[0:EXPERTS, :].astype(BF16)
        out[GAINS:, :] = jnp.where(row == 0, here[EXPERTS : EXPERTS + 1, :], 0.0).astype(BF16)


def add_all(refs):
    total = refs[0][...].astype(F32)
    for ref in refs[1:]:
        total = total + ref[...].astype(F32)
    return total.astype(BF16)


def quarter_rows(index):
    return pl.ds(pl.multiple_of(index * QUARTER, 16), QUARTER)


def reduce_core_kernel(spot, own, got, g0, g1, g2, g3, p0, p1, p2, p3, total):
    total[...] = add_all((own, got))
    gain = (g0[...] + g1[...]) + (g2[...] + g3[...])
    row = lax.broadcasted_iota(jnp.int32, (32, HALF), 0)
    tail = jnp.where(row == 1, gain[0:1, :HALF], total[GAINS:, :].astype(F32))
    total[GAINS:, :] = jnp.where(row == 2, gain[0:1, HALF:], tail).astype(BF16)
    for d, piece in enumerate((p0, p1, p2, p3)):
        piece[...] = total[quarter_rows((spot[2] + d) % RING), :]


def sum_kernel(spot, a, b, c, d, out):
    out[...] = add_all((a, b, c, d))


def gather_x_kernel(spot, a, b, c, d, out):
    for d, piece in enumerate((a, b, c, d)):
        out[quarter_rows((spot[2] + d) % RING), :] = piece[...]


def unpack_kernel(spot, own, got, query, key, value, grad_out, router, gains):
    for side, half in enumerate((own, got)):
        at = pl.ds(pl.multiple_of(((spot[3] + side) % 2) * HALF, HALF), HALF)
        query[at, :] = half[0:HALF, : 2 * LANES].astype(F32)
        key[at, :] = half[0:HALF, 2 * LANES : 3 * LANES].astype(F32)
        value[at, :] = half[0:HALF, 3 * LANES :].astype(F32)
        grad_out[:, at] = half[HALF:768, :].astype(F32)
        router[:, at] = half[768:GAINS, :].astype(F32)
        gains[0:1, at] = half[GAINS:, :].astype(F32)[0:1, :]
    both = own[GAINS:, :].astype(F32)[0:8, :] + got[GAINS:, :].astype(F32)[0:8, :]
    gains[1:2, :HALF] = both[1:2, :]
    gains[1:2, HALF:] = both[2:3, :]


def small_call(kernel, spot, refs, shapes, scratch=None, flops=1_000_000, others=()):
    return pl.pallas_call(
        ignoring(kernel, 1 + len(refs), len(others)),
        out_shape=[jax.ShapeDtypeStruct(shape, dtype) for shape, dtype in shapes],
        in_specs=[SCALARS] + [WHOLE] * len(refs) + [ANYWHERE] * len(others),
        out_specs=[WHOLE] * len(shapes),
        scratch_shapes=[pltpu.VMEM(scratch, BF16)] if scratch else [],
        compiler_params=params(),
        cost_estimate=pl.CostEstimate(flops=flops, bytes_accessed=2_000_000, transcendentals=0),
    )(spot, *refs, *others)


def sum_over_ep(spot, normed, dqkv, grad_out, sums, gains, dn, output, moe_slots):
    own, other = small_call(
        pack_kernel, spot, (normed, dqkv, grad_out, *sums), [((PAY, HALF), BF16)] * 2, flops=0
    )
    got = push(other, 0, 0, 1)
    pieces = small_call(
        reduce_core_kernel, spot, (own, got, *gains), [((QUARTER, HALF), BF16)] * 4, (PAY, HALF)
    )
    dn, halves = scatter_tp(*after(dn, pieces[0]))
    pieces = [push(pieces[d], 0, d, 0) for d in range(RING)]
    quarter = [((QUARTER, HALF), BF16)]
    (line,) = small_call(sum_kernel, spot, pieces, quarter, others=(*halves, moe_slots))
    (line,) = small_call(sum_kernel, spot, [push(line, d, 0, 0) for d in range(RING)], quarter, others=(output,))
    pieces = [push(line, 0, -d, 0) for d in range(RING)]
    (half,) = small_call(gather_x_kernel, spot, pieces, [((PAY, HALF), BF16)], others=dn[1:])
    made = small_call(
        unpack_kernel,
        spot,
        (half, push(half, 0, 0, 1)),
        [
            ((WIDTH, 2 * LANES), F32),
            ((WIDTH, LANES), F32),
            ((WIDTH, LANES), F32),
            ((ROWS, WIDTH), F32),
            ((EXPERTS, WIDTH), F32),
            ((8, WIDTH), F32),
        ],
    )
    return *made, dn


def hidden_kernel(a, b, c, hidden, gain, dmiddle, out):
    dn = a[...].astype(F32) + b[...].astype(F32) + c[...].astype(F32)
    x = hidden[...].astype(F32)
    inverse = lax.rsqrt(jnp.mean(x * x, axis=-1, keepdims=True) + NORM_EPS)
    plain = x * inverse
    scaled = dn * gain[...]
    along = jnp.mean(scaled * plain, axis=-1, keepdims=True)
    out[...] = dmiddle[...] + inverse * (scaled - plain * along)


def hidden_grad(dn, hidden, gain, dmiddle):
    return pl.pallas_call(
        hidden_kernel,
        out_shape=jax.ShapeDtypeStruct((ROWS, WIDTH), F32),
        in_specs=[WHOLE] * 6,
        out_specs=WHOLE,
        compiler_params=params(),
        cost_estimate=NO_COST,
        name="hidden_grad",
    )(*dn, hidden, gain, dmiddle)


def rope_tables(length):
    freqs = ROPE_BASE ** (-jnp.arange(HD // 2, dtype=F32) * 2.0 / HD)
    angles = jnp.arange(length, dtype=F32)[:, None] * freqs[None, :]
    cosine, sine = jnp.cos(angles), jnp.sin(angles)
    return jnp.concatenate([cosine] * 4, axis=1), jnp.concatenate([-sine, sine] * 2, axis=1)


def shards(
    hidden_in, segment_ids, expert_ids, slot_index, attn_gain, w_query, w_key, w_value, w_output,
    ffn_gain, w_router, w_gate_up, w_down, cotangent,
):
    length = RING * ROWS
    here, rank = lax.axis_index("ep"), lax.axis_index("tp")
    spot = jnp.stack([rank, here // 8, (here // 2) % 4, here % 2]).astype(jnp.int32)

    named = expert_ids[:, :, None] == jnp.arange(EXPERTS, dtype=jnp.int32)[None, None, :]
    slot_of = jnp.sum(jnp.where(named, slot_index[:, :, None] + 1, 0), axis=1) - 1
    chosen = (slot_of >= 0).astype(F32)
    table = slot_of.T.astype(F32)

    gain_one = attn_gain.astype(F32).reshape(1, WIDTH)
    gain_two = ffn_gain.astype(F32).reshape(1, WIDTH)
    cos, sin = rope_tables(length)
    seg_row = segment_ids
    seg_col = segment_ids.reshape(length, 1)

    group = [push_tp(hidden_in, -d) for d in range(RING)]
    cots = lax.all_gather(cotangent, "ep", axis=0, tiled=False, axis_index_groups=SAME_CORE)
    weights = jnp.concatenate([w_gate_up.reshape(WIDTH, 2 * HALF), w_down.reshape(HALF, WIDTH)], axis=0)
    made = attend(spot, group, gain_one, w_query, w_key, w_value, w_output, cos, sin, seg_col, seg_row)
    normed, q, k, v, mixed, lse = made[:6]
    branches = [push_tp(made[6 + d], d) for d in range(RING)]
    (weights,) = after((weights,), lse)
    weights = weights, push(weights, 0, 0, 1)
    middle, half_a, half_b, gates_t = route(hidden_in, branches, gain_two, w_router, chosen, table, weights[1])
    (pieces_a, pieces_b), slots_a, slots_b = dispatch(spot, half_a, half_b)
    first, second = Pieces(pieces_a[:4], pieces_b[:4]), Pieces(pieces_a[4:], pieces_b[4:])
    near = first.send_near()
    far = [first.send(0, 2)]
    held = after((pieces_b[2], pieces_b[6]), near[2], near[3])
    far += [first.send(1, 2, held[0]), second.send(1, 2, held[1])]
    held = after(second.near()[:2], *near)
    second.send(0, 1, held[0]), second.send(0, 3, held[1])
    held = after((*second.near()[2:], pieces_a[6]), *near, *far)
    second.send(1, 1, held[0]), second.send(1, 3, held[1]), second.send(0, 2, held[2])

    back_first, moe_slots, saved = expert(spot, 0, first, cots, weights[0])
    near = back_first.send_near()
    near.append(back_first.send(0, 2))
    back_second, moe_slots, saved_other = expert(spot, 1, second, cots, weights[1], moe_slots)
    held = after((back_first.made[1][2], *back_second.near()), *near)
    back_first.send(1, 2, held[0])
    near = back_second.send_near(held[1:])
    held = after((back_second.made[0][2], back_second.made[1][2], weight_grads(saved_other)), *near)
    back_second.send(0, 2, held[0])
    back_second.send(1, 2, held[1])
    grads_e = weight_grads(saved, push(held[2], 0, 0, 1))
    parts = to_owners(combine(slots_a, slots_b, back_first, back_second))

    dmiddle, dbranch, sums = unroute(
        spot, parts, gates_t, middle, cotangent, gain_two, w_router.T.astype(F32)
    )
    group_grad = gather_tp(dbranch)
    sums = [push_tp(sums, d) for d in range(RING)]

    (moe_slots,) = after((moe_slots,), *parts, grads_e)
    moe_slots = lax.all_to_all(
        moe_slots, "ep", split_axis=0, concat_axis=0, tiled=True, axis_index_groups=SAME_CORE
    )

    (summed_e,) = after((grads_e,), *group_grad[2])
    summed = lax.psum(summed_e, "tp")
    dmixed, grad_output = unmix(spot, group_grad, mixed, w_output, *sums[1:], summed_e)
    last = unattend(
        spot, q, k, v, lse, dmixed, normed, gain_one, w_query, w_key, w_value, cos, sin, seg_col, seg_row
    )
    gains = [push_tp(last[1], d) for d in range(RING)]
    output = finish(spot, table, moe_slots.reshape(CHIPS * PAIR, WIDTH), middle)
    grad_query, grad_key, grad_value, grad_output, grad_router, grad_gains, dn = sum_over_ep(
        spot, normed, last[0], grad_output, sums, gains, last[2:], output, moe_slots
    )
    grad_hidden = hidden_grad(dn, hidden_in, gain_one, dmiddle)
    grad_up, grad_down = cast_grads(summed, grad_query)
    return (
        output,
        grad_hidden,
        grad_gains[1],
        grad_query,
        grad_key,
        grad_value,
        grad_output,
        grad_gains[0],
        grad_router.T,
        grad_up.reshape(1, WIDTH, 2, HALF),
        grad_down.reshape(1, HALF, WIDTH),
    )


def solution(mesh):
    placed = (
        P(("ep", "tp"), None),
        P("ep", None),
        P(("ep", "tp"), None),
        P(("ep", "tp"), None),
        P(),
        P(None, "tp"),
        P(None, "tp"),
        P(None, "tp"),
        P("tp", None),
        P(),
        P(),
        P("ep", None, None, None),
        P("ep", None, None),
        P(("ep", "tp"), None),
    )
    return jax.shard_map(
        shards,
        mesh=mesh,
        in_specs=placed,
        out_specs=(
            P(("ep", "tp"), None),
            P(("ep", "tp"), None),
            P(),
            P(None, "tp"),
            P(None, "tp"),
            P(None, "tp"),
            P("tp", None),
            P(),
            P(),
            P("ep", None, None, None),
            P("ep", None, None),
        ),
        check_vma=False,
    )
```

```python
import jax
import jax.numpy as jnp
from jax import lax
from jax.experimental import pallas as pl
from jax.experimental.pallas import tpu as pltpu
from jax.sharding import PartitionSpec as P

HD = 64
ATT_SCALE = 0.015625
RES_SCALE = 0.22
NORM_EPS = 1e-06
ROPE_BASE = 10000.0
NEG_FILL = -1e30
HIGHEST = lax.Precision.HIGHEST
F32 = jnp.float32
BF16 = jnp.bfloat16

ROWS = 256
WIDTH = 1024
HALF = 512
CAP = 96
EXPERTS = 32
RING = 4
HEADS = 4
LANES = 128
VMEM_BYTES = 58 * 1024 * 1024
WHOLE = pl.BlockSpec(memory_space=pltpu.VMEM)
SCALARS = pl.BlockSpec(memory_space=pltpu.SMEM)
ANYWHERE = pl.BlockSpec(memory_space=pl.ANY)


def params():
    return pltpu.CompilerParams(vmem_limit_bytes=VMEM_BYTES)


NO_COST = pl.CostEstimate(flops=0, bytes_accessed=0, transcendentals=0)


def dot(a, b, precision=None):
    return jnp.dot(a, b, preferred_element_type=F32, precision=precision)


def dot_nt(a, b):
    return lax.dot_general(a, b, (((1,), (1,)), ((), ())), preferred_element_type=F32)


def dot_tn(a, b):
    return lax.dot_general(a, b, (((0,), (0,)), ((), ())), preferred_element_type=F32)


def place(z, x, core):
    return ((z % RING) * RING + (x % RING)) * 2 + core


def push(value, dz, dx, dc):
    if (dz % RING, dx % RING, dc) == (0, 0, 0):
        return value
    pairs = [
        (place(z, x, c), place(z + dz, x + dx, c ^ dc))
        for z in range(RING)
        for x in range(RING)
        for c in range(2)
    ]
    return lax.ppermute(value, "ep", pairs)


def push_tp(value, dy):
    if dy % RING == 0:
        return value
    return lax.ppermute(value, "tp", [(y, (y + dy) % RING) for y in range(RING)])


def after(values, *others):
    count = len(values)
    return pl.pallas_call(
        lambda *refs: None,
        out_shape=[jax.ShapeDtypeStruct(v.shape, v.dtype) for v in values],
        in_specs=[ANYWHERE] * (count + len(others)),
        out_specs=[ANYWHERE] * count,
        input_output_aliases={i: i for i in range(count)},
        cost_estimate=NO_COST,
        name="after",
    )(*values, *others)


def gather_tp(rows):
    after_me, before_me = push_tp(rows, -1), push_tp(rows, 1)
    half = rows.shape[0] // 2
    across = push_tp(after_me[:half], -1), push_tp(before_me[half:], 1)
    return rows, after_me, across, before_me


def add_halves_kernel(one, three, first, rest, ahead, behind):
    half = first.shape[0]
    ahead[0:half, :] = (one[0:half, :].astype(F32) + first[...].astype(F32)).astype(BF16)
    ahead[half:, :] = one[half:, :]
    behind[0:half, :] = three[0:half, :]
    behind[half:, :] = (three[half:, :].astype(F32) + rest[...].astype(F32)).astype(BF16)


def scatter_tp(own, one, two, two_rest, three):
    first, rest = push_tp(two, 1), push_tp(two_rest, -1)
    ahead, behind = pl.pallas_call(
        add_halves_kernel,
        out_shape=[jax.ShapeDtypeStruct(one.shape, BF16)] * 2,
        in_specs=[WHOLE] * 4,
        out_specs=[WHOLE] * 2,
        compiler_params=params(),
        cost_estimate=NO_COST,
        name="add_halves",
    )(one, three, first, rest)
    return (own, push_tp(ahead, 1), push_tp(behind, -1)), (first, rest)


def ignoring(kernel, first, count):
    return lambda *refs: kernel(*refs[:first], *refs[first + count :])


def swap_halves(v):
    lane = lax.broadcasted_iota(jnp.int32, v.shape, 1)
    return jnp.where(lane % HD < HD // 2, pltpu.roll(v, LANES - HD // 2, 1), pltpu.roll(v, HD // 2, 1))


def block_at(index):
    return pl.ds(pl.multiple_of(index * ROWS, ROWS), ROWS)


def key_range(block):
    return max(0, block - 2) * ROWS, (block + 1) * ROWS


def mask_bias(block, seg_col, seg_row):
    lo, hi = key_range(block)
    key_pos = lo + lax.broadcasted_iota(jnp.int32, (hi - lo, ROWS), 0)
    query_pos = block * ROWS + lax.broadcasted_iota(jnp.int32, (hi - lo, ROWS), 1)
    same = seg_col[lo:hi, :] == seg_row[:, block * ROWS : (block + 1) * ROWS]
    return jnp.where(same & (key_pos <= query_pos), 0.0, NEG_FILL)


def attend_kernel(
    rank, x0, x1, x2, x3, gain, wq, wk, wv, wo, cos, sin, seg_col, seg_row,
    normed_far, q_far, k_far, v_far, mixed_far, lse, br0, br1, br2, br3,
    normed, q_out, k_out, v_out, mixed, branches, vt, bias, sems,
):
    me = rank[0]
    pairs = ((normed, normed_far), (q_out, q_far), (k_out, k_far), (v_out, v_far), (mixed, mixed_far))
    stores = [pltpu.make_async_copy(near, far, sems.at[i]) for i, (near, far) in enumerate(pairs)]
    lane = lax.broadcasted_iota(jnp.int32, (ROWS, LANES), 1)
    for d, x_ref in enumerate((x0, x1, x2, x3)):
        at = block_at((me + d) % RING)
        x = x_ref[...].astype(F32)
        inverse = lax.rsqrt(jnp.mean(x * x, axis=-1, keepdims=True) + NORM_EPS)
        low = (x * inverse * gain[...]).astype(BF16)
        normed[at, :] = low
        cos_here, sin_here = cos[at, :], sin[at, :]

        def rope(v):
            return v * cos_here + swap_halves(v) * sin_here

        query = dot(low, wq[...])
        for pair in range(2):
            q = rope(query[:, pair * LANES : (pair + 1) * LANES]) * ATT_SCALE
            other = pltpu.roll(q, HD, 1)
            keep = (lane < HD) if pair == 0 else (lane >= HD)
            first, second = (q, other) if pair == 0 else (other, q)
            at_head = 2 * pair * LANES
            q_out[at, at_head : at_head + LANES] = jnp.where(keep, first, 0.0).astype(BF16)
            q_out[at, at_head + LANES : at_head + 2 * LANES] = jnp.where(keep, second, 0.0).astype(BF16)
        k_out[at, :] = rope(dot(low, wk[...])).astype(BF16)
        v_out[at, :] = dot(low, wv[...]).astype(BF16)
    for copy in stores[:4]:
        copy.start()
    vt[...] = v_out[...].astype(F32).T.astype(BF16)
    for b in range(RING):
        lo, hi = key_range(b)
        rows = slice(b * ROWS, (b + 1) * ROWS)
        bias[0 : hi - lo, :] = mask_bias(b, seg_col, seg_row)
        outs = []
        for h in range(HEADS):
            q = q_out[rows, h * LANES : (h + 1) * LANES]
            scores = dot_nt(k_out[lo:hi, :], q) + bias[0 : hi - lo, :]
            top = jnp.max(scores, axis=0, keepdims=True)
            weights = jnp.exp(scores - top)
            total = jnp.sum(weights, axis=0, keepdims=True)
            out = dot(vt[:, lo:hi], weights.astype(BF16)) * (1.0 / total)
            outs.append(out.T)
            lse[h : h + 1, rows] = top + jnp.log(total)
        mixed[rows, 0:LANES] = jnp.where(lane < HD, outs[0], pltpu.roll(outs[1], HD, 1)).astype(BF16)
        mixed[rows, LANES:] = jnp.where(lane < HD, pltpu.roll(outs[2], HD, 1), outs[3]).astype(BF16)
        branches[b] = dot(mixed[rows, :], wo[...]).astype(BF16)
        for d, br in enumerate((br0, br1, br2, br3)):

            @pl.when((b - me + RING) % RING == d)
            def _():
                pltpu.make_async_copy(branches.at[b], br, sems.at[5 + b]).start()

    stores[4].start()
    for copy in stores:
        copy.wait()
    for b in range(RING):
        for d, br in enumerate((br0, br1, br2, br3)):

            @pl.when((b - me + RING) % RING == d)
            def _():
                pltpu.make_async_copy(branches.at[b], br, sems.at[5 + b]).wait()


def attend(rank, pieces, gain, wq, wk, wv, wo, cos, sin, seg_col, seg_row, *others):
    length = RING * ROWS
    return pl.pallas_call(
        ignoring(attend_kernel, 14, len(others)),
        out_shape=[
            jax.ShapeDtypeStruct((length, WIDTH), BF16),
            jax.ShapeDtypeStruct((length, HEADS * LANES), BF16),
            jax.ShapeDtypeStruct((length, LANES), BF16),
            jax.ShapeDtypeStruct((length, LANES), BF16),
            jax.ShapeDtypeStruct((length, HEADS * HD), BF16),
            jax.ShapeDtypeStruct((8, length), F32),
        ]
        + [jax.ShapeDtypeStruct((ROWS, WIDTH), BF16)] * RING,
        in_specs=[SCALARS] + [WHOLE] * 13 + [ANYWHERE] * len(others),
        out_specs=[ANYWHERE] * 5 + [WHOLE] + [ANYWHERE] * 4,
        scratch_shapes=[
            pltpu.VMEM((length, WIDTH), BF16),
            pltpu.VMEM((length, HEADS * LANES), BF16),
            pltpu.VMEM((length, LANES), BF16),
            pltpu.VMEM((length, LANES), BF16),
            pltpu.VMEM((length, HEADS * HD), BF16),
            pltpu.VMEM((RING, ROWS, WIDTH), BF16),
            pltpu.VMEM((LANES, length), BF16),
            pltpu.VMEM((3 * ROWS, ROWS), F32),
            pltpu.SemaphoreType.DMA((9,)),
        ],
        compiler_params=params(),
        cost_estimate=NO_COST,
        name="attend",
    )(rank, *pieces, gain, wq, wk, wv, wo, cos, sin, seg_col, seg_row, *others)


def high_low(v):
    high = v.astype(BF16)
    return jnp.concatenate([high, (v - high.astype(F32)).astype(BF16)], axis=1)


def route_kernel(x, b0, b1, b2, b3, gain, wr, chosen, table, middle, half_a, half_b, gates_t):
    branch = b0[...].astype(F32) + b1[...].astype(F32) + b2[...].astype(F32) + b3[...].astype(F32)
    mid = x[...].astype(F32) + RES_SCALE * branch
    middle[...] = mid
    inverse = lax.rsqrt(jnp.mean(mid * mid, axis=-1, keepdims=True) + NORM_EPS)
    routed = (mid * inverse * gain[...]).astype(BF16)
    half_b[0:ROWS, :] = routed[:, HALF:]
    logits = jnp.where(chosen[...] > 0.0, dot(routed, wr[...]), NEG_FILL)
    weights = jnp.exp(logits - jnp.max(logits, axis=-1, keepdims=True))
    gates = (weights / jnp.sum(weights, axis=-1, keepdims=True)).T
    gates_t[...] = gates
    half_a[0:ROWS, :] = routed[:, :HALF]
    half_a[ROWS : ROWS + EXPERTS, :] = high_low(gates)
    slots = jnp.concatenate([table[...], jnp.zeros_like(gates)], axis=1).astype(BF16)
    half_a[ROWS + EXPERTS :, :] = slots
    half_b[ROWS:, :] = slots


def route(x, branches, gain, wr, chosen, table, *others):
    return pl.pallas_call(
        ignoring(route_kernel, 9, len(others)),
        out_shape=[
            jax.ShapeDtypeStruct((ROWS, WIDTH), F32),
            jax.ShapeDtypeStruct((ROWS + 2 * EXPERTS, HALF), BF16),
            jax.ShapeDtypeStruct((ROWS + EXPERTS, HALF), BF16),
            jax.ShapeDtypeStruct((EXPERTS, ROWS), F32),
        ],
        in_specs=[WHOLE] * 9 + [ANYWHERE] * len(others),
        out_specs=[WHOLE] * 4,
        compiler_params=params(),
        cost_estimate=pl.CostEstimate(flops=20_000_000, bytes_accessed=5_000_000, transcendentals=8192),
        name="route",
    )(x, *branches, gain, wr, chosen, table, *others)


PIECE = RING * CAP
EXTRA = 16


def line_row(d, p, e):
    return p * 8 + e * 4 + d


def slot_matrix(row):
    slot = lax.broadcasted_iota(jnp.int32, (CAP, ROWS), 0).astype(F32)
    return jnp.where(slot == row, 1.0, 0.0)


def line_matrix(slots, d):
    rows = [line_row(d, p, e) for p in range(RING) for e in range(2)]
    return jnp.concatenate([slot_matrix(slots[r : r + 1, :]).astype(BF16) for r in rows], axis=0)


def expert_row(spot, half, d, p, e):
    z, x, core = spot[1], spot[2], spot[3]
    if half == 0:
        x = (x + p) % RING
    else:
        z = (z + p) % RING
    return (z * RING + x) * 2 + (core + e) % 2


def fill_pieces(slots, rows, pieces):
    for d in range(RING):
        filled = dot(line_matrix(slots, d), rows[d][0:ROWS, :]).astype(BF16)
        for p in range(RING):
            for e in range(2):
                pieces[e * 4 + p][d * CAP : (d + 1) * CAP, :] = filled[(p * 2 + e) * CAP : (p * 2 + e + 1) * CAP, :]


def pick_rows(spot, half, blocks, first, table, picked):
    for d in range(RING):
        table[...] = blocks[d][first : first + EXPERTS, :].astype(F32)
        for p in range(RING):
            for e in range(2):
                r = line_row(d, p, e)
                picked[r : r + 1, :] = table[pl.ds(expert_row(spot, half, d, p, e), 1), :]


def dispatch_kernel(spot, *refs):
    blocks, pieces, slots, (table, gates, picked) = refs[:8], (refs[8:16], refs[16:24]), refs[24:26], refs[26:]
    pick_rows(spot, 0, blocks[:4], ROWS, table, gates)
    for half in range(2):
        mine = blocks[4 * half : 4 * half + 4]
        pick_rows(spot, half, mine, ROWS + EXPERTS * (1 - half), table, picked)
        slots[half][...] = picked[:, :ROWS]
        fill_pieces(slots[half], mine, pieces[half])
        if half == 0:
            for p in range(RING):
                for e in range(2):
                    at = slice(p * 8 + e * 4, p * 8 + e * 4 + 4)
                    extra = jnp.concatenate([gates[at, :], picked[at, :], jnp.zeros((8, HALF), F32)], axis=0)
                    pieces[0][e * 4 + p][PIECE:, :] = extra.astype(BF16)


def combine_kernel(slots_a, slots_b, *refs):
    everyone, (second, sems) = range(RING), refs[24:]
    fetches = [pltpu.make_async_copy(refs[8 + i], second.at[i], sems.at[i]) for i in range(8)]
    for copy in fetches:
        copy.start()
    for half, slots in enumerate((slots_a, slots_b)):
        if half == 1:
            for copy in fetches:
                copy.wait()
        pieces = refs[:8] if half == 0 else [second.at[i] for i in range(8)]
        rows = refs[16 + 4 * half : 20 + 4 * half]
        for d in everyone:
            filled = [pieces[e * 4 + p][d * CAP : (d + 1) * CAP, :] for p in everyone for e in range(2)]
            filled = jnp.concatenate(filled, axis=0)
            rows[d][0:ROWS, :] = dot_tn(line_matrix(slots, d), filled).astype(BF16)
        if half == 0:
            tables = [pieces[i][PIECE:, :].astype(F32) for i in range(8)]
            for d in everyone:
                picked = [tables[e * 4 + p][d : d + 1, :] for p in everyone for e in range(2)]
                extra = jnp.concatenate(picked + [jnp.zeros((8, HALF), F32)], axis=0)
                rows[d][ROWS:, :] = extra.astype(BF16)


SLOT_COST = pl.CostEstimate(flops=1_000_000_000, bytes_accessed=5_000_000, transcendentals=0)
TABLE = pltpu.VMEM((EXPERTS, HALF), F32)


def shape_of(rows, dtype=BF16):
    return jax.ShapeDtypeStruct((rows, HALF), dtype)


def spread_rows(half_a, half_b):
    return [push(half_a, -d, 0, 0) for d in range(RING)] + [push(half_b, 0, -d, 0) for d in range(RING)]


def dispatch(spot, half_a, half_b):
    made = pl.pallas_call(
        dispatch_kernel,
        out_shape=[shape_of(PIECE + EXTRA)] * 8
        + [shape_of(PIECE)] * 8
        + [jax.ShapeDtypeStruct((EXPERTS, ROWS), F32)] * 2,
        in_specs=[SCALARS] + [WHOLE] * 8,
        out_specs=[WHOLE] * 18,
        scratch_shapes=[TABLE] * 3,
        compiler_params=params(),
        cost_estimate=SLOT_COST,
        name="dispatch",
    )(spot, *spread_rows(half_a, half_b))
    return (made[:8], made[8:16]), made[16], made[17]


class Pieces:
    def __init__(self, half_a, half_b):
        self.made = list(half_a), list(half_b)
        self.got = [half_a[0], None, None, None], [half_b[0], None, None, None]

    def send(self, half, p, held=None):
        piece = self.made[half][p] if held is None else held
        self.got[half][-p % RING] = push(piece, 0, p, 0) if half == 0 else push(piece, p, 0, 0)
        return self.got[half][-p % RING]

    def send_near(self, held=(None,) * 4):
        places = (0, 1), (0, 3), (1, 1), (1, 3)
        return [self.send(half, p, piece) for (half, p), piece in zip(places, held)]

    def near(self):
        return self.made[0][1], self.made[0][3], self.made[1][1], self.made[1][3]


def combine(slots_a, slots_b, first, second, *others):
    pieces = [*first.got[0], *second.got[0], *first.got[1], *second.got[1]]
    return pl.pallas_call(
        ignoring(combine_kernel, 18, len(others)),
        out_shape=[shape_of(ROWS + EXTRA)] * RING + [shape_of(ROWS)] * RING,
        in_specs=[WHOLE] * 10 + [ANYWHERE] * (8 + len(others)),
        out_specs=[WHOLE] * 8,
        scratch_shapes=[pltpu.VMEM((8, PIECE, HALF), BF16), pltpu.SemaphoreType.DMA((8,))],
        compiler_params=params(),
        cost_estimate=pl.CostEstimate(flops=60_000_000_000, bytes_accessed=0, transcendentals=0),
        name="combine",
    )(slots_a, slots_b, *pieces, *others)


def to_owners(partial):
    got = [None] * 8
    for d in range(RING):
        got[-d % RING] = push(partial[d], d, 0, 0)
        got[4 + -d % RING] = push(partial[4 + d], 0, d, 0)
    return got


CHIPS = RING * RING
PAIR = 2 * CAP


def chips_matrix(spot, table, step):
    rows = []
    for i in range(RING):
        for e in range(2):
            expert = (step * RING + i) * 2 + (spot[3] + e) % 2
            rows.append(slot_matrix(table[pl.ds(expert, 1), :]).astype(BF16))
    return jnp.concatenate(rows, axis=0)


def finish_kernel(spot, table, slots, middle, out, total):
    step = pl.program_id(0)
    term = dot_tn(chips_matrix(spot, table, step), slots[...])

    @pl.when(step == 0)
    def _():
        total[...] = term

    @pl.when(step > 0)
    def _():
        total[...] += term

    @pl.when(step == RING - 1)
    def _():
        out[...] = (middle[...] + RES_SCALE * total[...]).astype(BF16)


def finish(spot, table, slots, middle):
    return pl.pallas_call(
        finish_kernel,
        grid=(RING,),
        out_shape=jax.ShapeDtypeStruct((ROWS, WIDTH), BF16),
        in_specs=[SCALARS, WHOLE, pl.BlockSpec((RING * PAIR, WIDTH), lambda s: (s, 0)), WHOLE],
        out_specs=pl.BlockSpec((ROWS, WIDTH), lambda s: (0, 0)),
        scratch_shapes=[pltpu.VMEM((ROWS, WIDTH), F32)],
        compiler_params=params(),
        cost_estimate=SLOT_COST,
        name="finish",
    )(spot, table, slots, middle)


SAME_CORE = [list(range(core, EXPERTS, 2)) for core in range(2)]


STEPS = RING
STEP_ROWS = RING * CAP


def expert_kernel(e, spot, *refs):
    ra, rb, cot, weights = refs[:4], refs[4:8], refs[8], refs[9]
    refs = refs[10 + e :]
    qa, qb, moe, (disp_out, dgu_out, inner_out, dex_out) = refs[:4], refs[4:8], refs[8], refs[9:13]
    wgu, wd, rows_in, cot_in, extra_in, back_out, moe_out, extra_out, weight_sem, in_sem, out_sem = refs[13:]
    step = pl.program_id(0)
    loads = [
        pltpu.make_async_copy(weights.at[pl.ds(0, WIDTH)], wgu, weight_sem.at[0]),
        pltpu.make_async_copy(weights.at[pl.ds(WIDTH, HALF)], wd, weight_sem.at[1]),
    ]

    def places(dx, half_a, half_b, halves, extra):
        slot = dx % 2
        ends = [
            (half_a[dx].at[pl.ds(0, PIECE)], halves.at[slot, :, pl.ds(0, HALF)]),
            (half_a[dx].at[pl.ds(PIECE, EXTRA)], extra.at[slot]),
        ]
        for dz in range(RING):
            ends.append((half_b[dz].at[pl.ds(dx * CAP, CAP)], halves.at[slot, pl.ds(dz * CAP, CAP), pl.ds(HALF, HALF)]))
        return ends

    def chip(dz, dx):
        return ((spot[1] + dz) % RING) * RING + (spot[2] + dx) % RING

    def fetches(dx):
        ends = places(dx, ra, rb, rows_in, extra_in)
        for dz in range(RING):
            ends.append((cot.at[chip(dz, dx)], cot_in.at[dx % 2, pl.ds(dz * ROWS, ROWS)]))
        return [pltpu.make_async_copy(far, near, in_sem.at[dx % 2, n]) for n, (far, near) in enumerate(ends)]

    def stores(dx):
        ends = places(dx, qa, qb, back_out, extra_out)
        for dz in range(RING):
            ends.append((moe.at[chip(dz, dx), pl.ds(e * CAP, CAP)], moe_out.at[dx % 2, pl.ds(dz * CAP, CAP)]))
        return [pltpu.make_async_copy(near, far, out_sem.at[dx % 2, n]) for n, (far, near) in enumerate(ends)]

    for j in range(STEPS):

        @pl.when(step == j)
        def _():
            if j == 0:
                for copy in fetches(0) + loads:
                    copy.start()
            if j + 1 < STEPS:
                for copy in fetches(j + 1):
                    copy.start()
            for copy in fetches(j):
                copy.wait()
            if j == 0:
                for copy in loads:
                    copy.wait()
            if j >= 2:
                for copy in stores(j - 2):
                    copy.wait()

    slot = step % 2
    extra = extra_in[slot].astype(F32)
    gates = extra[0:4, :ROWS] + extra[0:4, ROWS:]
    fills = [slot_matrix(extra[4 + dz : 5 + dz, :ROWS]) for dz in range(RING)]
    gate_slot = jnp.concatenate(
        [jnp.sum(fills[dz] * gates[dz : dz + 1, :], axis=1, keepdims=True) for dz in range(RING)], axis=0
    )
    rows = rows_in[slot]
    disp_out[...] = rows
    gate_up = dot(rows, wgu[...])
    dmoe = [
        dot(fills[dz].astype(BF16), cot_in[slot, dz * ROWS : (dz + 1) * ROWS, :]) for dz in range(RING)
    ]
    dmoe = RES_SCALE * jnp.concatenate(dmoe, axis=0)
    dex = (gate_slot * dmoe).astype(BF16)
    dex_out[...] = dex
    dinner = dot_nt(dex, wd[...])
    gate, up = gate_up[:, :HALF], gate_up[:, HALF:]
    sigmoid = jax.nn.sigmoid(gate)
    silu = gate * sigmoid
    inner = (silu * up).astype(BF16)
    inner_out[...] = inner
    made = dot(inner, wd[...]).astype(BF16).astype(F32)
    dgate = dinner * up * sigmoid * (1.0 + gate * (1.0 - sigmoid))
    dgu = jnp.concatenate([dgate.astype(BF16), (dinner * silu).astype(BF16)], axis=1)
    dgu_out[...] = dgu
    back_out[slot] = dot_nt(dgu, wgu[...]).astype(BF16)
    moe_out[slot] = (gate_slot * made).astype(BF16)
    dgate_slot = jnp.sum(dmoe * made, axis=1, keepdims=True)
    dgates = [
        jnp.sum(fills[dz] * dgate_slot[dz * CAP : (dz + 1) * CAP, :], axis=0, keepdims=True) for dz in range(RING)
    ]
    dgates = jnp.concatenate(dgates + [jnp.zeros((EXTRA - RING, ROWS), F32)], axis=0)
    extra_out[slot] = high_low(dgates)

    for j in range(STEPS):

        @pl.when(step == j)
        def _():
            for copy in stores(j):
                copy.start()
            if j == STEPS - 1:
                for copy in stores(j - 1) + stores(j):
                    copy.wait()


def expert(spot, e, pieces, cots, weights, *moe):
    total = STEPS * STEP_ROWS
    wide = pl.BlockSpec((STEP_ROWS, WIDTH), lambda s: (s, 0))
    narrow = pl.BlockSpec((STEP_ROWS, HALF), lambda s: (s, 0))
    buf, small = pltpu.VMEM((2, STEP_ROWS, WIDTH), BF16), pltpu.VMEM((2, EXTRA, HALF), BF16)
    made = pl.pallas_call(
        lambda *refs: expert_kernel(e, *refs),
        grid=(STEPS,),
        out_shape=[shape_of(PIECE + EXTRA)] * RING
        + [shape_of(PIECE)] * RING
        + [
            jax.ShapeDtypeStruct((CHIPS, PAIR, WIDTH), BF16),
            jax.ShapeDtypeStruct((total, WIDTH), BF16),
            jax.ShapeDtypeStruct((total, WIDTH), BF16),
            jax.ShapeDtypeStruct((total, HALF), BF16),
            jax.ShapeDtypeStruct((total, WIDTH), BF16),
        ],
        in_specs=[SCALARS] + [ANYWHERE] * (10 + e),
        out_specs=[ANYWHERE] * 9 + [wide, wide, narrow, wide],
        scratch_shapes=[
            pltpu.VMEM((WIDTH, WIDTH), BF16),
            pltpu.VMEM((HALF, WIDTH), BF16),
            buf, pltpu.VMEM((2, RING * ROWS, WIDTH), BF16), small, buf, buf, small,
            pltpu.SemaphoreType.DMA((2,)),
            pltpu.SemaphoreType.DMA((2, 10)),
            pltpu.SemaphoreType.DMA((2, 10)),
        ],
        input_output_aliases={11: 8} if e else {},
        compiler_params=params(),
        cost_estimate=NO_COST,
        name="expert",
    )(spot, *pieces.got[0], *pieces.got[1], cots, weights, *moe)
    return Pieces(made[:4], made[4:8]), made[8], made[9:]


def weight_grads_kernel(with_other, *refs):
    disp, dgu, inner, dex = refs[:4]
    other, out = refs[4] if with_other else None, refs[4 + with_other]
    disp_in, dgu_in, inner_in, dex_in, made, other_in, sems, out_sems = refs[5 + with_other :]
    pairs = [(disp, disp_in), (dgu, dgu_in), (inner, inner_in), (dex, dex_in)]
    if with_other:
        pairs.append((other, other_in))
    fetches = [pltpu.make_async_copy(far, near, sems.at[i]) for i, (far, near) in enumerate(pairs)]
    stores = [
        pltpu.make_async_copy(made.at[pl.ds(i * HALF, HALF)], out.at[pl.ds(i * HALF, HALF)], out_sems.at[i])
        for i in range(3)
    ]
    for copy in fetches:
        copy.start()
    for i, left in enumerate((disp_in, disp_in, inner_in)):
        if i == 0:
            fetches[0].wait()
            fetches[1].wait()
        if i == 2:
            fetches[2].wait()
            fetches[3].wait()
        if with_other and i == 0:
            fetches[4].wait()
        cols = slice(i * HALF, (i + 1) * HALF) if i < 2 else slice(None)
        grad = dot_tn(left[:, cols], (dgu_in if i < 2 else dex_in)[...])
        if with_other:
            grad = grad.astype(BF16).astype(F32) + other_in[i * HALF : (i + 1) * HALF, :].astype(F32)
        made[i * HALF : (i + 1) * HALF, :] = grad.astype(BF16)
        stores[i].start()
    for copy in stores:
        copy.wait()


def weight_grads(saved, *other):
    wide, narrow = pltpu.VMEM((4 * STEP_ROWS, WIDTH), BF16), pltpu.VMEM((4 * STEP_ROWS, HALF), BF16)
    grads = pltpu.VMEM((WIDTH + HALF, WIDTH), BF16)
    return pl.pallas_call(
        lambda *refs: weight_grads_kernel(len(other), *refs),
        out_shape=jax.ShapeDtypeStruct((WIDTH + HALF, WIDTH), BF16),
        in_specs=[ANYWHERE] * (4 + len(other)),
        out_specs=ANYWHERE,
        scratch_shapes=[
            wide, wide, narrow, wide, grads, grads, pltpu.SemaphoreType.DMA((5,)), pltpu.SemaphoreType.DMA((3,)),
        ],
        compiler_params=params(),
        cost_estimate=NO_COST,
        name="weight_grads",
    )(*saved, *other)


def cast_grads_kernel(grads, up, down):
    for i in range(2):
        up[:, i, :] = grads[0:WIDTH, i * HALF : (i + 1) * HALF].astype(F32)
    down[...] = grads[WIDTH:, :].astype(F32)


def cast_grads(grads, *others):
    return pl.pallas_call(
        ignoring(cast_grads_kernel, 1, len(others)),
        out_shape=[
            jax.ShapeDtypeStruct((WIDTH, 2, HALF), F32),
            jax.ShapeDtypeStruct((HALF, WIDTH), F32),
        ],
        in_specs=[WHOLE] + [ANYWHERE] * len(others),
        out_specs=[WHOLE] * 2,
        compiler_params=params(),
        cost_estimate=NO_COST,
        name="cast_grads",
    )(grads, *others)


def unroute_kernel(spot, *refs):
    parts, (gates_t, middle, cot, gain, wr_t, dmiddle, dbranch, sums, gates, dlogits) = refs[:8], refs[8:]

    def four(pieces):
        a, b, c, d = (piece[0:ROWS, :].astype(F32) for piece in pieces)
        return (a + b) + (c + d)

    order = [
        (((spot[1] + dz) % RING) * RING + (spot[2] + dx) % RING) * 2 + (spot[3] + e) % 2
        for dz in range(RING)
        for dx in range(RING)
        for e in range(2)
    ]
    for i, at in enumerate(order):
        gates[i : i + 1, :] = gates_t[pl.ds(at, 1), :]
    tables = [part[ROWS:, :].astype(F32) for part in parts[:4]]
    dgates = jnp.concatenate([t[0:8, :ROWS] + t[0:8, ROWS:] for t in tables], axis=0)
    made = gates[...] * (dgates - jnp.sum(gates[...] * dgates, axis=0, keepdims=True))
    for i, at in enumerate(order):
        dlogits[pl.ds(at, 1), :] = made[i : i + 1, :]
    drouted = jnp.concatenate([four(parts[:4]), four(parts[4:])], axis=1)
    drouted = drouted + dot(dlogits[...].T, wr_t[...], HIGHEST)
    mid = middle[...]
    inverse = lax.rsqrt(jnp.mean(mid * mid, axis=-1, keepdims=True) + NORM_EPS)
    plain = mid * inverse
    routed = (plain * gain[...]).astype(BF16).astype(F32)
    sums[0:EXPERTS, :] = dot(dlogits[...], routed, HIGHEST)
    sums[EXPERTS : EXPERTS + 8, :] = jnp.broadcast_to(jnp.sum(drouted * plain, axis=0, keepdims=True), (8, WIDTH))
    scaled = drouted * gain[...]
    along = jnp.mean(scaled * plain, axis=-1, keepdims=True)
    total = cot[...].astype(F32) + inverse * (scaled - plain * along)
    dmiddle[...] = total
    dbranch[...] = (RES_SCALE * total).astype(BF16)


def unroute(spot, parts, gates_t, middle, cot, gain, wr_t, *others):
    return pl.pallas_call(
        ignoring(unroute_kernel, 14, len(others)),
        out_shape=[
            jax.ShapeDtypeStruct((ROWS, WIDTH), F32),
            jax.ShapeDtypeStruct((ROWS, WIDTH), BF16),
            jax.ShapeDtypeStruct((EXPERTS + 8, WIDTH), F32),
        ],
        in_specs=[SCALARS] + [WHOLE] * 13 + [ANYWHERE] * len(others),
        out_specs=[WHOLE] * 3,
        scratch_shapes=[pltpu.VMEM((EXPERTS, ROWS), F32), pltpu.VMEM((EXPERTS, ROWS), F32)],
        compiler_params=params(),
        cost_estimate=NO_COST,
        name="unroute",
    )(spot, *parts, gates_t, middle, cot, gain, wr_t, *others)


def unmix_kernel(rank, d0, d1, d2, d2_rest, d3, mixed, wo, dmixed, grad_out):
    me = rank[0]
    lane = lax.broadcasted_iota(jnp.int32, (ROWS, LANES), 1)
    for d, ref in enumerate((d0, d1, d2, d3)):
        at = block_at((me + d) % RING)
        grad = jnp.concatenate([d2[...], d2_rest[...]], axis=0) if d == 2 else ref[...]
        low = dot_nt(grad, wo[...])
        for pair in range(2):
            both = low[:, pair * LANES : (pair + 1) * LANES]
            other = pltpu.roll(both, HD, 1)
            keep = (lane < HD) if pair == 0 else (lane >= HD)
            first, second = (both, other) if pair == 0 else (other, both)
            at_head = 2 * pair * LANES
            dmixed[at, at_head : at_head + LANES] = jnp.where(keep, first, 0.0).astype(BF16)
            dmixed[at, at_head + LANES : at_head + 2 * LANES] = jnp.where(keep, second, 0.0).astype(BF16)
        term = dot_tn(mixed[at, :], grad)
        total = term if d == 0 else total + term
    grad_out[...] = total.astype(BF16)


def unmix(rank, pieces, mixed, wo, *others):
    length = RING * ROWS
    return pl.pallas_call(
        ignoring(unmix_kernel, 8, len(others)),
        out_shape=[
            jax.ShapeDtypeStruct((length, HEADS * LANES), BF16),
            jax.ShapeDtypeStruct((HEADS * HD, WIDTH), BF16),
        ],
        in_specs=[SCALARS] + [WHOLE] * 7 + [ANYWHERE] * len(others),
        out_specs=[WHOLE] * 2,
        compiler_params=params(),
        cost_estimate=pl.CostEstimate(flops=1_100_000_000, bytes_accessed=5_000_000, transcendentals=0),
        name="unmix",
    )(rank, pieces[0], pieces[1], *pieces[2], pieces[3], mixed, wo, *others)


def unattend_kernel(
    spot, q_in, k_in, v_in, lse, dmixed, normed, gain, wq, wk, wv, cos, sin, seg_col, seg_row,
    dqkv, dgain, dn0, dn1, dn2, dn2_rest, dn3, kt, bias, dk, dv,
):
    me = spot[0]
    lane = lax.broadcasted_iota(jnp.int32, (ROWS, LANES), 1)
    kt[...] = k_in[...].astype(F32).T.astype(BF16)
    dk[...] = jnp.zeros_like(dk)
    dv[...] = jnp.zeros_like(dv)

    def unrope(v, rows):
        return v * cos[rows, :] - swap_halves(v) * sin[rows, :]

    for b in range(RING):
        lo, hi = key_range(b)
        rows = slice(b * ROWS, (b + 1) * ROWS)
        bias[0 : hi - lo, :] = mask_bias(b, seg_col, seg_row)
        dqs = []
        for h in range(HEADS):
            cols = slice(h * LANES, (h + 1) * LANES)
            q, do = q_in[rows, cols], dmixed[rows, cols]
            scores = dot_nt(k_in[lo:hi, :], q) + bias[0 : hi - lo, :]
            probs = jnp.exp(scores - lse[h : h + 1, rows])
            dprobs = dot_nt(v_in[lo:hi, :], do)
            delta = jnp.sum(probs * dprobs, axis=0, keepdims=True)
            dscores = (probs * (dprobs - delta)).astype(BF16)
            dv[lo:hi, :] += dot(probs.astype(BF16), do)
            dk[lo:hi, :] += dot(dscores, q)
            dqs.append(dot(kt[:, lo:hi], dscores).T * ATT_SCALE)
        first = jnp.where(lane < HD, dqs[0], pltpu.roll(dqs[1], HD, 1))
        second = jnp.where(lane < HD, pltpu.roll(dqs[2], HD, 1), dqs[3])
        dqkv[rows, 0:LANES] = unrope(first, rows).astype(BF16)
        dqkv[rows, LANES : 2 * LANES] = unrope(second, rows).astype(BF16)
    for b in range(RING):
        rows = slice(b * ROWS, (b + 1) * ROWS)
        dqkv[rows, 2 * LANES : 3 * LANES] = unrope(dk[rows, :], rows).astype(BF16)
        dqkv[rows, 3 * LANES :] = dv[rows, :].astype(BF16)
        dn = dot_nt(dqkv[rows, : 2 * LANES], wq[...])
        dn = dn + dot_nt(dqkv[rows, 2 * LANES : 3 * LANES], wk[...])
        dn = dn + dot_nt(dqkv[rows, 3 * LANES :], wv[...])
        term = jnp.sum(dn * normed[rows, :].astype(F32), axis=0, keepdims=True)
        gain_sum = term if b == 0 else gain_sum + term
        dn = dn.astype(BF16)
        relative = (b - me + RING) % RING
        for d, ref in ((0, dn0), (1, dn1), (3, dn3)):

            @pl.when(relative == d)
            def _():
                ref[...] = dn

        @pl.when(relative == 2)
        def _():
            dn2[...] = dn[: ROWS // 2, :]
            dn2_rest[...] = dn[ROWS // 2 :, :]

    dgain[...] = jnp.broadcast_to(gain_sum / gain[...], (8, WIDTH))


def unattend(spot, q, k, v, lse, dmixed, normed, gain, wq, wk, wv, cos, sin, seg_col, seg_row):
    length = RING * ROWS
    return pl.pallas_call(
        unattend_kernel,
        out_shape=[
            jax.ShapeDtypeStruct((length, HALF), BF16),
            jax.ShapeDtypeStruct((8, WIDTH), F32),
        ]
        + [jax.ShapeDtypeStruct((rows, WIDTH), BF16) for rows in (ROWS, ROWS, ROWS // 2, ROWS // 2, ROWS)],
        in_specs=[SCALARS] + [WHOLE] * 14,
        out_specs=[WHOLE] * 7,
        scratch_shapes=[
            pltpu.VMEM((LANES, length), BF16),
            pltpu.VMEM((3 * ROWS, ROWS), F32),
            pltpu.VMEM((length, LANES), F32),
            pltpu.VMEM((length, LANES), F32),
        ],
        compiler_params=params(),
        cost_estimate=NO_COST,
        name="unattend",
    )(spot, q, k, v, lse, dmixed, normed, gain, wq, wk, wv, cos, sin, seg_col, seg_row)


PAY = 832
QUARTER = PAY // RING
GAINS = 768 + EXPERTS


def pack_kernel(spot, normed, dqkv, grad_out, s0, s1, s2, s3, own, other):
    core = spot[3]
    sums = (s0[...] + s1[...]) + (s2[...] + s3[...])
    row = lax.broadcasted_iota(jnp.int32, (32, HALF), 0)
    for side, out in enumerate((own, other)):
        cols = pl.ds(pl.multiple_of(((core + side) % 2) * HALF, HALF), HALF)
        left = (core + side) % 2 == 0
        out[0:HALF, :] = dot_tn(normed[:, cols], dqkv[...]).astype(BF16)
        out[HALF:768, :] = grad_out[:, cols]
        here = jnp.where(left, sums[:, :HALF], sums[:, HALF:])
        out[768:GAINS, :] = here[0:EXPERTS, :].astype(BF16)
        out[GAINS:, :] = jnp.where(row == 0, here[EXPERTS : EXPERTS + 1, :], 0.0).astype(BF16)


def add_all(refs):
    total = refs[0][...].astype(F32)
    for ref in refs[1:]:
        total = total + ref[...].astype(F32)
    return total.astype(BF16)


def quarter_rows(index):
    return pl.ds(pl.multiple_of(index * QUARTER, 16), QUARTER)


def reduce_core_kernel(spot, own, got, g0, g1, g2, g3, p0, p1, p2, p3, total):
    total[...] = add_all((own, got))
    gain = (g0[...] + g1[...]) + (g2[...] + g3[...])
    row = lax.broadcasted_iota(jnp.int32, (32, HALF), 0)
    tail = jnp.where(row == 1, gain[0:1, :HALF], total[GAINS:, :].astype(F32))
    total[GAINS:, :] = jnp.where(row == 2, gain[0:1, HALF:], tail).astype(BF16)
    for d, piece in enumerate((p0, p1, p2, p3)):
        piece[...] = total[quarter_rows((spot[2] + d) % RING), :]


def sum_kernel(spot, a, b, c, d, out):
    out[...] = add_all((a, b, c, d))


def gather_x_kernel(spot, a, b, c, d, out):
    for d, piece in enumerate((a, b, c, d)):
        out[quarter_rows((spot[2] + d) % RING), :] = piece[...]


def unpack_kernel(spot, own, got, query, key, value, grad_out, router, gains):
    for side, half in enumerate((own, got)):
        at = pl.ds(pl.multiple_of(((spot[3] + side) % 2) * HALF, HALF), HALF)
        query[at, :] = half[0:HALF, : 2 * LANES].astype(F32)
        key[at, :] = half[0:HALF, 2 * LANES : 3 * LANES].astype(F32)
        value[at, :] = half[0:HALF, 3 * LANES :].astype(F32)
        grad_out[:, at] = half[HALF:768, :].astype(F32)
        router[:, at] = half[768:GAINS, :].astype(F32)
        gains[0:1, at] = half[GAINS:, :].astype(F32)[0:1, :]
    both = own[GAINS:, :].astype(F32)[0:8, :] + got[GAINS:, :].astype(F32)[0:8, :]
    gains[1:2, :HALF] = both[1:2, :]
    gains[1:2, HALF:] = both[2:3, :]


def small_call(kernel, spot, refs, shapes, scratch=None, flops=1_000_000, others=()):
    return pl.pallas_call(
        ignoring(kernel, 1 + len(refs), len(others)),
        out_shape=[jax.ShapeDtypeStruct(shape, dtype) for shape, dtype in shapes],
        in_specs=[SCALARS] + [WHOLE] * len(refs) + [ANYWHERE] * len(others),
        out_specs=[WHOLE] * len(shapes),
        scratch_shapes=[pltpu.VMEM(scratch, BF16)] if scratch else [],
        compiler_params=params(),
        cost_estimate=pl.CostEstimate(flops=flops, bytes_accessed=2_000_000, transcendentals=0),
    )(spot, *refs, *others)


def sum_over_ep(spot, normed, dqkv, grad_out, sums, gains, dn, output, moe_slots, make_hidden):
    own, other = small_call(
        pack_kernel, spot, (normed, dqkv, grad_out, *sums), [((PAY, HALF), BF16)] * 2, flops=0
    )
    got = push(other, 0, 0, 1)
    pieces = small_call(
        reduce_core_kernel, spot, (own, got, *gains), [((QUARTER, HALF), BF16)] * 4, (PAY, HALF)
    )
    dn, halves = scatter_tp(*after(dn, pieces[0]))
    pieces = [push(pieces[d], 0, d, 0) for d in range(RING)]
    quarter = [((QUARTER, HALF), BF16)]
    (line,) = small_call(sum_kernel, spot, pieces, quarter, others=(*halves, moe_slots))
    (line,) = small_call(sum_kernel, spot, [push(line, d, 0, 0) for d in range(RING)], quarter)
    pieces = [push(line, 0, -d, 0) for d in range(RING)]
    hidden = make_hidden(dn)
    (half,) = small_call(gather_x_kernel, spot, pieces, [((PAY, HALF), BF16)], others=(hidden, output))
    made = small_call(
        unpack_kernel,
        spot,
        (half, push(half, 0, 0, 1)),
        [
            ((WIDTH, 2 * LANES), F32),
            ((WIDTH, LANES), F32),
            ((WIDTH, LANES), F32),
            ((ROWS, WIDTH), F32),
            ((EXPERTS, WIDTH), F32),
            ((8, WIDTH), F32),
        ],
    )
    return *made, hidden


def hidden_kernel(a, b, c, hidden, gain, dmiddle, out):
    dn = a[...].astype(F32) + b[...].astype(F32) + c[...].astype(F32)
    x = hidden[...].astype(F32)
    inverse = lax.rsqrt(jnp.mean(x * x, axis=-1, keepdims=True) + NORM_EPS)
    plain = x * inverse
    scaled = dn * gain[...]
    along = jnp.mean(scaled * plain, axis=-1, keepdims=True)
    out[...] = dmiddle[...] + inverse * (scaled - plain * along)


def hidden_grad(dn, hidden, gain, dmiddle):
    return pl.pallas_call(
        hidden_kernel,
        out_shape=jax.ShapeDtypeStruct((ROWS, WIDTH), F32),
        in_specs=[WHOLE] * 6,
        out_specs=WHOLE,
        compiler_params=params(),
        cost_estimate=NO_COST,
        name="hidden_grad",
    )(*dn, hidden, gain, dmiddle)


def rope_tables(length):
    freqs = ROPE_BASE ** (-jnp.arange(HD // 2, dtype=F32) * 2.0 / HD)
    angles = jnp.arange(length, dtype=F32)[:, None] * freqs[None, :]
    cosine, sine = jnp.cos(angles), jnp.sin(angles)
    return jnp.concatenate([cosine] * 4, axis=1), jnp.concatenate([-sine, sine] * 2, axis=1)


def shards(
    hidden_in, segment_ids, expert_ids, slot_index, attn_gain, w_query, w_key, w_value, w_output,
    ffn_gain, w_router, w_gate_up, w_down, cotangent,
):
    length = RING * ROWS
    here, rank = lax.axis_index("ep"), lax.axis_index("tp")
    spot = jnp.stack([rank, here // 8, (here // 2) % 4, here % 2]).astype(jnp.int32)

    named = expert_ids[:, :, None] == jnp.arange(EXPERTS, dtype=jnp.int32)[None, None, :]
    slot_of = jnp.sum(jnp.where(named, slot_index[:, :, None] + 1, 0), axis=1) - 1
    chosen = (slot_of >= 0).astype(F32)
    table = slot_of.T.astype(F32)

    gain_one = attn_gain.astype(F32).reshape(1, WIDTH)
    gain_two = ffn_gain.astype(F32).reshape(1, WIDTH)
    cos, sin = rope_tables(length)
    seg_row = segment_ids
    seg_col = segment_ids.reshape(length, 1)

    group = [push_tp(hidden_in, -d) for d in range(RING)]
    cots = lax.all_gather(cotangent, "ep", axis=0, tiled=False, axis_index_groups=SAME_CORE)
    weights = jnp.concatenate([w_gate_up.reshape(WIDTH, 2 * HALF), w_down.reshape(HALF, WIDTH)], axis=0)
    made = attend(spot, group, gain_one, w_query, w_key, w_value, w_output, cos, sin, seg_col, seg_row)
    normed, q, k, v, mixed, lse = made[:6]
    branches = [push_tp(made[6 + d], d) for d in range(RING)]
    (weights,) = after((weights,), lse)
    weights = weights, push(weights, 0, 0, 1)
    middle, half_a, half_b, gates_t = route(hidden_in, branches, gain_two, w_router, chosen, table, weights[1])
    (pieces_a, pieces_b), slots_a, slots_b = dispatch(spot, half_a, half_b)
    first, second = Pieces(pieces_a[:4], pieces_b[:4]), Pieces(pieces_a[4:], pieces_b[4:])
    near = first.send_near()
    far = [first.send(0, 2)]
    held = after((pieces_b[2], pieces_b[6]), near[2], near[3])
    far += [first.send(1, 2, held[0]), second.send(1, 2, held[1])]
    held = after(second.near()[:2], *near)
    second.send(0, 1, held[0]), second.send(0, 3, held[1])
    held = after((*second.near()[2:], pieces_a[6]), *near, *far)
    second.send(1, 1, held[0]), second.send(1, 3, held[1]), second.send(0, 2, held[2])

    back_first, moe_slots, saved = expert(spot, 0, first, cots, weights[0])
    near = back_first.send_near()
    near.append(back_first.send(0, 2))
    back_second, moe_slots, saved_other = expert(spot, 1, second, cots, weights[1], moe_slots)
    held = after((back_first.made[1][2], *back_second.near()), *near)
    back_first.send(1, 2, held[0])
    near = back_second.send_near(held[1:])
    held = after((back_second.made[0][2], back_second.made[1][2], weight_grads(saved_other)), *near)
    back_second.send(0, 2, held[0])
    back_second.send(1, 2, held[1])
    grads_e = weight_grads(saved, push(held[2], 0, 0, 1))
    parts = to_owners(combine(slots_a, slots_b, back_first, back_second))

    dmiddle, dbranch, sums = unroute(
        spot, parts, gates_t, middle, cotangent, gain_two, w_router.T.astype(F32)
    )
    group_grad = gather_tp(dbranch)
    sums = [push_tp(sums, d) for d in range(RING)]

    (moe_slots,) = after((moe_slots,), *parts, grads_e)
    moe_slots = lax.all_to_all(
        moe_slots, "ep", split_axis=0, concat_axis=0, tiled=True, axis_index_groups=SAME_CORE
    )

    (summed_e,) = after((grads_e,), *group_grad[2])
    summed = lax.psum(summed_e, "tp")
    dmixed, grad_output = unmix(spot, group_grad, mixed, w_output, *sums[1:], summed_e)
    last = unattend(
        spot, q, k, v, lse, dmixed, normed, gain_one, w_query, w_key, w_value, cos, sin, seg_col, seg_row
    )
    gains = [push_tp(last[1], d) for d in range(RING)]
    output = finish(spot, table, moe_slots.reshape(CHIPS * PAIR, WIDTH), middle)
    grad_query, grad_key, grad_value, grad_output, grad_router, grad_gains, grad_hidden = sum_over_ep(
        spot, normed, last[0], grad_output, sums, gains, last[2:], output, moe_slots,
        lambda dn: hidden_grad(dn, hidden_in, gain_one, dmiddle),
    )
    grad_up, grad_down = cast_grads(summed)
    return (
        output,
        grad_hidden,
        grad_gains[1],
        grad_query,
        grad_key,
        grad_value,
        grad_output,
        grad_gains[0],
        grad_router.T,
        grad_up.reshape(1, WIDTH, 2, HALF),
        grad_down.reshape(1, HALF, WIDTH),
    )


def solution(mesh):
    placed = (
        P(("ep", "tp"), None),
        P("ep", None),
        P(("ep", "tp"), None),
        P(("ep", "tp"), None),
        P(),
        P(None, "tp"),
        P(None, "tp"),
        P(None, "tp"),
        P("tp", None),
        P(),
        P(),
        P("ep", None, None, None),
        P("ep", None, None),
        P(("ep", "tp"), None),
    )
    return jax.shard_map(
        shards,
        mesh=mesh,
        in_specs=placed,
        out_specs=(
            P(("ep", "tp"), None),
            P(("ep", "tp"), None),
            P(),
            P(None, "tp"),
            P(None, "tp"),
            P(None, "tp"),
            P("tp", None),
            P(),
            P(),
            P("ep", None, None, None),
            P("ep", None, None),
        ),
        check_vma=False,
    )
```

```python
import jax
import jax.numpy as jnp
from jax import lax
from jax.experimental import pallas as pl
from jax.experimental.pallas import tpu as pltpu
from jax.sharding import PartitionSpec as P

HD = 64
ATT_SCALE = 0.015625
RES_SCALE = 0.22
NORM_EPS = 1e-06
ROPE_BASE = 10000.0
NEG_FILL = -1e30
HIGHEST = lax.Precision.HIGHEST
F32 = jnp.float32
BF16 = jnp.bfloat16

ROWS = 256
WIDTH = 1024
HALF = 512
CAP = 96
EXPERTS = 32
RING = 4
HEADS = 4
LANES = 128
VMEM_BYTES = 58 * 1024 * 1024
WHOLE = pl.BlockSpec(memory_space=pltpu.VMEM)
SCALARS = pl.BlockSpec(memory_space=pltpu.SMEM)
ANYWHERE = pl.BlockSpec(memory_space=pl.ANY)


def params():
    return pltpu.CompilerParams(vmem_limit_bytes=VMEM_BYTES)


NO_COST = pl.CostEstimate(flops=0, bytes_accessed=0, transcendentals=0)


def dot(a, b, precision=None):
    return jnp.dot(a, b, preferred_element_type=F32, precision=precision)


def dot_nt(a, b):
    return lax.dot_general(a, b, (((1,), (1,)), ((), ())), preferred_element_type=F32)


def dot_tn(a, b):
    return lax.dot_general(a, b, (((0,), (0,)), ((), ())), preferred_element_type=F32)


def place(z, x, core):
    return ((z % RING) * RING + (x % RING)) * 2 + core


def push(value, dz, dx, dc):
    if (dz % RING, dx % RING, dc) == (0, 0, 0):
        return value
    pairs = [
        (place(z, x, c), place(z + dz, x + dx, c ^ dc))
        for z in range(RING)
        for x in range(RING)
        for c in range(2)
    ]
    return lax.ppermute(value, "ep", pairs)


def push_tp(value, dy):
    if dy % RING == 0:
        return value
    return lax.ppermute(value, "tp", [(y, (y + dy) % RING) for y in range(RING)])


def after(values, *others):
    count = len(values)
    return pl.pallas_call(
        lambda *refs: None,
        out_shape=[jax.ShapeDtypeStruct(v.shape, v.dtype) for v in values],
        in_specs=[ANYWHERE] * (count + len(others)),
        out_specs=[ANYWHERE] * count,
        input_output_aliases={i: i for i in range(count)},
        cost_estimate=NO_COST,
        name="after",
    )(*values, *others)


def gather_tp(rows):
    after_me, before_me = push_tp(rows, -1), push_tp(rows, 1)
    half = rows.shape[0] // 2
    across = push_tp(after_me[:half], -1), push_tp(before_me[half:], 1)
    return rows, after_me, across, before_me


def add_halves_kernel(one, three, first, rest, ahead, behind):
    half = first.shape[0]
    ahead[0:half, :] = (one[0:half, :].astype(F32) + first[...].astype(F32)).astype(BF16)
    ahead[half:, :] = one[half:, :]
    behind[0:half, :] = three[0:half, :]
    behind[half:, :] = (three[half:, :].astype(F32) + rest[...].astype(F32)).astype(BF16)


def scatter_tp(own, one, two, two_rest, three):
    first, rest = push_tp(two, 1), push_tp(two_rest, -1)
    ahead, behind = pl.pallas_call(
        add_halves_kernel,
        out_shape=[jax.ShapeDtypeStruct(one.shape, BF16)] * 2,
        in_specs=[WHOLE] * 4,
        out_specs=[WHOLE] * 2,
        compiler_params=params(),
        cost_estimate=NO_COST,
        name="add_halves",
    )(one, three, first, rest)
    return (own, push_tp(ahead, 1), push_tp(behind, -1)), (first, rest)


def ignoring(kernel, first, count):
    return lambda *refs: kernel(*refs[:first], *refs[first + count :])


def swap_halves(v):
    lane = lax.broadcasted_iota(jnp.int32, v.shape, 1)
    return jnp.where(lane % HD < HD // 2, pltpu.roll(v, LANES - HD // 2, 1), pltpu.roll(v, HD // 2, 1))


def block_at(index):
    return pl.ds(pl.multiple_of(index * ROWS, ROWS), ROWS)


def key_range(block):
    return max(0, block - 2) * ROWS, (block + 1) * ROWS


def mask_bias(block, seg_col, seg_row):
    lo, hi = key_range(block)
    key_pos = lo + lax.broadcasted_iota(jnp.int32, (hi - lo, ROWS), 0)
    query_pos = block * ROWS + lax.broadcasted_iota(jnp.int32, (hi - lo, ROWS), 1)
    same = seg_col[lo:hi, :] == seg_row[:, block * ROWS : (block + 1) * ROWS]
    return jnp.where(same & (key_pos <= query_pos), 0.0, NEG_FILL)


def attend_kernel(
    rank, x0, x1, x2, x3, gain, wq, wk, wv, wo, cos, sin, seg_col, seg_row,
    normed_far, q_far, k_far, v_far, mixed_far, lse, br0, br1, br2, br3,
    normed, q_out, k_out, v_out, mixed, branches, vt, bias, sems,
):
    me = rank[0]
    pairs = ((normed, normed_far), (q_out, q_far), (k_out, k_far), (v_out, v_far), (mixed, mixed_far))
    stores = [pltpu.make_async_copy(near, far, sems.at[i]) for i, (near, far) in enumerate(pairs)]
    lane = lax.broadcasted_iota(jnp.int32, (ROWS, LANES), 1)
    for d, x_ref in enumerate((x0, x1, x2, x3)):
        at = block_at((me + d) % RING)
        x = x_ref[...].astype(F32)
        inverse = lax.rsqrt(jnp.mean(x * x, axis=-1, keepdims=True) + NORM_EPS)
        low = (x * inverse * gain[...]).astype(BF16)
        normed[at, :] = low
        cos_here, sin_here = cos[at, :], sin[at, :]

        def rope(v):
            return v * cos_here + swap_halves(v) * sin_here

        query = dot(low, wq[...])
        for pair in range(2):
            q = rope(query[:, pair * LANES : (pair + 1) * LANES]) * ATT_SCALE
            other = pltpu.roll(q, HD, 1)
            keep = (lane < HD) if pair == 0 else (lane >= HD)
            first, second = (q, other) if pair == 0 else (other, q)
            at_head = 2 * pair * LANES
            q_out[at, at_head : at_head + LANES] = jnp.where(keep, first, 0.0).astype(BF16)
            q_out[at, at_head + LANES : at_head + 2 * LANES] = jnp.where(keep, second, 0.0).astype(BF16)
        k_out[at, :] = rope(dot(low, wk[...])).astype(BF16)
        v_out[at, :] = dot(low, wv[...]).astype(BF16)
    for copy in stores[:4]:
        copy.start()
    vt[...] = v_out[...].astype(F32).T.astype(BF16)
    for b in range(RING):
        lo, hi = key_range(b)
        rows = slice(b * ROWS, (b + 1) * ROWS)
        bias[0 : hi - lo, :] = mask_bias(b, seg_col, seg_row)
        outs = []
        for h in range(HEADS):
            q = q_out[rows, h * LANES : (h + 1) * LANES]
            scores = dot_nt(k_out[lo:hi, :], q) + bias[0 : hi - lo, :]
            top = jnp.max(scores, axis=0, keepdims=True)
            weights = jnp.exp(scores - top)
            total = jnp.sum(weights, axis=0, keepdims=True)
            out = dot(vt[:, lo:hi], weights.astype(BF16)) * (1.0 / total)
            outs.append(out.T)
            lse[h : h + 1, rows] = top + jnp.log(total)
        mixed[rows, 0:LANES] = jnp.where(lane < HD, outs[0], pltpu.roll(outs[1], HD, 1)).astype(BF16)
        mixed[rows, LANES:] = jnp.where(lane < HD, pltpu.roll(outs[2], HD, 1), outs[3]).astype(BF16)
        branches[b] = dot(mixed[rows, :], wo[...]).astype(BF16)
        for d, br in enumerate((br0, br1, br2, br3)):

            @pl.when((b - me + RING) % RING == d)
            def _():
                pltpu.make_async_copy(branches.at[b], br, sems.at[5 + b]).start()

    stores[4].start()
    for copy in stores:
        copy.wait()
    for b in range(RING):
        for d, br in enumerate((br0, br1, br2, br3)):

            @pl.when((b - me + RING) % RING == d)
            def _():
                pltpu.make_async_copy(branches.at[b], br, sems.at[5 + b]).wait()


def attend(rank, pieces, gain, wq, wk, wv, wo, cos, sin, seg_col, seg_row, *others):
    length = RING * ROWS
    return pl.pallas_call(
        ignoring(attend_kernel, 14, len(others)),
        out_shape=[
            jax.ShapeDtypeStruct((length, WIDTH), BF16),
            jax.ShapeDtypeStruct((length, HEADS * LANES), BF16),
            jax.ShapeDtypeStruct((length, LANES), BF16),
            jax.ShapeDtypeStruct((length, LANES), BF16),
            jax.ShapeDtypeStruct((length, HEADS * HD), BF16),
            jax.ShapeDtypeStruct((8, length), F32),
        ]
        + [jax.ShapeDtypeStruct((ROWS, WIDTH), BF16)] * RING,
        in_specs=[SCALARS] + [WHOLE] * 13 + [ANYWHERE] * len(others),
        out_specs=[ANYWHERE] * 5 + [WHOLE] + [ANYWHERE] * 4,
        scratch_shapes=[
            pltpu.VMEM((length, WIDTH), BF16),
            pltpu.VMEM((length, HEADS * LANES), BF16),
            pltpu.VMEM((length, LANES), BF16),
            pltpu.VMEM((length, LANES), BF16),
            pltpu.VMEM((length, HEADS * HD), BF16),
            pltpu.VMEM((RING, ROWS, WIDTH), BF16),
            pltpu.VMEM((LANES, length), BF16),
            pltpu.VMEM((3 * ROWS, ROWS), F32),
            pltpu.SemaphoreType.DMA((9,)),
        ],
        compiler_params=params(),
        cost_estimate=NO_COST,
        name="attend",
    )(rank, *pieces, gain, wq, wk, wv, wo, cos, sin, seg_col, seg_row, *others)


def high_low(v):
    high = v.astype(BF16)
    return jnp.concatenate([high, (v - high.astype(F32)).astype(BF16)], axis=1)


def route_kernel(x, b0, b1, b2, b3, gain, wr, chosen, table, middle, half_a, half_b, gates_t):
    branch = b0[...].astype(F32) + b1[...].astype(F32) + b2[...].astype(F32) + b3[...].astype(F32)
    mid = x[...].astype(F32) + RES_SCALE * branch
    middle[...] = mid
    inverse = lax.rsqrt(jnp.mean(mid * mid, axis=-1, keepdims=True) + NORM_EPS)
    routed = (mid * inverse * gain[...]).astype(BF16)
    half_b[0:ROWS, :] = routed[:, HALF:]
    logits = jnp.where(chosen[...] > 0.0, dot(routed, wr[...]), NEG_FILL)
    weights = jnp.exp(logits - jnp.max(logits, axis=-1, keepdims=True))
    gates = (weights / jnp.sum(weights, axis=-1, keepdims=True)).T
    gates_t[...] = gates
    half_a[0:ROWS, :] = routed[:, :HALF]
    half_a[ROWS : ROWS + EXPERTS, :] = high_low(gates)
    slots = jnp.concatenate([table[...], jnp.zeros_like(gates)], axis=1).astype(BF16)
    half_a[ROWS + EXPERTS :, :] = slots
    half_b[ROWS:, :] = slots


def route(x, branches, gain, wr, chosen, table, *others):
    return pl.pallas_call(
        ignoring(route_kernel, 9, len(others)),
        out_shape=[
            jax.ShapeDtypeStruct((ROWS, WIDTH), F32),
            jax.ShapeDtypeStruct((ROWS + 2 * EXPERTS, HALF), BF16),
            jax.ShapeDtypeStruct((ROWS + EXPERTS, HALF), BF16),
            jax.ShapeDtypeStruct((EXPERTS, ROWS), F32),
        ],
        in_specs=[WHOLE] * 9 + [ANYWHERE] * len(others),
        out_specs=[WHOLE] * 4,
        compiler_params=params(),
        cost_estimate=pl.CostEstimate(flops=20_000_000, bytes_accessed=5_000_000, transcendentals=8192),
        name="route",
    )(x, *branches, gain, wr, chosen, table, *others)


PIECE = RING * CAP
EXTRA = 16


def line_row(d, p, e):
    return p * 8 + e * 4 + d


def slot_matrix(row):
    slot = lax.broadcasted_iota(jnp.int32, (CAP, ROWS), 0).astype(F32)
    return jnp.where(slot == row, 1.0, 0.0)


def line_matrix(slots, d):
    rows = [line_row(d, p, e) for p in range(RING) for e in range(2)]
    return jnp.concatenate([slot_matrix(slots[r : r + 1, :]).astype(BF16) for r in rows], axis=0)


def expert_row(spot, half, d, p, e):
    z, x, core = spot[1], spot[2], spot[3]
    if half == 0:
        x = (x + p) % RING
    else:
        z = (z + p) % RING
    return (z * RING + x) * 2 + (core + e) % 2


def fill_pieces(slots, rows, pieces):
    for d in range(RING):
        filled = dot(line_matrix(slots, d), rows[d][0:ROWS, :]).astype(BF16)
        for p in range(RING):
            for e in range(2):
                pieces[e * 4 + p][d * CAP : (d + 1) * CAP, :] = filled[(p * 2 + e) * CAP : (p * 2 + e + 1) * CAP, :]


def pick_rows(spot, half, blocks, first, table, picked):
    for d in range(RING):
        table[...] = blocks[d][first : first + EXPERTS, :].astype(F32)
        for p in range(RING):
            for e in range(2):
                r = line_row(d, p, e)
                picked[r : r + 1, :] = table[pl.ds(expert_row(spot, half, d, p, e), 1), :]


def dispatch_kernel(spot, *refs):
    blocks, pieces, slots, (table, gates, picked) = refs[:8], (refs[8:16], refs[16:24]), refs[24:26], refs[26:]
    pick_rows(spot, 0, blocks[:4], ROWS, table, gates)
    for half in range(2):
        mine = blocks[4 * half : 4 * half + 4]
        pick_rows(spot, half, mine, ROWS + EXPERTS * (1 - half), table, picked)
        slots[half][...] = picked[:, :ROWS]
        fill_pieces(slots[half], mine, pieces[half])
        if half == 0:
            for p in range(RING):
                for e in range(2):
                    at = slice(p * 8 + e * 4, p * 8 + e * 4 + 4)
                    extra = jnp.concatenate([gates[at, :], picked[at, :], jnp.zeros((8, HALF), F32)], axis=0)
                    pieces[0][e * 4 + p][PIECE:, :] = extra.astype(BF16)


def combine_kernel(slots_a, slots_b, *refs):
    everyone, (second, sems) = range(RING), refs[24:]
    fetches = [pltpu.make_async_copy(refs[8 + i], second.at[i], sems.at[i]) for i in range(8)]
    for copy in fetches:
        copy.start()
    for half, slots in enumerate((slots_a, slots_b)):
        if half == 1:
            for copy in fetches:
                copy.wait()
        pieces = refs[:8] if half == 0 else [second.at[i] for i in range(8)]
        rows = refs[16 + 4 * half : 20 + 4 * half]
        for d in everyone:
            filled = [pieces[e * 4 + p][d * CAP : (d + 1) * CAP, :] for p in everyone for e in range(2)]
            filled = jnp.concatenate(filled, axis=0)
            rows[d][0:ROWS, :] = dot_tn(line_matrix(slots, d), filled).astype(BF16)
        if half == 0:
            tables = [pieces[i][PIECE:, :].astype(F32) for i in range(8)]
            for d in everyone:
                picked = [tables[e * 4 + p][d : d + 1, :] for p in everyone for e in range(2)]
                extra = jnp.concatenate(picked + [jnp.zeros((8, HALF), F32)], axis=0)
                rows[d][ROWS:, :] = extra.astype(BF16)


SLOT_COST = pl.CostEstimate(flops=1_000_000_000, bytes_accessed=5_000_000, transcendentals=0)
TABLE = pltpu.VMEM((EXPERTS, HALF), F32)


def shape_of(rows, dtype=BF16):
    return jax.ShapeDtypeStruct((rows, HALF), dtype)


def spread_rows(half_a, half_b):
    return [push(half_a, -d, 0, 0) for d in range(RING)] + [push(half_b, 0, -d, 0) for d in range(RING)]


def dispatch(spot, half_a, half_b):
    made = pl.pallas_call(
        dispatch_kernel,
        out_shape=[shape_of(PIECE + EXTRA)] * 8
        + [shape_of(PIECE)] * 8
        + [jax.ShapeDtypeStruct((EXPERTS, ROWS), F32)] * 2,
        in_specs=[SCALARS] + [WHOLE] * 8,
        out_specs=[WHOLE] * 18,
        scratch_shapes=[TABLE] * 3,
        compiler_params=params(),
        cost_estimate=SLOT_COST,
        name="dispatch",
    )(spot, *spread_rows(half_a, half_b))
    return (made[:8], made[8:16]), made[16], made[17]


class Pieces:
    def __init__(self, half_a, half_b):
        self.made = list(half_a), list(half_b)
        self.got = [half_a[0], None, None, None], [half_b[0], None, None, None]

    def send(self, half, p, held=None):
        piece = self.made[half][p] if held is None else held
        self.got[half][-p % RING] = push(piece, 0, p, 0) if half == 0 else push(piece, p, 0, 0)
        return self.got[half][-p % RING]

    def send_near(self, held=(None,) * 4):
        places = (0, 1), (0, 3), (1, 1), (1, 3)
        return [self.send(half, p, piece) for (half, p), piece in zip(places, held)]

    def near(self):
        return self.made[0][1], self.made[0][3], self.made[1][1], self.made[1][3]


def combine(slots_a, slots_b, first, second, *others):
    pieces = [*first.got[0], *second.got[0], *first.got[1], *second.got[1]]
    return pl.pallas_call(
        ignoring(combine_kernel, 18, len(others)),
        out_shape=[shape_of(ROWS + EXTRA)] * RING + [shape_of(ROWS)] * RING,
        in_specs=[WHOLE] * 10 + [ANYWHERE] * (8 + len(others)),
        out_specs=[WHOLE] * 8,
        scratch_shapes=[pltpu.VMEM((8, PIECE, HALF), BF16), pltpu.SemaphoreType.DMA((8,))],
        compiler_params=params(),
        cost_estimate=pl.CostEstimate(flops=60_000_000_000, bytes_accessed=0, transcendentals=0),
        name="combine",
    )(slots_a, slots_b, *pieces, *others)


def to_owners(partial):
    got = [None] * 8
    for d in range(RING):
        got[-d % RING] = push(partial[d], d, 0, 0)
        got[4 + -d % RING] = push(partial[4 + d], 0, d, 0)
    return got


CHIPS = RING * RING
PAIR = 2 * CAP


def chips_matrix(spot, table, step):
    rows = []
    for i in range(RING):
        for e in range(2):
            expert = (step * RING + i) * 2 + (spot[3] + e) % 2
            rows.append(slot_matrix(table[pl.ds(expert, 1), :]).astype(BF16))
    return jnp.concatenate(rows, axis=0)


def finish_kernel(spot, table, slots, middle, out, total):
    step = pl.program_id(0)
    term = dot_tn(chips_matrix(spot, table, step), slots[...])

    @pl.when(step == 0)
    def _():
        total[...] = term

    @pl.when(step > 0)
    def _():
        total[...] += term

    @pl.when(step == RING - 1)
    def _():
        out[...] = (middle[...] + RES_SCALE * total[...]).astype(BF16)


def finish(spot, table, slots, middle):
    return pl.pallas_call(
        finish_kernel,
        grid=(RING,),
        out_shape=jax.ShapeDtypeStruct((ROWS, WIDTH), BF16),
        in_specs=[SCALARS, WHOLE, pl.BlockSpec((RING * PAIR, WIDTH), lambda s: (s, 0)), WHOLE],
        out_specs=pl.BlockSpec((ROWS, WIDTH), lambda s: (0, 0)),
        scratch_shapes=[pltpu.VMEM((ROWS, WIDTH), F32)],
        compiler_params=params(),
        cost_estimate=SLOT_COST,
        name="finish",
    )(spot, table, slots, middle)


SAME_CORE = [list(range(core, EXPERTS, 2)) for core in range(2)]


STEPS = RING
STEP_ROWS = RING * CAP


def expert_kernel(e, spot, *refs):
    ra, rb, cot, weights = refs[:4], refs[4:8], refs[8], refs[9]
    refs = refs[10 + e :]
    qa, qb, moe, (disp_out, dgu_out, inner_out, dex_out) = refs[:4], refs[4:8], refs[8], refs[9:13]
    wgu, wd, rows_in, cot_in, extra_in, back_out, moe_out, extra_out, weight_sem, in_sem, out_sem = refs[13:]
    step = pl.program_id(0)
    loads = [
        pltpu.make_async_copy(weights.at[pl.ds(0, WIDTH)], wgu, weight_sem.at[0]),
        pltpu.make_async_copy(weights.at[pl.ds(WIDTH, HALF)], wd, weight_sem.at[1]),
    ]

    def places(dx, half_a, half_b, halves, extra):
        slot = dx % 2
        ends = [
            (half_a[dx].at[pl.ds(0, PIECE)], halves.at[slot, :, pl.ds(0, HALF)]),
            (half_a[dx].at[pl.ds(PIECE, EXTRA)], extra.at[slot]),
        ]
        for dz in range(RING):
            ends.append((half_b[dz].at[pl.ds(dx * CAP, CAP)], halves.at[slot, pl.ds(dz * CAP, CAP), pl.ds(HALF, HALF)]))
        return ends

    def chip(dz, dx):
        return ((spot[1] + dz) % RING) * RING + (spot[2] + dx) % RING

    def fetches(dx):
        ends = places(dx, ra, rb, rows_in, extra_in)
        for dz in range(RING):
            ends.append((cot.at[chip(dz, dx)], cot_in.at[dx % 2, pl.ds(dz * ROWS, ROWS)]))
        return [pltpu.make_async_copy(far, near, in_sem.at[dx % 2, n]) for n, (far, near) in enumerate(ends)]

    def stores(dx):
        ends = places(dx, qa, qb, back_out, extra_out)
        for dz in range(RING):
            ends.append((moe.at[chip(dz, dx), pl.ds(e * CAP, CAP)], moe_out.at[dx % 2, pl.ds(dz * CAP, CAP)]))
        return [pltpu.make_async_copy(near, far, out_sem.at[dx % 2, n]) for n, (far, near) in enumerate(ends)]

    for j in range(STEPS):

        @pl.when(step == j)
        def _():
            if j == 0:
                for copy in fetches(0) + loads:
                    copy.start()
            if j + 1 < STEPS:
                for copy in fetches(j + 1):
                    copy.start()
            for copy in fetches(j):
                copy.wait()
            if j == 0:
                for copy in loads:
                    copy.wait()
            if j >= 2:
                for copy in stores(j - 2):
                    copy.wait()

    slot = step % 2
    extra = extra_in[slot].astype(F32)
    gates = extra[0:4, :ROWS] + extra[0:4, ROWS:]
    fills = [slot_matrix(extra[4 + dz : 5 + dz, :ROWS]) for dz in range(RING)]
    gate_slot = jnp.concatenate(
        [jnp.sum(fills[dz] * gates[dz : dz + 1, :], axis=1, keepdims=True) for dz in range(RING)], axis=0
    )
    rows = rows_in[slot]
    disp_out[...] = rows
    gate_up = dot(rows, wgu[...])
    dmoe = [
        dot(fills[dz].astype(BF16), cot_in[slot, dz * ROWS : (dz + 1) * ROWS, :]) for dz in range(RING)
    ]
    dmoe = RES_SCALE * jnp.concatenate(dmoe, axis=0)
    dex = (gate_slot * dmoe).astype(BF16)
    dex_out[...] = dex
    dinner = dot_nt(dex, wd[...])
    gate, up = gate_up[:, :HALF], gate_up[:, HALF:]
    sigmoid = jax.nn.sigmoid(gate)
    silu = gate * sigmoid
    inner = (silu * up).astype(BF16)
    inner_out[...] = inner
    made = dot(inner, wd[...]).astype(BF16).astype(F32)
    dgate = dinner * up * sigmoid * (1.0 + gate * (1.0 - sigmoid))
    dgu = jnp.concatenate([dgate.astype(BF16), (dinner * silu).astype(BF16)], axis=1)
    dgu_out[...] = dgu
    back_out[slot] = dot_nt(dgu, wgu[...]).astype(BF16)
    moe_out[slot] = (gate_slot * made).astype(BF16)
    dgate_slot = jnp.sum(dmoe * made, axis=1, keepdims=True)
    dgates = [
        jnp.sum(fills[dz] * dgate_slot[dz * CAP : (dz + 1) * CAP, :], axis=0, keepdims=True) for dz in range(RING)
    ]
    dgates = jnp.concatenate(dgates + [jnp.zeros((EXTRA - RING, ROWS), F32)], axis=0)
    extra_out[slot] = high_low(dgates)

    for j in range(STEPS):

        @pl.when(step == j)
        def _():
            for copy in stores(j):
                copy.start()
            if j == STEPS - 1:
                for copy in stores(j - 1) + stores(j):
                    copy.wait()


def expert(spot, e, pieces, cots, weights, *moe):
    total = STEPS * STEP_ROWS
    wide = pl.BlockSpec((STEP_ROWS, WIDTH), lambda s: (s, 0))
    narrow = pl.BlockSpec((STEP_ROWS, HALF), lambda s: (s, 0))
    buf, small = pltpu.VMEM((2, STEP_ROWS, WIDTH), BF16), pltpu.VMEM((2, EXTRA, HALF), BF16)
    made = pl.pallas_call(
        lambda *refs: expert_kernel(e, *refs),
        grid=(STEPS,),
        out_shape=[shape_of(PIECE + EXTRA)] * RING
        + [shape_of(PIECE)] * RING
        + [
            jax.ShapeDtypeStruct((CHIPS, PAIR, WIDTH), BF16),
            jax.ShapeDtypeStruct((total, WIDTH), BF16),
            jax.ShapeDtypeStruct((total, WIDTH), BF16),
            jax.ShapeDtypeStruct((total, HALF), BF16),
            jax.ShapeDtypeStruct((total, WIDTH), BF16),
        ],
        in_specs=[SCALARS] + [ANYWHERE] * (10 + e),
        out_specs=[ANYWHERE] * 9 + [wide, wide, narrow, wide],
        scratch_shapes=[
            pltpu.VMEM((WIDTH, WIDTH), BF16),
            pltpu.VMEM((HALF, WIDTH), BF16),
            buf, pltpu.VMEM((2, RING * ROWS, WIDTH), BF16), small, buf, buf, small,
            pltpu.SemaphoreType.DMA((2,)),
            pltpu.SemaphoreType.DMA((2, 10)),
            pltpu.SemaphoreType.DMA((2, 10)),
        ],
        input_output_aliases={11: 8} if e else {},
        compiler_params=params(),
        cost_estimate=NO_COST,
        name="expert",
    )(spot, *pieces.got[0], *pieces.got[1], cots, weights, *moe)
    return Pieces(made[:4], made[4:8]), made[8], made[9:]


def weight_grads_kernel(with_other, *refs):
    disp, dgu, inner, dex = refs[:4]
    other, out = refs[4] if with_other else None, refs[4 + with_other]
    disp_in, dgu_in, inner_in, dex_in, made, other_in, sems, out_sems = refs[5 + with_other :]
    pairs = [(disp, disp_in), (dgu, dgu_in), (inner, inner_in), (dex, dex_in)]
    if with_other:
        pairs.append((other, other_in))
    fetches = [pltpu.make_async_copy(far, near, sems.at[i]) for i, (far, near) in enumerate(pairs)]
    stores = [
        pltpu.make_async_copy(made.at[pl.ds(i * HALF, HALF)], out.at[pl.ds(i * HALF, HALF)], out_sems.at[i])
        for i in range(3)
    ]
    for copy in fetches:
        copy.start()
    for i, left in enumerate((disp_in, disp_in, inner_in)):
        if i == 0:
            fetches[0].wait()
            fetches[1].wait()
        if i == 2:
            fetches[2].wait()
            fetches[3].wait()
        if with_other and i == 0:
            fetches[4].wait()
        cols = slice(i * HALF, (i + 1) * HALF) if i < 2 else slice(None)
        grad = dot_tn(left[:, cols], (dgu_in if i < 2 else dex_in)[...])
        if with_other:
            grad = grad.astype(BF16).astype(F32) + other_in[i * HALF : (i + 1) * HALF, :].astype(F32)
        made[i * HALF : (i + 1) * HALF, :] = grad.astype(BF16)
        stores[i].start()
    for copy in stores:
        copy.wait()


def weight_grads(saved, *other):
    wide, narrow = pltpu.VMEM((4 * STEP_ROWS, WIDTH), BF16), pltpu.VMEM((4 * STEP_ROWS, HALF), BF16)
    grads = pltpu.VMEM((WIDTH + HALF, WIDTH), BF16)
    return pl.pallas_call(
        lambda *refs: weight_grads_kernel(len(other), *refs),
        out_shape=jax.ShapeDtypeStruct((WIDTH + HALF, WIDTH), BF16),
        in_specs=[ANYWHERE] * (4 + len(other)),
        out_specs=ANYWHERE,
        scratch_shapes=[
            wide, wide, narrow, wide, grads, grads, pltpu.SemaphoreType.DMA((5,)), pltpu.SemaphoreType.DMA((3,)),
        ],
        compiler_params=params(),
        cost_estimate=NO_COST,
        name="weight_grads",
    )(*saved, *other)


def cast_grads_kernel(grads, up, down):
    for i in range(2):
        up[:, i, :] = grads[0:WIDTH, i * HALF : (i + 1) * HALF].astype(F32)
    down[...] = grads[WIDTH:, :].astype(F32)


def cast_grads(grads, *others):
    return pl.pallas_call(
        ignoring(cast_grads_kernel, 1, len(others)),
        out_shape=[
            jax.ShapeDtypeStruct((WIDTH, 2, HALF), F32),
            jax.ShapeDtypeStruct((HALF, WIDTH), F32),
        ],
        in_specs=[WHOLE] + [ANYWHERE] * len(others),
        out_specs=[WHOLE] * 2,
        compiler_params=params(),
        cost_estimate=NO_COST,
        name="cast_grads",
    )(grads, *others)


def unroute_kernel(spot, *refs):
    parts, (gates_t, middle, cot, gain, wr_t, dmiddle, dbranch, sums, gates, dlogits) = refs[:8], refs[8:]

    def four(pieces):
        a, b, c, d = (piece[0:ROWS, :].astype(F32) for piece in pieces)
        return (a + b) + (c + d)

    order = [
        (((spot[1] + dz) % RING) * RING + (spot[2] + dx) % RING) * 2 + (spot[3] + e) % 2
        for dz in range(RING)
        for dx in range(RING)
        for e in range(2)
    ]
    for i, at in enumerate(order):
        gates[i : i + 1, :] = gates_t[pl.ds(at, 1), :]
    tables = [part[ROWS:, :].astype(F32) for part in parts[:4]]
    dgates = jnp.concatenate([t[0:8, :ROWS] + t[0:8, ROWS:] for t in tables], axis=0)
    made = gates[...] * (dgates - jnp.sum(gates[...] * dgates, axis=0, keepdims=True))
    for i, at in enumerate(order):
        dlogits[pl.ds(at, 1), :] = made[i : i + 1, :]
    drouted = jnp.concatenate([four(parts[:4]), four(parts[4:])], axis=1)
    drouted = drouted + dot(dlogits[...].T, wr_t[...], HIGHEST)
    mid = middle[...]
    inverse = lax.rsqrt(jnp.mean(mid * mid, axis=-1, keepdims=True) + NORM_EPS)
    plain = mid * inverse
    routed = (plain * gain[...]).astype(BF16).astype(F32)
    sums[0:EXPERTS, :] = dot(dlogits[...], routed, HIGHEST)
    sums[EXPERTS : EXPERTS + 8, :] = jnp.broadcast_to(jnp.sum(drouted * plain, axis=0, keepdims=True), (8, WIDTH))
    scaled = drouted * gain[...]
    along = jnp.mean(scaled * plain, axis=-1, keepdims=True)
    total = cot[...].astype(F32) + inverse * (scaled - plain * along)
    dmiddle[...] = total
    dbranch[...] = (RES_SCALE * total).astype(BF16)


def unroute(spot, parts, gates_t, middle, cot, gain, wr_t, *others):
    return pl.pallas_call(
        ignoring(unroute_kernel, 14, len(others)),
        out_shape=[
            jax.ShapeDtypeStruct((ROWS, WIDTH), F32),
            jax.ShapeDtypeStruct((ROWS, WIDTH), BF16),
            jax.ShapeDtypeStruct((EXPERTS + 8, WIDTH), F32),
        ],
        in_specs=[SCALARS] + [WHOLE] * 13 + [ANYWHERE] * len(others),
        out_specs=[WHOLE] * 3,
        scratch_shapes=[pltpu.VMEM((EXPERTS, ROWS), F32), pltpu.VMEM((EXPERTS, ROWS), F32)],
        compiler_params=params(),
        cost_estimate=NO_COST,
        name="unroute",
    )(spot, *parts, gates_t, middle, cot, gain, wr_t, *others)


def unmix_kernel(rank, d0, d1, d2, d2_rest, d3, mixed, wo, dmixed, grad_out):
    me = rank[0]
    lane = lax.broadcasted_iota(jnp.int32, (ROWS, LANES), 1)
    for d, ref in enumerate((d0, d1, d2, d3)):
        at = block_at((me + d) % RING)
        grad = jnp.concatenate([d2[...], d2_rest[...]], axis=0) if d == 2 else ref[...]
        low = dot_nt(grad, wo[...])
        for pair in range(2):
            both = low[:, pair * LANES : (pair + 1) * LANES]
            other = pltpu.roll(both, HD, 1)
            keep = (lane < HD) if pair == 0 else (lane >= HD)
            first, second = (both, other) if pair == 0 else (other, both)
            at_head = 2 * pair * LANES
            dmixed[at, at_head : at_head + LANES] = jnp.where(keep, first, 0.0).astype(BF16)
            dmixed[at, at_head + LANES : at_head + 2 * LANES] = jnp.where(keep, second, 0.0).astype(BF16)
        term = dot_tn(mixed[at, :], grad)
        total = term if d == 0 else total + term
    grad_out[...] = total.astype(BF16)


def unmix(rank, pieces, mixed, wo, *others):
    length = RING * ROWS
    return pl.pallas_call(
        ignoring(unmix_kernel, 8, len(others)),
        out_shape=[
            jax.ShapeDtypeStruct((length, HEADS * LANES), BF16),
            jax.ShapeDtypeStruct((HEADS * HD, WIDTH), BF16),
        ],
        in_specs=[SCALARS] + [WHOLE] * 7 + [ANYWHERE] * len(others),
        out_specs=[WHOLE] * 2,
        compiler_params=params(),
        cost_estimate=pl.CostEstimate(flops=1_100_000_000, bytes_accessed=5_000_000, transcendentals=0),
        name="unmix",
    )(rank, pieces[0], pieces[1], *pieces[2], pieces[3], mixed, wo, *others)


def unattend_kernel(
    spot, q_in, k_in, v_in, lse, dmixed, normed, gain, wq, wk, wv, cos, sin, seg_col, seg_row,
    dqkv, dgain, dn0, dn1, dn2, dn2_rest, dn3, kt, bias, dk, dv,
):
    me = spot[0]
    lane = lax.broadcasted_iota(jnp.int32, (ROWS, LANES), 1)
    kt[...] = k_in[...].astype(F32).T.astype(BF16)
    dk[...] = jnp.zeros_like(dk)
    dv[...] = jnp.zeros_like(dv)

    def unrope(v, rows):
        return v * cos[rows, :] - swap_halves(v) * sin[rows, :]

    for b in range(RING):
        lo, hi = key_range(b)
        rows = slice(b * ROWS, (b + 1) * ROWS)
        bias[0 : hi - lo, :] = mask_bias(b, seg_col, seg_row)
        dqs = []
        for h in range(HEADS):
            cols = slice(h * LANES, (h + 1) * LANES)
            q, do = q_in[rows, cols], dmixed[rows, cols]
            scores = dot_nt(k_in[lo:hi, :], q) + bias[0 : hi - lo, :]
            probs = jnp.exp(scores - lse[h : h + 1, rows])
            dprobs = dot_nt(v_in[lo:hi, :], do)
            delta = jnp.sum(probs * dprobs, axis=0, keepdims=True)
            dscores = (probs * (dprobs - delta)).astype(BF16)
            dv[lo:hi, :] += dot(probs.astype(BF16), do)
            dk[lo:hi, :] += dot(dscores, q)
            dqs.append(dot(kt[:, lo:hi], dscores).T * ATT_SCALE)
        first = jnp.where(lane < HD, dqs[0], pltpu.roll(dqs[1], HD, 1))
        second = jnp.where(lane < HD, pltpu.roll(dqs[2], HD, 1), dqs[3])
        dqkv[rows, 0:LANES] = unrope(first, rows).astype(BF16)
        dqkv[rows, LANES : 2 * LANES] = unrope(second, rows).astype(BF16)
    for b in range(RING):
        rows = slice(b * ROWS, (b + 1) * ROWS)
        dqkv[rows, 2 * LANES : 3 * LANES] = unrope(dk[rows, :], rows).astype(BF16)
        dqkv[rows, 3 * LANES :] = dv[rows, :].astype(BF16)
        dn = dot_nt(dqkv[rows, : 2 * LANES], wq[...])
        dn = dn + dot_nt(dqkv[rows, 2 * LANES : 3 * LANES], wk[...])
        dn = dn + dot_nt(dqkv[rows, 3 * LANES :], wv[...])
        term = jnp.sum(dn * normed[rows, :].astype(F32), axis=0, keepdims=True)
        gain_sum = term if b == 0 else gain_sum + term
        dn = dn.astype(BF16)
        relative = (b - me + RING) % RING
        for d, ref in ((0, dn0), (1, dn1), (3, dn3)):

            @pl.when(relative == d)
            def _():
                ref[...] = dn

        @pl.when(relative == 2)
        def _():
            dn2[...] = dn[: ROWS // 2, :]
            dn2_rest[...] = dn[ROWS // 2 :, :]

    dgain[...] = jnp.broadcast_to(gain_sum / gain[...], (8, WIDTH))


def unattend(spot, q, k, v, lse, dmixed, normed, gain, wq, wk, wv, cos, sin, seg_col, seg_row):
    length = RING * ROWS
    return pl.pallas_call(
        unattend_kernel,
        out_shape=[
            jax.ShapeDtypeStruct((length, HALF), BF16),
            jax.ShapeDtypeStruct((8, WIDTH), F32),
        ]
        + [jax.ShapeDtypeStruct((rows, WIDTH), BF16) for rows in (ROWS, ROWS, ROWS // 2, ROWS // 2, ROWS)],
        in_specs=[SCALARS] + [WHOLE] * 14,
        out_specs=[WHOLE] * 7,
        scratch_shapes=[
            pltpu.VMEM((LANES, length), BF16),
            pltpu.VMEM((3 * ROWS, ROWS), F32),
            pltpu.VMEM((length, LANES), F32),
            pltpu.VMEM((length, LANES), F32),
        ],
        compiler_params=params(),
        cost_estimate=NO_COST,
        name="unattend",
    )(spot, q, k, v, lse, dmixed, normed, gain, wq, wk, wv, cos, sin, seg_col, seg_row)


PAY = 832
QUARTER = PAY // RING
GAINS = 768 + EXPERTS


def pack_kernel(spot, normed, dqkv, grad_out, s0, s1, s2, s3, own, other):
    core = spot[3]
    sums = (s0[...] + s1[...]) + (s2[...] + s3[...])
    row = lax.broadcasted_iota(jnp.int32, (32, HALF), 0)
    for side, out in enumerate((own, other)):
        cols = pl.ds(pl.multiple_of(((core + side) % 2) * HALF, HALF), HALF)
        left = (core + side) % 2 == 0
        out[0:HALF, :] = dot_tn(normed[:, cols], dqkv[...]).astype(BF16)
        out[HALF:768, :] = grad_out[:, cols]
        here = jnp.where(left, sums[:, :HALF], sums[:, HALF:])
        out[768:GAINS, :] = here[0:EXPERTS, :].astype(BF16)
        out[GAINS:, :] = jnp.where(row == 0, here[EXPERTS : EXPERTS + 1, :], 0.0).astype(BF16)


def add_all(refs):
    total = refs[0][...].astype(F32)
    for ref in refs[1:]:
        total = total + ref[...].astype(F32)
    return total.astype(BF16)


def quarter_rows(index):
    return pl.ds(pl.multiple_of(index * QUARTER, 16), QUARTER)


def reduce_core_kernel(spot, own, got, g0, g1, g2, g3, p0, p1, p2, p3, total):
    total[...] = add_all((own, got))
    gain = (g0[...] + g1[...]) + (g2[...] + g3[...])
    row = lax.broadcasted_iota(jnp.int32, (32, HALF), 0)
    tail = jnp.where(row == 1, gain[0:1, :HALF], total[GAINS:, :].astype(F32))
    total[GAINS:, :] = jnp.where(row == 2, gain[0:1, HALF:], tail).astype(BF16)
    for d, piece in enumerate((p0, p1, p2, p3)):
        piece[...] = total[quarter_rows((spot[2] + d) % RING), :]


def sum_kernel(spot, a, b, c, d, out):
    out[...] = add_all((a, b, c, d))


def gather_x_kernel(spot, a, b, c, d, out):
    for d, piece in enumerate((a, b, c, d)):
        out[quarter_rows((spot[2] + d) % RING), :] = piece[...]


def unpack_kernel(spot, own, got, query, key, value, grad_out, router, gains):
    for side, half in enumerate((own, got)):
        at = pl.ds(pl.multiple_of(((spot[3] + side) % 2) * HALF, HALF), HALF)
        query[at, :] = half[0:HALF, : 2 * LANES].astype(F32)
        key[at, :] = half[0:HALF, 2 * LANES : 3 * LANES].astype(F32)
        value[at, :] = half[0:HALF, 3 * LANES :].astype(F32)
        grad_out[:, at] = half[HALF:768, :].astype(F32)
        router[:, at] = half[768:GAINS, :].astype(F32)
        gains[0:1, at] = half[GAINS:, :].astype(F32)[0:1, :]
    both = own[GAINS:, :].astype(F32)[0:8, :] + got[GAINS:, :].astype(F32)[0:8, :]
    gains[1:2, :HALF] = both[1:2, :]
    gains[1:2, HALF:] = both[2:3, :]


def small_call(kernel, spot, refs, shapes, scratch=None, flops=1_000_000, others=()):
    return pl.pallas_call(
        ignoring(kernel, 1 + len(refs), len(others)),
        out_shape=[jax.ShapeDtypeStruct(shape, dtype) for shape, dtype in shapes],
        in_specs=[SCALARS] + [WHOLE] * len(refs) + [ANYWHERE] * len(others),
        out_specs=[WHOLE] * len(shapes),
        scratch_shapes=[pltpu.VMEM(scratch, BF16)] if scratch else [],
        compiler_params=params(),
        cost_estimate=pl.CostEstimate(flops=flops, bytes_accessed=2_000_000, transcendentals=0),
    )(spot, *refs, *others)


def sum_over_ep(spot, normed, dqkv, grad_out, sums, gains, dn, output, moe_slots, make_hidden):
    own, other = small_call(
        pack_kernel, spot, (normed, dqkv, grad_out, *sums), [((PAY, HALF), BF16)] * 2, flops=0
    )
    got = push(other, 0, 0, 1)
    pieces = small_call(
        reduce_core_kernel, spot, (own, got, *gains), [((QUARTER, HALF), BF16)] * 4, (PAY, HALF)
    )
    dn, halves = scatter_tp(*after(dn, pieces[0]))
    pieces = [push(pieces[d], 0, d, 0) for d in range(RING)]
    quarter = [((QUARTER, HALF), BF16)]
    (line,) = small_call(sum_kernel, spot, pieces, quarter, others=(*halves, moe_slots))
    (line,) = small_call(sum_kernel, spot, [push(line, d, 0, 0) for d in range(RING)], quarter, others=(output,))
    pieces = [push(line, 0, -d, 0) for d in range(RING)]
    hidden = make_hidden(dn)
    (half,) = small_call(gather_x_kernel, spot, pieces, [((PAY, HALF), BF16)], others=(hidden,))
    made = small_call(
        unpack_kernel,
        spot,
        (half, push(half, 0, 0, 1)),
        [
            ((WIDTH, 2 * LANES), F32),
            ((WIDTH, LANES), F32),
            ((WIDTH, LANES), F32),
            ((ROWS, WIDTH), F32),
            ((EXPERTS, WIDTH), F32),
            ((8, WIDTH), F32),
        ],
    )
    return *made, hidden


def hidden_kernel(a, b, c, hidden, gain, dmiddle, out):
    dn = a[...].astype(F32) + b[...].astype(F32) + c[...].astype(F32)
    x = hidden[...].astype(F32)
    inverse = lax.rsqrt(jnp.mean(x * x, axis=-1, keepdims=True) + NORM_EPS)
    plain = x * inverse
    scaled = dn * gain[...]
    along = jnp.mean(scaled * plain, axis=-1, keepdims=True)
    out[...] = dmiddle[...] + inverse * (scaled - plain * along)


def hidden_grad(dn, hidden, gain, dmiddle):
    return pl.pallas_call(
        hidden_kernel,
        out_shape=jax.ShapeDtypeStruct((ROWS, WIDTH), F32),
        in_specs=[WHOLE] * 6,
        out_specs=WHOLE,
        compiler_params=params(),
        cost_estimate=NO_COST,
        name="hidden_grad",
    )(*dn, hidden, gain, dmiddle)


def rope_tables(length):
    freqs = ROPE_BASE ** (-jnp.arange(HD // 2, dtype=F32) * 2.0 / HD)
    angles = jnp.arange(length, dtype=F32)[:, None] * freqs[None, :]
    cosine, sine = jnp.cos(angles), jnp.sin(angles)
    return jnp.concatenate([cosine] * 4, axis=1), jnp.concatenate([-sine, sine] * 2, axis=1)


def shards(
    hidden_in, segment_ids, expert_ids, slot_index, attn_gain, w_query, w_key, w_value, w_output,
    ffn_gain, w_router, w_gate_up, w_down, cotangent,
):
    length = RING * ROWS
    here, rank = lax.axis_index("ep"), lax.axis_index("tp")
    spot = jnp.stack([rank, here // 8, (here // 2) % 4, here % 2]).astype(jnp.int32)

    named = expert_ids[:, :, None] == jnp.arange(EXPERTS, dtype=jnp.int32)[None, None, :]
    slot_of = jnp.sum(jnp.where(named, slot_index[:, :, None] + 1, 0), axis=1) - 1
    chosen = (slot_of >= 0).astype(F32)
    table = slot_of.T.astype(F32)

    gain_one = attn_gain.astype(F32).reshape(1, WIDTH)
    gain_two = ffn_gain.astype(F32).reshape(1, WIDTH)
    cos, sin = rope_tables(length)
    seg_row = segment_ids
    seg_col = segment_ids.reshape(length, 1)

    group = [push_tp(hidden_in, -d) for d in range(RING)]
    cots = lax.all_gather(cotangent, "ep", axis=0, tiled=False, axis_index_groups=SAME_CORE)
    weights = jnp.concatenate([w_gate_up.reshape(WIDTH, 2 * HALF), w_down.reshape(HALF, WIDTH)], axis=0)
    made = attend(spot, group, gain_one, w_query, w_key, w_value, w_output, cos, sin, seg_col, seg_row)
    normed, q, k, v, mixed, lse = made[:6]
    branches = [push_tp(made[6 + d], d) for d in range(RING)]
    (weights,) = after((weights,), lse)
    weights = weights, push(weights, 0, 0, 1)
    middle, half_a, half_b, gates_t = route(hidden_in, branches, gain_two, w_router, chosen, table, weights[1])
    (pieces_a, pieces_b), slots_a, slots_b = dispatch(spot, half_a, half_b)
    first, second = Pieces(pieces_a[:4], pieces_b[:4]), Pieces(pieces_a[4:], pieces_b[4:])
    near = first.send_near()
    far = [first.send(0, 2)]
    held = after((pieces_b[2], pieces_b[6]), near[2], near[3])
    far += [first.send(1, 2, held[0]), second.send(1, 2, held[1])]
    held = after(second.near()[:2], *near)
    second.send(0, 1, held[0]), second.send(0, 3, held[1])
    held = after((*second.near()[2:], pieces_a[6]), *near, *far)
    second.send(1, 1, held[0]), second.send(1, 3, held[1]), second.send(0, 2, held[2])

    back_first, moe_slots, saved = expert(spot, 0, first, cots, weights[0])
    near = back_first.send_near()
    near.append(back_first.send(0, 2))
    back_second, moe_slots, saved_other = expert(spot, 1, second, cots, weights[1], moe_slots)
    held = after((back_first.made[1][2], *back_second.near()), *near)
    back_first.send(1, 2, held[0])
    near = back_second.send_near(held[1:])
    held = after((back_second.made[0][2], back_second.made[1][2], weight_grads(saved_other)), *near)
    back_second.send(0, 2, held[0])
    back_second.send(1, 2, held[1])
    grads_e = weight_grads(saved, push(held[2], 0, 0, 1))
    parts = to_owners(combine(slots_a, slots_b, back_first, back_second))

    dmiddle, dbranch, sums = unroute(
        spot, parts, gates_t, middle, cotangent, gain_two, w_router.T.astype(F32)
    )
    group_grad = gather_tp(dbranch)
    sums = [push_tp(sums, d) for d in range(RING)]

    (moe_slots,) = after((moe_slots,), *parts, grads_e)
    moe_slots = lax.all_to_all(
        moe_slots, "ep", split_axis=0, concat_axis=0, tiled=True, axis_index_groups=SAME_CORE
    )

    (summed_e,) = after((grads_e,), *group_grad[2])
    summed = lax.psum(summed_e, "tp")
    dmixed, grad_output = unmix(spot, group_grad, mixed, w_output, summed_e)
    last = unattend(
        spot, q, k, v, lse, dmixed, normed, gain_one, w_query, w_key, w_value, cos, sin, seg_col, seg_row
    )
    gains = [push_tp(last[1], d) for d in range(RING)]
    output = finish(spot, table, moe_slots.reshape(CHIPS * PAIR, WIDTH), middle)
    grad_query, grad_key, grad_value, grad_output, grad_router, grad_gains, grad_hidden = sum_over_ep(
        spot, normed, last[0], grad_output, sums, gains, last[2:], output, moe_slots,
        lambda dn: hidden_grad(dn, hidden_in, gain_one, dmiddle),
    )
    grad_up, grad_down = cast_grads(summed)
    return (
        output,
        grad_hidden,
        grad_gains[1],
        grad_query,
        grad_key,
        grad_value,
        grad_output,
        grad_gains[0],
        grad_router.T,
        grad_up.reshape(1, WIDTH, 2, HALF),
        grad_down.reshape(1, HALF, WIDTH),
    )


def solution(mesh):
    placed = (
        P(("ep", "tp"), None),
        P("ep", None),
        P(("ep", "tp"), None),
        P(("ep", "tp"), None),
        P(),
        P(None, "tp"),
        P(None, "tp"),
        P(None, "tp"),
        P("tp", None),
        P(),
        P(),
        P("ep", None, None, None),
        P("ep", None, None),
        P(("ep", "tp"), None),
    )
    return jax.shard_map(
        shards,
        mesh=mesh,
        in_specs=placed,
        out_specs=(
            P(("ep", "tp"), None),
            P(("ep", "tp"), None),
            P(),
            P(None, "tp"),
            P(None, "tp"),
            P(None, "tp"),
            P("tp", None),
            P(),
            P(),
            P("ep", None, None, None),
            P("ep", None, None),
        ),
        check_vma=False,
    )
```

```python
import jax
import jax.numpy as jnp
from jax import lax
from jax.experimental import pallas as pl
from jax.experimental.pallas import tpu as pltpu
from jax.sharding import PartitionSpec as P

HD = 64
ATT_SCALE = 0.015625
RES_SCALE = 0.22
NORM_EPS = 1e-06
ROPE_BASE = 10000.0
NEG_FILL = -1e30
HIGHEST = lax.Precision.HIGHEST
F32 = jnp.float32
BF16 = jnp.bfloat16

ROWS = 256
WIDTH = 1024
HALF = 512
CAP = 96
EXPERTS = 32
RING = 4
HEADS = 4
LANES = 128
VMEM_BYTES = 58 * 1024 * 1024
WHOLE = pl.BlockSpec(memory_space=pltpu.VMEM)
SCALARS = pl.BlockSpec(memory_space=pltpu.SMEM)
ANYWHERE = pl.BlockSpec(memory_space=pl.ANY)


def params():
    return pltpu.CompilerParams(vmem_limit_bytes=VMEM_BYTES)


NO_COST = pl.CostEstimate(flops=0, bytes_accessed=0, transcendentals=0)


def dot(a, b, precision=None):
    return jnp.dot(a, b, preferred_element_type=F32, precision=precision)


def dot_nt(a, b):
    return lax.dot_general(a, b, (((1,), (1,)), ((), ())), preferred_element_type=F32)


def dot_tn(a, b):
    return lax.dot_general(a, b, (((0,), (0,)), ((), ())), preferred_element_type=F32)


def place(z, x, core):
    return ((z % RING) * RING + (x % RING)) * 2 + core


def push(value, dz, dx, dc):
    if (dz % RING, dx % RING, dc) == (0, 0, 0):
        return value
    pairs = [
        (place(z, x, c), place(z + dz, x + dx, c ^ dc))
        for z in range(RING)
        for x in range(RING)
        for c in range(2)
    ]
    return lax.ppermute(value, "ep", pairs)


def push_tp(value, dy):
    if dy % RING == 0:
        return value
    return lax.ppermute(value, "tp", [(y, (y + dy) % RING) for y in range(RING)])


def after(values, *others):
    count = len(values)
    return pl.pallas_call(
        lambda *refs: None,
        out_shape=[jax.ShapeDtypeStruct(v.shape, v.dtype) for v in values],
        in_specs=[ANYWHERE] * (count + len(others)),
        out_specs=[ANYWHERE] * count,
        input_output_aliases={i: i for i in range(count)},
        cost_estimate=NO_COST,
        name="after",
    )(*values, *others)


def gather_tp(rows):
    after_me, before_me = push_tp(rows, -1), push_tp(rows, 1)
    half = rows.shape[0] // 2
    across = push_tp(after_me[:half], -1), push_tp(before_me[half:], 1)
    return rows, after_me, across, before_me


def add_halves_kernel(one, three, first, rest, ahead, behind):
    half = first.shape[0]
    ahead[0:half, :] = (one[0:half, :].astype(F32) + first[...].astype(F32)).astype(BF16)
    ahead[half:, :] = one[half:, :]
    behind[0:half, :] = three[0:half, :]
    behind[half:, :] = (three[half:, :].astype(F32) + rest[...].astype(F32)).astype(BF16)


def scatter_tp(own, one, two, two_rest, three):
    first, rest = push_tp(two, 1), push_tp(two_rest, -1)
    ahead, behind = pl.pallas_call(
        add_halves_kernel,
        out_shape=[jax.ShapeDtypeStruct(one.shape, BF16)] * 2,
        in_specs=[WHOLE] * 4,
        out_specs=[WHOLE] * 2,
        compiler_params=params(),
        cost_estimate=NO_COST,
        name="add_halves",
    )(one, three, first, rest)
    return (own, push_tp(ahead, 1), push_tp(behind, -1)), (first, rest)


def ignoring(kernel, first, count):
    return lambda *refs: kernel(*refs[:first], *refs[first + count :])


def swap_halves(v):
    lane = lax.broadcasted_iota(jnp.int32, v.shape, 1)
    return jnp.where(lane % HD < HD // 2, pltpu.roll(v, LANES - HD // 2, 1), pltpu.roll(v, HD // 2, 1))


def block_at(index):
    return pl.ds(pl.multiple_of(index * ROWS, ROWS), ROWS)


def key_range(block):
    return max(0, block - 2) * ROWS, (block + 1) * ROWS


def mask_bias(block, seg_col, seg_row):
    lo, hi = key_range(block)
    key_pos = lo + lax.broadcasted_iota(jnp.int32, (hi - lo, ROWS), 0)
    query_pos = block * ROWS + lax.broadcasted_iota(jnp.int32, (hi - lo, ROWS), 1)
    same = seg_col[lo:hi, :] == seg_row[:, block * ROWS : (block + 1) * ROWS]
    return jnp.where(same & (key_pos <= query_pos), 0.0, NEG_FILL)


def attend_kernel(
    rank, x0, x1, x2, x3, gain, wq, wk, wv, wo, cos, sin, seg_col, seg_row,
    normed_far, q_far, k_far, v_far, mixed_far, lse, br0, br1, br2, br3,
    normed, q_out, k_out, v_out, mixed, branches, vt, bias, sems,
):
    me = rank[0]
    pairs = ((normed, normed_far), (q_out, q_far), (k_out, k_far), (v_out, v_far), (mixed, mixed_far))
    stores = [pltpu.make_async_copy(near, far, sems.at[i]) for i, (near, far) in enumerate(pairs)]
    lane = lax.broadcasted_iota(jnp.int32, (ROWS, LANES), 1)
    for d, x_ref in enumerate((x0, x1, x2, x3)):
        at = block_at((me + d) % RING)
        x = x_ref[...].astype(F32)
        inverse = lax.rsqrt(jnp.mean(x * x, axis=-1, keepdims=True) + NORM_EPS)
        low = (x * inverse * gain[...]).astype(BF16)
        normed[at, :] = low
        cos_here, sin_here = cos[at, :], sin[at, :]

        def rope(v):
            return v * cos_here + swap_halves(v) * sin_here

        query = dot(low, wq[...])
        for pair in range(2):
            q = rope(query[:, pair * LANES : (pair + 1) * LANES]) * ATT_SCALE
            other = pltpu.roll(q, HD, 1)
            keep = (lane < HD) if pair == 0 else (lane >= HD)
            first, second = (q, other) if pair == 0 else (other, q)
            at_head = 2 * pair * LANES
            q_out[at, at_head : at_head + LANES] = jnp.where(keep, first, 0.0).astype(BF16)
            q_out[at, at_head + LANES : at_head + 2 * LANES] = jnp.where(keep, second, 0.0).astype(BF16)
        k_out[at, :] = rope(dot(low, wk[...])).astype(BF16)
        v_out[at, :] = dot(low, wv[...]).astype(BF16)
    for copy in stores[:4]:
        copy.start()
    vt[...] = v_out[...].astype(F32).T.astype(BF16)
    for b in range(RING):
        lo, hi = key_range(b)
        rows = slice(b * ROWS, (b + 1) * ROWS)
        bias[0 : hi - lo, :] = mask_bias(b, seg_col, seg_row)
        outs = []
        for h in range(HEADS):
            q = q_out[rows, h * LANES : (h + 1) * LANES]
            scores = dot_nt(k_out[lo:hi, :], q) + bias[0 : hi - lo, :]
            top = jnp.max(scores, axis=0, keepdims=True)
            weights = jnp.exp(scores - top)
            total = jnp.sum(weights, axis=0, keepdims=True)
            out = dot(vt[:, lo:hi], weights.astype(BF16)) * (1.0 / total)
            outs.append(out.T)
            lse[h : h + 1, rows] = top + jnp.log(total)
        mixed[rows, 0:LANES] = jnp.where(lane < HD, outs[0], pltpu.roll(outs[1], HD, 1)).astype(BF16)
        mixed[rows, LANES:] = jnp.where(lane < HD, pltpu.roll(outs[2], HD, 1), outs[3]).astype(BF16)
        branches[b] = dot(mixed[rows, :], wo[...]).astype(BF16)
        for d, br in enumerate((br0, br1, br2, br3)):

            @pl.when((b - me + RING) % RING == d)
            def _():
                pltpu.make_async_copy(branches.at[b], br, sems.at[5 + b]).start()

    stores[4].start()
    for copy in stores:
        copy.wait()
    for b in range(RING):
        for d, br in enumerate((br0, br1, br2, br3)):

            @pl.when((b - me + RING) % RING == d)
            def _():
                pltpu.make_async_copy(branches.at[b], br, sems.at[5 + b]).wait()


def attend(rank, pieces, gain, wq, wk, wv, wo, cos, sin, seg_col, seg_row, *others):
    length = RING * ROWS
    return pl.pallas_call(
        ignoring(attend_kernel, 14, len(others)),
        out_shape=[
            jax.ShapeDtypeStruct((length, WIDTH), BF16),
            jax.ShapeDtypeStruct((length, HEADS * LANES), BF16),
            jax.ShapeDtypeStruct((length, LANES), BF16),
            jax.ShapeDtypeStruct((length, LANES), BF16),
            jax.ShapeDtypeStruct((length, HEADS * HD), BF16),
            jax.ShapeDtypeStruct((8, length), F32),
        ]
        + [jax.ShapeDtypeStruct((ROWS, WIDTH), BF16)] * RING,
        in_specs=[SCALARS] + [WHOLE] * 13 + [ANYWHERE] * len(others),
        out_specs=[ANYWHERE] * 5 + [WHOLE] + [ANYWHERE] * 4,
        scratch_shapes=[
            pltpu.VMEM((length, WIDTH), BF16),
            pltpu.VMEM((length, HEADS * LANES), BF16),
            pltpu.VMEM((length, LANES), BF16),
            pltpu.VMEM((length, LANES), BF16),
            pltpu.VMEM((length, HEADS * HD), BF16),
            pltpu.VMEM((RING, ROWS, WIDTH), BF16),
            pltpu.VMEM((LANES, length), BF16),
            pltpu.VMEM((3 * ROWS, ROWS), F32),
            pltpu.SemaphoreType.DMA((9,)),
        ],
        compiler_params=params(),
        cost_estimate=NO_COST,
        name="attend",
    )(rank, *pieces, gain, wq, wk, wv, wo, cos, sin, seg_col, seg_row, *others)


def high_low(v):
    high = v.astype(BF16)
    return jnp.concatenate([high, (v - high.astype(F32)).astype(BF16)], axis=1)


def route_kernel(x, b0, b1, b2, b3, gain, wr, chosen, table, middle, half_a, half_b, gates_t):
    branch = b0[...].astype(F32) + b1[...].astype(F32) + b2[...].astype(F32) + b3[...].astype(F32)
    mid = x[...].astype(F32) + RES_SCALE * branch
    middle[...] = mid
    inverse = lax.rsqrt(jnp.mean(mid * mid, axis=-1, keepdims=True) + NORM_EPS)
    routed = (mid * inverse * gain[...]).astype(BF16)
    half_b[0:ROWS, :] = routed[:, HALF:]
    logits = jnp.where(chosen[...] > 0.0, dot(routed, wr[...]), NEG_FILL)
    weights = jnp.exp(logits - jnp.max(logits, axis=-1, keepdims=True))
    gates = (weights / jnp.sum(weights, axis=-1, keepdims=True)).T
    gates_t[...] = gates
    half_a[0:ROWS, :] = routed[:, :HALF]
    half_a[ROWS : ROWS + EXPERTS, :] = high_low(gates)
    slots = jnp.concatenate([table[...], jnp.zeros_like(gates)], axis=1).astype(BF16)
    half_a[ROWS + EXPERTS :, :] = slots
    half_b[ROWS:, :] = slots


def route(x, branches, gain, wr, chosen, table, *others):
    return pl.pallas_call(
        ignoring(route_kernel, 9, len(others)),
        out_shape=[
            jax.ShapeDtypeStruct((ROWS, WIDTH), F32),
            jax.ShapeDtypeStruct((ROWS + 2 * EXPERTS, HALF), BF16),
            jax.ShapeDtypeStruct((ROWS + EXPERTS, HALF), BF16),
            jax.ShapeDtypeStruct((EXPERTS, ROWS), F32),
        ],
        in_specs=[WHOLE] * 9 + [ANYWHERE] * len(others),
        out_specs=[WHOLE] * 4,
        compiler_params=params(),
        cost_estimate=pl.CostEstimate(flops=20_000_000, bytes_accessed=5_000_000, transcendentals=8192),
        name="route",
    )(x, *branches, gain, wr, chosen, table, *others)


PIECE = RING * CAP
EXTRA = 16


def line_row(d, p, e):
    return p * 8 + e * 4 + d


def slot_matrix(row):
    slot = lax.broadcasted_iota(jnp.int32, (CAP, ROWS), 0).astype(F32)
    return jnp.where(slot == row, 1.0, 0.0)


def line_matrix(slots, d):
    rows = [line_row(d, p, e) for p in range(RING) for e in range(2)]
    return jnp.concatenate([slot_matrix(slots[r : r + 1, :]).astype(BF16) for r in rows], axis=0)


def expert_row(spot, half, d, p, e):
    z, x, core = spot[1], spot[2], spot[3]
    if half == 0:
        x = (x + p) % RING
    else:
        z = (z + p) % RING
    return (z * RING + x) * 2 + (core + e) % 2


def fill_pieces(slots, rows, pieces):
    for d in range(RING):
        filled = dot(line_matrix(slots, d), rows[d][0:ROWS, :]).astype(BF16)
        for p in range(RING):
            for e in range(2):
                pieces[e * 4 + p][d * CAP : (d + 1) * CAP, :] = filled[(p * 2 + e) * CAP : (p * 2 + e + 1) * CAP, :]


def pick_rows(spot, half, blocks, first, table, picked):
    for d in range(RING):
        table[...] = blocks[d][first : first + EXPERTS, :].astype(F32)
        for p in range(RING):
            for e in range(2):
                r = line_row(d, p, e)
                picked[r : r + 1, :] = table[pl.ds(expert_row(spot, half, d, p, e), 1), :]


def dispatch_kernel(spot, *refs):
    blocks, pieces, slots, (table, gates, picked) = refs[:8], (refs[8:16], refs[16:24]), refs[24:26], refs[26:]
    pick_rows(spot, 0, blocks[:4], ROWS, table, gates)
    for half in range(2):
        mine = blocks[4 * half : 4 * half + 4]
        pick_rows(spot, half, mine, ROWS + EXPERTS * (1 - half), table, picked)
        slots[half][...] = picked[:, :ROWS]
        fill_pieces(slots[half], mine, pieces[half])
        if half == 0:
            for p in range(RING):
                for e in range(2):
                    at = slice(p * 8 + e * 4, p * 8 + e * 4 + 4)
                    extra = jnp.concatenate([gates[at, :], picked[at, :], jnp.zeros((8, HALF), F32)], axis=0)
                    pieces[0][e * 4 + p][PIECE:, :] = extra.astype(BF16)


def combine_kernel(slots_a, slots_b, *refs):
    everyone, (second, sems) = range(RING), refs[24:]
    fetches = [pltpu.make_async_copy(refs[8 + i], second.at[i], sems.at[i]) for i in range(8)]
    for copy in fetches:
        copy.start()
    for half, slots in enumerate((slots_a, slots_b)):
        if half == 1:
            for copy in fetches:
                copy.wait()
        pieces = refs[:8] if half == 0 else [second.at[i] for i in range(8)]
        rows = refs[16 + 4 * half : 20 + 4 * half]
        for d in everyone:
            filled = [pieces[e * 4 + p][d * CAP : (d + 1) * CAP, :] for p in everyone for e in range(2)]
            filled = jnp.concatenate(filled, axis=0)
            rows[d][0:ROWS, :] = dot_tn(line_matrix(slots, d), filled).astype(BF16)
        if half == 0:
            tables = [pieces[i][PIECE:, :].astype(F32) for i in range(8)]
            for d in everyone:
                picked = [tables[e * 4 + p][d : d + 1, :] for p in everyone for e in range(2)]
                extra = jnp.concatenate(picked + [jnp.zeros((8, HALF), F32)], axis=0)
                rows[d][ROWS:, :] = extra.astype(BF16)


SLOT_COST = pl.CostEstimate(flops=1_000_000_000, bytes_accessed=5_000_000, transcendentals=0)
TABLE = pltpu.VMEM((EXPERTS, HALF), F32)


def shape_of(rows, dtype=BF16):
    return jax.ShapeDtypeStruct((rows, HALF), dtype)


def spread_rows(half_a, half_b):
    return [push(half_a, -d, 0, 0) for d in range(RING)] + [push(half_b, 0, -d, 0) for d in range(RING)]


def dispatch(spot, half_a, half_b):
    made = pl.pallas_call(
        dispatch_kernel,
        out_shape=[shape_of(PIECE + EXTRA)] * 8
        + [shape_of(PIECE)] * 8
        + [jax.ShapeDtypeStruct((EXPERTS, ROWS), F32)] * 2,
        in_specs=[SCALARS] + [WHOLE] * 8,
        out_specs=[WHOLE] * 18,
        scratch_shapes=[TABLE] * 3,
        compiler_params=params(),
        cost_estimate=SLOT_COST,
        name="dispatch",
    )(spot, *spread_rows(half_a, half_b))
    return (made[:8], made[8:16]), made[16], made[17]


class Pieces:
    def __init__(self, half_a, half_b):
        self.made = list(half_a), list(half_b)
        self.got = [half_a[0], None, None, None], [half_b[0], None, None, None]

    def send(self, half, p, held=None):
        piece = self.made[half][p] if held is None else held
        self.got[half][-p % RING] = push(piece, 0, p, 0) if half == 0 else push(piece, p, 0, 0)
        return self.got[half][-p % RING]

    def send_near(self, held=(None,) * 4):
        places = (0, 1), (0, 3), (1, 1), (1, 3)
        return [self.send(half, p, piece) for (half, p), piece in zip(places, held)]

    def near(self):
        return self.made[0][1], self.made[0][3], self.made[1][1], self.made[1][3]


def combine(slots_a, slots_b, first, second, *others):
    pieces = [*first.got[0], *second.got[0], *first.got[1], *second.got[1]]
    return pl.pallas_call(
        ignoring(combine_kernel, 18, len(others)),
        out_shape=[shape_of(ROWS + EXTRA)] * RING + [shape_of(ROWS)] * RING,
        in_specs=[WHOLE] * 10 + [ANYWHERE] * (8 + len(others)),
        out_specs=[WHOLE] * 8,
        scratch_shapes=[pltpu.VMEM((8, PIECE, HALF), BF16), pltpu.SemaphoreType.DMA((8,))],
        compiler_params=params(),
        cost_estimate=pl.CostEstimate(flops=60_000_000_000, bytes_accessed=0, transcendentals=0),
        name="combine",
    )(slots_a, slots_b, *pieces, *others)


def to_owners(partial):
    got = [None] * 8
    for d in range(RING):
        got[-d % RING] = push(partial[d], d, 0, 0)
        got[4 + -d % RING] = push(partial[4 + d], 0, d, 0)
    return got


CHIPS = RING * RING
PAIR = 2 * CAP


def chips_matrix(spot, table, step):
    rows = []
    for i in range(RING):
        for e in range(2):
            expert = (step * RING + i) * 2 + (spot[3] + e) % 2
            rows.append(slot_matrix(table[pl.ds(expert, 1), :]).astype(BF16))
    return jnp.concatenate(rows, axis=0)


def finish_kernel(spot, table, slots, middle, out, total):
    step = pl.program_id(0)
    term = dot_tn(chips_matrix(spot, table, step), slots[...])

    @pl.when(step == 0)
    def _():
        total[...] = term

    @pl.when(step > 0)
    def _():
        total[...] += term

    @pl.when(step == RING - 1)
    def _():
        out[...] = (middle[...] + RES_SCALE * total[...]).astype(BF16)


def finish(spot, table, slots, middle):
    return pl.pallas_call(
        finish_kernel,
        grid=(RING,),
        out_shape=jax.ShapeDtypeStruct((ROWS, WIDTH), BF16),
        in_specs=[SCALARS, WHOLE, pl.BlockSpec((RING * PAIR, WIDTH), lambda s: (s, 0)), WHOLE],
        out_specs=pl.BlockSpec((ROWS, WIDTH), lambda s: (0, 0)),
        scratch_shapes=[pltpu.VMEM((ROWS, WIDTH), F32)],
        compiler_params=params(),
        cost_estimate=SLOT_COST,
        name="finish",
    )(spot, table, slots, middle)


SAME_CORE = [list(range(core, EXPERTS, 2)) for core in range(2)]


STEPS = RING
STEP_ROWS = RING * CAP


def expert_kernel(e, spot, *refs):
    ra, rb, cot, weights = refs[:4], refs[4:8], refs[8], refs[9]
    refs = refs[10 + e :]
    qa, qb, moe, (disp_out, dgu_out, inner_out, dex_out) = refs[:4], refs[4:8], refs[8], refs[9:13]
    wgu, wd, rows_in, cot_in, extra_in, back_out, moe_out, extra_out, weight_sem, in_sem, out_sem = refs[13:]
    step = pl.program_id(0)
    loads = [
        pltpu.make_async_copy(weights.at[pl.ds(0, WIDTH)], wgu, weight_sem.at[0]),
        pltpu.make_async_copy(weights.at[pl.ds(WIDTH, HALF)], wd, weight_sem.at[1]),
    ]

    def places(dx, half_a, half_b, halves, extra):
        slot = dx % 2
        ends = [
            (half_a[dx].at[pl.ds(0, PIECE)], halves.at[slot, :, pl.ds(0, HALF)]),
            (half_a[dx].at[pl.ds(PIECE, EXTRA)], extra.at[slot]),
        ]
        for dz in range(RING):
            ends.append((half_b[dz].at[pl.ds(dx * CAP, CAP)], halves.at[slot, pl.ds(dz * CAP, CAP), pl.ds(HALF, HALF)]))
        return ends

    def chip(dz, dx):
        return ((spot[1] + dz) % RING) * RING + (spot[2] + dx) % RING

    def fetches(dx):
        ends = places(dx, ra, rb, rows_in, extra_in)
        for dz in range(RING):
            ends.append((cot.at[chip(dz, dx)], cot_in.at[dx % 2, pl.ds(dz * ROWS, ROWS)]))
        return [pltpu.make_async_copy(far, near, in_sem.at[dx % 2, n]) for n, (far, near) in enumerate(ends)]

    def stores(dx):
        ends = places(dx, qa, qb, back_out, extra_out)
        for dz in range(RING):
            ends.append((moe.at[chip(dz, dx), pl.ds(e * CAP, CAP)], moe_out.at[dx % 2, pl.ds(dz * CAP, CAP)]))
        return [pltpu.make_async_copy(near, far, out_sem.at[dx % 2, n]) for n, (far, near) in enumerate(ends)]

    for j in range(STEPS):

        @pl.when(step == j)
        def _():
            if j == 0:
                for copy in fetches(0) + loads:
                    copy.start()
            if j + 1 < STEPS:
                for copy in fetches(j + 1):
                    copy.start()
            for copy in fetches(j):
                copy.wait()
            if j == 0:
                for copy in loads:
                    copy.wait()
            if j >= 2:
                for copy in stores(j - 2):
                    copy.wait()

    slot = step % 2
    extra = extra_in[slot].astype(F32)
    gates = extra[0:4, :ROWS] + extra[0:4, ROWS:]
    fills = [slot_matrix(extra[4 + dz : 5 + dz, :ROWS]) for dz in range(RING)]
    gate_slot = jnp.concatenate(
        [jnp.sum(fills[dz] * gates[dz : dz + 1, :], axis=1, keepdims=True) for dz in range(RING)], axis=0
    )
    rows = rows_in[slot]
    disp_out[...] = rows
    gate_up = dot(rows, wgu[...])
    dmoe = [
        dot(fills[dz].astype(BF16), cot_in[slot, dz * ROWS : (dz + 1) * ROWS, :]) for dz in range(RING)
    ]
    dmoe = RES_SCALE * jnp.concatenate(dmoe, axis=0)
    dex = (gate_slot * dmoe).astype(BF16)
    dex_out[...] = dex
    dinner = dot_nt(dex, wd[...])
    gate, up = gate_up[:, :HALF], gate_up[:, HALF:]
    sigmoid = jax.nn.sigmoid(gate)
    silu = gate * sigmoid
    inner = (silu * up).astype(BF16)
    inner_out[...] = inner
    made = dot(inner, wd[...]).astype(BF16).astype(F32)
    dgate = dinner * up * sigmoid * (1.0 + gate * (1.0 - sigmoid))
    dgu = jnp.concatenate([dgate.astype(BF16), (dinner * silu).astype(BF16)], axis=1)
    dgu_out[...] = dgu
    back_out[slot] = dot_nt(dgu, wgu[...]).astype(BF16)
    moe_out[slot] = (gate_slot * made).astype(BF16)
    dgate_slot = jnp.sum(dmoe * made, axis=1, keepdims=True)
    dgates = [
        jnp.sum(fills[dz] * dgate_slot[dz * CAP : (dz + 1) * CAP, :], axis=0, keepdims=True) for dz in range(RING)
    ]
    dgates = jnp.concatenate(dgates + [jnp.zeros((EXTRA - RING, ROWS), F32)], axis=0)
    extra_out[slot] = high_low(dgates)

    for j in range(STEPS):

        @pl.when(step == j)
        def _():
            for copy in stores(j):
                copy.start()
            if j == STEPS - 1:
                for copy in stores(j - 1) + stores(j):
                    copy.wait()


def expert(spot, e, pieces, cots, weights, *moe):
    total = STEPS * STEP_ROWS
    wide = pl.BlockSpec((STEP_ROWS, WIDTH), lambda s: (s, 0))
    narrow = pl.BlockSpec((STEP_ROWS, HALF), lambda s: (s, 0))
    buf, small = pltpu.VMEM((2, STEP_ROWS, WIDTH), BF16), pltpu.VMEM((2, EXTRA, HALF), BF16)
    made = pl.pallas_call(
        lambda *refs: expert_kernel(e, *refs),
        grid=(STEPS,),
        out_shape=[shape_of(PIECE + EXTRA)] * RING
        + [shape_of(PIECE)] * RING
        + [
            jax.ShapeDtypeStruct((CHIPS, PAIR, WIDTH), BF16),
            jax.ShapeDtypeStruct((total, WIDTH), BF16),
            jax.ShapeDtypeStruct((total, WIDTH), BF16),
            jax.ShapeDtypeStruct((total, HALF), BF16),
            jax.ShapeDtypeStruct((total, WIDTH), BF16),
        ],
        in_specs=[SCALARS] + [ANYWHERE] * (10 + e),
        out_specs=[ANYWHERE] * 9 + [wide, wide, narrow, wide],
        scratch_shapes=[
            pltpu.VMEM((WIDTH, WIDTH), BF16),
            pltpu.VMEM((HALF, WIDTH), BF16),
            buf, pltpu.VMEM((2, RING * ROWS, WIDTH), BF16), small, buf, buf, small,
            pltpu.SemaphoreType.DMA((2,)),
            pltpu.SemaphoreType.DMA((2, 10)),
            pltpu.SemaphoreType.DMA((2, 10)),
        ],
        input_output_aliases={11: 8} if e else {},
        compiler_params=params(),
        cost_estimate=NO_COST,
        name="expert",
    )(spot, *pieces.got[0], *pieces.got[1], cots, weights, *moe)
    return Pieces(made[:4], made[4:8]), made[8], made[9:]


def weight_grads_kernel(with_other, *refs):
    disp, dgu, inner, dex = refs[:4]
    other, out = refs[4] if with_other else None, refs[4 + with_other]
    disp_in, dgu_in, inner_in, dex_in, made, other_in, sems, out_sems = refs[5 + with_other :]
    pairs = [(disp, disp_in), (dgu, dgu_in), (inner, inner_in), (dex, dex_in)]
    if with_other:
        pairs.append((other, other_in))
    fetches = [pltpu.make_async_copy(far, near, sems.at[i]) for i, (far, near) in enumerate(pairs)]
    stores = [
        pltpu.make_async_copy(made.at[pl.ds(i * HALF, HALF)], out.at[pl.ds(i * HALF, HALF)], out_sems.at[i])
        for i in range(3)
    ]
    for copy in fetches:
        copy.start()
    for i, left in enumerate((disp_in, disp_in, inner_in)):
        if i == 0:
            fetches[0].wait()
            fetches[1].wait()
        if i == 2:
            fetches[2].wait()
            fetches[3].wait()
        if with_other and i == 0:
            fetches[4].wait()
        cols = slice(i * HALF, (i + 1) * HALF) if i < 2 else slice(None)
        grad = dot_tn(left[:, cols], (dgu_in if i < 2 else dex_in)[...])
        if with_other:
            grad = grad.astype(BF16).astype(F32) + other_in[i * HALF : (i + 1) * HALF, :].astype(F32)
        made[i * HALF : (i + 1) * HALF, :] = grad.astype(BF16)
        stores[i].start()
    for copy in stores:
        copy.wait()


def weight_grads(saved, *other):
    wide, narrow = pltpu.VMEM((4 * STEP_ROWS, WIDTH), BF16), pltpu.VMEM((4 * STEP_ROWS, HALF), BF16)
    grads = pltpu.VMEM((WIDTH + HALF, WIDTH), BF16)
    return pl.pallas_call(
        lambda *refs: weight_grads_kernel(len(other), *refs),
        out_shape=jax.ShapeDtypeStruct((WIDTH + HALF, WIDTH), BF16),
        in_specs=[ANYWHERE] * (4 + len(other)),
        out_specs=ANYWHERE,
        scratch_shapes=[
            wide, wide, narrow, wide, grads, grads, pltpu.SemaphoreType.DMA((5,)), pltpu.SemaphoreType.DMA((3,)),
        ],
        compiler_params=params(),
        cost_estimate=NO_COST,
        name="weight_grads",
    )(*saved, *other)


def cast_grads_kernel(grads, up, down):
    for i in range(2):
        up[:, i, :] = grads[0:WIDTH, i * HALF : (i + 1) * HALF].astype(F32)
    down[...] = grads[WIDTH:, :].astype(F32)


def cast_grads(grads, *others):
    return pl.pallas_call(
        ignoring(cast_grads_kernel, 1, len(others)),
        out_shape=[
            jax.ShapeDtypeStruct((WIDTH, 2, HALF), F32),
            jax.ShapeDtypeStruct((HALF, WIDTH), F32),
        ],
        in_specs=[WHOLE] + [ANYWHERE] * len(others),
        out_specs=[WHOLE] * 2,
        compiler_params=params(),
        cost_estimate=NO_COST,
        name="cast_grads",
    )(grads, *others)


def unroute_kernel(spot, *refs):
    parts, (gates_t, middle, cot, gain, wr_t, dmiddle, dbranch, sums, gates, dlogits) = refs[:8], refs[8:]

    def four(pieces):
        a, b, c, d = (piece[0:ROWS, :].astype(F32) for piece in pieces)
        return (a + b) + (c + d)

    order = [
        (((spot[1] + dz) % RING) * RING + (spot[2] + dx) % RING) * 2 + (spot[3] + e) % 2
        for dz in range(RING)
        for dx in range(RING)
        for e in range(2)
    ]
    for i, at in enumerate(order):
        gates[i : i + 1, :] = gates_t[pl.ds(at, 1), :]
    tables = [part[ROWS:, :].astype(F32) for part in parts[:4]]
    dgates = jnp.concatenate([t[0:8, :ROWS] + t[0:8, ROWS:] for t in tables], axis=0)
    made = gates[...] * (dgates - jnp.sum(gates[...] * dgates, axis=0, keepdims=True))
    for i, at in enumerate(order):
        dlogits[pl.ds(at, 1), :] = made[i : i + 1, :]
    drouted = jnp.concatenate([four(parts[:4]), four(parts[4:])], axis=1)
    drouted = drouted + dot(dlogits[...].T, wr_t[...], HIGHEST)
    mid = middle[...]
    inverse = lax.rsqrt(jnp.mean(mid * mid, axis=-1, keepdims=True) + NORM_EPS)
    plain = mid * inverse
    routed = (plain * gain[...]).astype(BF16).astype(F32)
    sums[0:EXPERTS, :] = dot(dlogits[...], routed, HIGHEST)
    sums[EXPERTS : EXPERTS + 8, :] = jnp.broadcast_to(jnp.sum(drouted * plain, axis=0, keepdims=True), (8, WIDTH))
    scaled = drouted * gain[...]
    along = jnp.mean(scaled * plain, axis=-1, keepdims=True)
    total = cot[...].astype(F32) + inverse * (scaled - plain * along)
    dmiddle[...] = total
    dbranch[...] = (RES_SCALE * total).astype(BF16)


def unroute(spot, parts, gates_t, middle, cot, gain, wr_t, *others):
    return pl.pallas_call(
        ignoring(unroute_kernel, 14, len(others)),
        out_shape=[
            jax.ShapeDtypeStruct((ROWS, WIDTH), F32),
            jax.ShapeDtypeStruct((ROWS, WIDTH), BF16),
            jax.ShapeDtypeStruct((EXPERTS + 8, WIDTH), F32),
        ],
        in_specs=[SCALARS] + [WHOLE] * 13 + [ANYWHERE] * len(others),
        out_specs=[WHOLE] * 3,
        scratch_shapes=[pltpu.VMEM((EXPERTS, ROWS), F32), pltpu.VMEM((EXPERTS, ROWS), F32)],
        compiler_params=params(),
        cost_estimate=NO_COST,
        name="unroute",
    )(spot, *parts, gates_t, middle, cot, gain, wr_t, *others)


def unmix_kernel(rank, d0, d1, d2, d2_rest, d3, mixed, wo, dmixed, grad_out):
    me = rank[0]
    lane = lax.broadcasted_iota(jnp.int32, (ROWS, LANES), 1)
    for d, ref in enumerate((d0, d1, d2, d3)):
        at = block_at((me + d) % RING)
        grad = jnp.concatenate([d2[...], d2_rest[...]], axis=0) if d == 2 else ref[...]
        low = dot_nt(grad, wo[...])
        for pair in range(2):
            both = low[:, pair * LANES : (pair + 1) * LANES]
            other = pltpu.roll(both, HD, 1)
            keep = (lane < HD) if pair == 0 else (lane >= HD)
            first, second = (both, other) if pair == 0 else (other, both)
            at_head = 2 * pair * LANES
            dmixed[at, at_head : at_head + LANES] = jnp.where(keep, first, 0.0).astype(BF16)
            dmixed[at, at_head + LANES : at_head + 2 * LANES] = jnp.where(keep, second, 0.0).astype(BF16)
        term = dot_tn(mixed[at, :], grad)
        total = term if d == 0 else total + term
    grad_out[...] = total.astype(BF16)


def unmix(rank, pieces, mixed, wo, *others):
    length = RING * ROWS
    return pl.pallas_call(
        ignoring(unmix_kernel, 8, len(others)),
        out_shape=[
            jax.ShapeDtypeStruct((length, HEADS * LANES), BF16),
            jax.ShapeDtypeStruct((HEADS * HD, WIDTH), BF16),
        ],
        in_specs=[SCALARS] + [WHOLE] * 7 + [ANYWHERE] * len(others),
        out_specs=[WHOLE] * 2,
        compiler_params=params(),
        cost_estimate=pl.CostEstimate(flops=1_100_000_000, bytes_accessed=5_000_000, transcendentals=0),
        name="unmix",
    )(rank, pieces[0], pieces[1], *pieces[2], pieces[3], mixed, wo, *others)


def unattend_kernel(
    spot, q_in, k_in, v_in, lse, dmixed, normed, gain, wq, wk, wv, cos, sin, seg_col, seg_row,
    dqkv, dgain, dn0, dn1, dn2, dn2_rest, dn3, kt, bias, dk, dv,
):
    me = spot[0]
    lane = lax.broadcasted_iota(jnp.int32, (ROWS, LANES), 1)
    kt[...] = k_in[...].astype(F32).T.astype(BF16)
    dk[...] = jnp.zeros_like(dk)
    dv[...] = jnp.zeros_like(dv)

    def unrope(v, rows):
        return v * cos[rows, :] - swap_halves(v) * sin[rows, :]

    for b in range(RING):
        lo, hi = key_range(b)
        rows = slice(b * ROWS, (b + 1) * ROWS)
        bias[0 : hi - lo, :] = mask_bias(b, seg_col, seg_row)
        dqs = []
        for h in range(HEADS):
            cols = slice(h * LANES, (h + 1) * LANES)
            q, do = q_in[rows, cols], dmixed[rows, cols]
            scores = dot_nt(k_in[lo:hi, :], q) + bias[0 : hi - lo, :]
            probs = jnp.exp(scores - lse[h : h + 1, rows])
            dprobs = dot_nt(v_in[lo:hi, :], do)
            delta = jnp.sum(probs * dprobs, axis=0, keepdims=True)
            dscores = (probs * (dprobs - delta)).astype(BF16)
            dv[lo:hi, :] += dot(probs.astype(BF16), do)
            dk[lo:hi, :] += dot(dscores, q)
            dqs.append(dot(kt[:, lo:hi], dscores).T * ATT_SCALE)
        first = jnp.where(lane < HD, dqs[0], pltpu.roll(dqs[1], HD, 1))
        second = jnp.where(lane < HD, pltpu.roll(dqs[2], HD, 1), dqs[3])
        dqkv[rows, 0:LANES] = unrope(first, rows).astype(BF16)
        dqkv[rows, LANES : 2 * LANES] = unrope(second, rows).astype(BF16)
    for b in range(RING):
        rows = slice(b * ROWS, (b + 1) * ROWS)
        dqkv[rows, 2 * LANES : 3 * LANES] = unrope(dk[rows, :], rows).astype(BF16)
        dqkv[rows, 3 * LANES :] = dv[rows, :].astype(BF16)
        dn = dot_nt(dqkv[rows, : 2 * LANES], wq[...])
        dn = dn + dot_nt(dqkv[rows, 2 * LANES : 3 * LANES], wk[...])
        dn = dn + dot_nt(dqkv[rows, 3 * LANES :], wv[...])
        term = jnp.sum(dn * normed[rows, :].astype(F32), axis=0, keepdims=True)
        gain_sum = term if b == 0 else gain_sum + term
        dn = dn.astype(BF16)
        relative = (b - me + RING) % RING
        for d, ref in ((0, dn0), (1, dn1), (3, dn3)):

            @pl.when(relative == d)
            def _():
                ref[...] = dn

        @pl.when(relative == 2)
        def _():
            dn2[...] = dn[: ROWS // 2, :]
            dn2_rest[...] = dn[ROWS // 2 :, :]

    dgain[...] = jnp.broadcast_to(gain_sum / gain[...], (8, WIDTH))


def unattend(spot, q, k, v, lse, dmixed, normed, gain, wq, wk, wv, cos, sin, seg_col, seg_row):
    length = RING * ROWS
    return pl.pallas_call(
        unattend_kernel,
        out_shape=[
            jax.ShapeDtypeStruct((length, HALF), BF16),
            jax.ShapeDtypeStruct((8, WIDTH), F32),
        ]
        + [jax.ShapeDtypeStruct((rows, WIDTH), BF16) for rows in (ROWS, ROWS, ROWS // 2, ROWS // 2, ROWS)],
        in_specs=[SCALARS] + [WHOLE] * 14,
        out_specs=[WHOLE] * 7,
        scratch_shapes=[
            pltpu.VMEM((LANES, length), BF16),
            pltpu.VMEM((3 * ROWS, ROWS), F32),
            pltpu.VMEM((length, LANES), F32),
            pltpu.VMEM((length, LANES), F32),
        ],
        compiler_params=params(),
        cost_estimate=NO_COST,
        name="unattend",
    )(spot, q, k, v, lse, dmixed, normed, gain, wq, wk, wv, cos, sin, seg_col, seg_row)


PAY = 832
QUARTER = PAY // RING
GAINS = 768 + EXPERTS


def pack_kernel(spot, normed, dqkv, grad_out, s0, s1, s2, s3, own, other):
    core = spot[3]
    sums = (s0[...] + s1[...]) + (s2[...] + s3[...])
    row = lax.broadcasted_iota(jnp.int32, (32, HALF), 0)
    for side, out in enumerate((own, other)):
        cols = pl.ds(pl.multiple_of(((core + side) % 2) * HALF, HALF), HALF)
        left = (core + side) % 2 == 0
        out[0:HALF, :] = dot_tn(normed[:, cols], dqkv[...]).astype(BF16)
        out[HALF:768, :] = grad_out[:, cols]
        here = jnp.where(left, sums[:, :HALF], sums[:, HALF:])
        out[768:GAINS, :] = here[0:EXPERTS, :].astype(BF16)
        out[GAINS:, :] = jnp.where(row == 0, here[EXPERTS : EXPERTS + 1, :], 0.0).astype(BF16)


def add_all(refs):
    total = refs[0][...].astype(F32)
    for ref in refs[1:]:
        total = total + ref[...].astype(F32)
    return total.astype(BF16)


def quarter_rows(index):
    return pl.ds(pl.multiple_of(index * QUARTER, 16), QUARTER)


def reduce_core_kernel(spot, own, got, g0, g1, g2, g3, p0, p1, p2, p3, total):
    total[...] = add_all((own, got))
    gain = (g0[...] + g1[...]) + (g2[...] + g3[...])
    row = lax.broadcasted_iota(jnp.int32, (32, HALF), 0)
    tail = jnp.where(row == 1, gain[0:1, :HALF], total[GAINS:, :].astype(F32))
    total[GAINS:, :] = jnp.where(row == 2, gain[0:1, HALF:], tail).astype(BF16)
    for d, piece in enumerate((p0, p1, p2, p3)):
        piece[...] = total[quarter_rows((spot[2] + d) % RING), :]


def sum_kernel(spot, a, b, c, d, out):
    out[...] = add_all((a, b, c, d))


def gather_x_kernel(spot, a, b, c, d, out):
    for d, piece in enumerate((a, b, c, d)):
        out[quarter_rows((spot[2] + d) % RING), :] = piece[...]


def unpack_kernel(spot, own, got, query, key, value, grad_out, router, gains):
    for side, half in enumerate((own, got)):
        at = pl.ds(pl.multiple_of(((spot[3] + side) % 2) * HALF, HALF), HALF)
        query[at, :] = half[0:HALF, : 2 * LANES].astype(F32)
        key[at, :] = half[0:HALF, 2 * LANES : 3 * LANES].astype(F32)
        value[at, :] = half[0:HALF, 3 * LANES :].astype(F32)
        grad_out[:, at] = half[HALF:768, :].astype(F32)
        router[:, at] = half[768:GAINS, :].astype(F32)
        gains[0:1, at] = half[GAINS:, :].astype(F32)[0:1, :]
    both = own[GAINS:, :].astype(F32)[0:8, :] + got[GAINS:, :].astype(F32)[0:8, :]
    gains[1:2, :HALF] = both[1:2, :]
    gains[1:2, HALF:] = both[2:3, :]


def small_call(kernel, spot, refs, shapes, scratch=None, flops=1_000_000, others=()):
    return pl.pallas_call(
        ignoring(kernel, 1 + len(refs), len(others)),
        out_shape=[jax.ShapeDtypeStruct(shape, dtype) for shape, dtype in shapes],
        in_specs=[SCALARS] + [WHOLE] * len(refs) + [ANYWHERE] * len(others),
        out_specs=[WHOLE] * len(shapes),
        scratch_shapes=[pltpu.VMEM(scratch, BF16)] if scratch else [],
        compiler_params=params(),
        cost_estimate=pl.CostEstimate(flops=flops, bytes_accessed=2_000_000, transcendentals=0),
    )(spot, *refs, *others)


def sum_over_ep(spot, normed, dqkv, grad_out, sums, gains, dn, output, moe_slots, make_hidden):
    own, other = small_call(
        pack_kernel, spot, (normed, dqkv, grad_out, *sums), [((PAY, HALF), BF16)] * 2, flops=0
    )
    got = push(other, 0, 0, 1)
    pieces = small_call(
        reduce_core_kernel, spot, (own, got, *gains), [((QUARTER, HALF), BF16)] * 4, (PAY, HALF)
    )
    dn, halves = scatter_tp(*after(dn, pieces[0]))
    pieces = [push(pieces[d], 0, d, 0) for d in range(RING)]
    quarter = [((QUARTER, HALF), BF16)]
    (line,) = small_call(sum_kernel, spot, pieces, quarter, others=(*halves, moe_slots))
    (line,) = small_call(sum_kernel, spot, [push(line, d, 0, 0) for d in range(RING)], quarter, others=(output,))
    pieces = [push(line, 0, -d, 0) for d in range(RING)]
    hidden = make_hidden(dn)
    (half,) = small_call(gather_x_kernel, spot, pieces, [((PAY, HALF), BF16)], others=(hidden,))
    made = small_call(
        unpack_kernel,
        spot,
        (half, push(half, 0, 0, 1)),
        [
            ((WIDTH, 2 * LANES), F32),
            ((WIDTH, LANES), F32),
            ((WIDTH, LANES), F32),
            ((ROWS, WIDTH), F32),
            ((EXPERTS, WIDTH), F32),
            ((8, WIDTH), F32),
        ],
    )
    return *made, hidden


def hidden_kernel(a, b, c, hidden, gain, dmiddle, out):
    dn = a[...].astype(F32) + b[...].astype(F32) + c[...].astype(F32)
    x = hidden[...].astype(F32)
    inverse = lax.rsqrt(jnp.mean(x * x, axis=-1, keepdims=True) + NORM_EPS)
    plain = x * inverse
    scaled = dn * gain[...]
    along = jnp.mean(scaled * plain, axis=-1, keepdims=True)
    out[...] = dmiddle[...] + inverse * (scaled - plain * along)


def hidden_grad(dn, hidden, gain, dmiddle):
    return pl.pallas_call(
        hidden_kernel,
        out_shape=jax.ShapeDtypeStruct((ROWS, WIDTH), F32),
        in_specs=[WHOLE] * 6,
        out_specs=WHOLE,
        compiler_params=params(),
        cost_estimate=NO_COST,
        name="hidden_grad",
    )(*dn, hidden, gain, dmiddle)


def rope_tables(length):
    freqs = ROPE_BASE ** (-jnp.arange(HD // 2, dtype=F32) * 2.0 / HD)
    angles = jnp.arange(length, dtype=F32)[:, None] * freqs[None, :]
    cosine, sine = jnp.cos(angles), jnp.sin(angles)
    return jnp.concatenate([cosine] * 4, axis=1), jnp.concatenate([-sine, sine] * 2, axis=1)


def shards(
    hidden_in, segment_ids, expert_ids, slot_index, attn_gain, w_query, w_key, w_value, w_output,
    ffn_gain, w_router, w_gate_up, w_down, cotangent,
):
    length = RING * ROWS
    here, rank = lax.axis_index("ep"), lax.axis_index("tp")
    spot = jnp.stack([rank, here // 8, (here // 2) % 4, here % 2]).astype(jnp.int32)

    named = expert_ids[:, :, None] == jnp.arange(EXPERTS, dtype=jnp.int32)[None, None, :]
    slot_of = jnp.sum(jnp.where(named, slot_index[:, :, None] + 1, 0), axis=1) - 1
    chosen = (slot_of >= 0).astype(F32)
    table = slot_of.T.astype(F32)

    gain_one = attn_gain.astype(F32).reshape(1, WIDTH)
    gain_two = ffn_gain.astype(F32).reshape(1, WIDTH)
    cos, sin = rope_tables(length)
    seg_row = segment_ids
    seg_col = segment_ids.reshape(length, 1)

    group = [push_tp(hidden_in, -d) for d in range(RING)]
    cots = lax.all_gather(cotangent, "ep", axis=0, tiled=False, axis_index_groups=SAME_CORE)
    weights = jnp.concatenate([w_gate_up.reshape(WIDTH, 2 * HALF), w_down.reshape(HALF, WIDTH)], axis=0)
    made = attend(spot, group, gain_one, w_query, w_key, w_value, w_output, cos, sin, seg_col, seg_row)
    normed, q, k, v, mixed, lse = made[:6]
    branches = [push_tp(made[6 + d], d) for d in range(RING)]
    (weights,) = after((weights,), lse)
    weights = weights, push(weights, 0, 0, 1)
    middle, half_a, half_b, gates_t = route(hidden_in, branches, gain_two, w_router, chosen, table, weights[1])
    (pieces_a, pieces_b), slots_a, slots_b = dispatch(spot, half_a, half_b)
    first, second = Pieces(pieces_a[:4], pieces_b[:4]), Pieces(pieces_a[4:], pieces_b[4:])
    near = first.send_near()
    far = [first.send(0, 2)]
    held = after((pieces_b[2], pieces_b[6]), near[2], near[3])
    far += [first.send(1, 2, held[0]), second.send(1, 2, held[1])]
    held = after(second.near()[:2], *near)
    second.send(0, 1, held[0]), second.send(0, 3, held[1])
    held = after((*second.near()[2:], pieces_a[6]), *near, *far)
    second.send(1, 1, held[0]), second.send(1, 3, held[1]), second.send(0, 2, held[2])

    back_first, moe_slots, saved = expert(spot, 0, first, cots, weights[0])
    near = back_first.send_near()
    near.append(back_first.send(0, 2))
    back_second, moe_slots, saved_other = expert(spot, 1, second, cots, weights[1], moe_slots)
    held = after((back_first.made[1][2], *back_second.near()), *near)
    back_first.send(1, 2, held[0])
    near = back_second.send_near(held[1:])
    held = after((back_second.made[0][2], back_second.made[1][2], weight_grads(saved_other)), *near)
    back_second.send(0, 2, held[0])
    back_second.send(1, 2, held[1])
    grads_e = weight_grads(saved, push(held[2], 0, 0, 1))
    parts = to_owners(combine(slots_a, slots_b, back_first, back_second))

    dmiddle, dbranch, sums = unroute(
        spot, parts, gates_t, middle, cotangent, gain_two, w_router.T.astype(F32)
    )
    group_grad = gather_tp(dbranch)
    sums = [push_tp(sums, d) for d in range(RING)]

    (moe_slots,) = after((moe_slots,), *parts)
    moe_slots = lax.all_to_all(
        moe_slots, "ep", split_axis=0, concat_axis=0, tiled=True, axis_index_groups=SAME_CORE
    )

    (summed_e,) = after((grads_e,), *group_grad[2])
    summed = lax.psum(summed_e, "tp")
    dmixed, grad_output = unmix(spot, group_grad, mixed, w_output, summed_e)
    last = unattend(
        spot, q, k, v, lse, dmixed, normed, gain_one, w_query, w_key, w_value, cos, sin, seg_col, seg_row
    )
    gains = [push_tp(last[1], d) for d in range(RING)]
    output = finish(spot, table, moe_slots.reshape(CHIPS * PAIR, WIDTH), middle)
    grad_query, grad_key, grad_value, grad_output, grad_router, grad_gains, grad_hidden = sum_over_ep(
        spot, normed, last[0], grad_output, sums, gains, last[2:], output, moe_slots,
        lambda dn: hidden_grad(dn, hidden_in, gain_one, dmiddle),
    )
    grad_up, grad_down = cast_grads(summed)
    return (
        output,
        grad_hidden,
        grad_gains[1],
        grad_query,
        grad_key,
        grad_value,
        grad_output,
        grad_gains[0],
        grad_router.T,
        grad_up.reshape(1, WIDTH, 2, HALF),
        grad_down.reshape(1, HALF, WIDTH),
    )


def solution(mesh):
    placed = (
        P(("ep", "tp"), None),
        P("ep", None),
        P(("ep", "tp"), None),
        P(("ep", "tp"), None),
        P(),
        P(None, "tp"),
        P(None, "tp"),
        P(None, "tp"),
        P("tp", None),
        P(),
        P(),
        P("ep", None, None, None),
        P("ep", None, None),
        P(("ep", "tp"), None),
    )
    return jax.shard_map(
        shards,
        mesh=mesh,
        in_specs=placed,
        out_specs=(
            P(("ep", "tp"), None),
            P(("ep", "tp"), None),
            P(),
            P(None, "tp"),
            P(None, "tp"),
            P(None, "tp"),
            P("tp", None),
            P(),
            P(),
            P("ep", None, None, None),
            P("ep", None, None),
        ),
        check_vma=False,
    )
```
